32 devices in a mesh: dp: 2 (over x), context: 4 (over y, core), tensor: 4 (over z).
Axes of the slice: x: 2, y: 2, z: 4, core: 2. Of those that a mesh axis runs over, the one named last changes fastest.
Arguments:
- patches: bfloat16 [6144, 1280], P(('dp', 'context')), parts along dimension 0, may hold values from -6 to 6
- valid: int32 [6144], P(('dp', 'context')), parts along dimension 0, may hold values from 0 to 1, as said below
- place: int32 [1536], P(('dp', 'context')), parts along dimension 0, may hold values from -1 to 767, as said below
- gain_attn: float32 [1280], replicated, may hold values from 0.25 to 1.75
- w_qkv: bfloat16 [1280, 3, 1280], P('context', None, 'tensor'), may hold values from -1 to 1
- w_proj: bfloat16 [1280, 1280], P('tensor', 'context'), may hold values from -0.15625 to 0.15625
- gain_merge: float32 [1280], replicated, may hold values from 0.25 to 1.75
Outputs:
- placed: bfloat16 [1536, 5120], P(('dp', 'context'), 'tensor'), parts along dimension 0
The draws below stay inside these ranges and needn't reach their ends.
There are 2 independent parts, one for each index of `dp`. The reference program is written for one: setup_inputs(seed, part) draws one part's arguments, and reference() takes and returns one part's arrays. A program takes and returns all parts, laid end to end along the dimension named above; an argument that names none is the same for every part. Nothing has to cross between parts.
Inputs may be any that keep to these rules, and one draw needn't show every extreme that they name: `valid`: slots of a window are ordered by 2 x 2 groups of 4 (group row-major over a 4 x 4 grid, then within the group row-major); the real patches of a window form its top-left h x w block with h and w even and at least 4. `place`: A merged row has a position exactly when its 4 slots are real; positions are distinct.
All inputs are finite; a program needn't handle non-finite values.
Results may differ from the reference program's by a relative error of at most 0.0073.
Values may be sent and summed in bfloat16 or wider, within the bound.
No kernel may reach another device: no remote copies, remote signals or barrier semaphores. Data moves between devices by JAX's collectives and lax.ppermute only.
A program may use at most 64 MiB of HBM per device.

```python
import math
import jax
import jax.numpy as jnp
from jax import lax

D = 1280
HEADS = 16
HD = 80
WIN = 64
WINS = 12
PATCHES = 3072
MERGED = 768
POSITIONS = 768
N_CONTEXT = 4


def layout(key):
    window_count = N_CONTEXT * WINS
    height_cells = 2 * jax.random.randint(jax.random.fold_in(key, 11), (window_count,), 2, 5)
    width_cells = 2 * jax.random.randint(jax.random.fold_in(key, 12), (window_count,), 2, 5)
    inner_index = jnp.arange(WIN)
    group_index = inner_index // 4
    within_group = inner_index % 4
    row_spot = 2 * (group_index // 4) + within_group // 2
    col_spot = 2 * (group_index % 4) + within_group % 2
    inside = (row_spot[None, :] < height_cells[:, None]) & (col_spot[None, :] < width_cells[:, None])
    valid = inside.astype(jnp.int32).reshape(-1)
    group_live = valid.reshape(-1, 4)[:, 0]
    shuffled = jax.random.permutation(jax.random.fold_in(key, 13), POSITIONS).astype(jnp.int32)
    spot_order = jnp.argsort(shuffled, stable=True).astype(jnp.int32)
    group_rank = jnp.maximum(jnp.cumsum(group_live) - 1, 0).astype(jnp.int32)
    place = jnp.where(group_live > 0, spot_order[group_rank], -1).astype(jnp.int32)
    return (valid, place)


def draw_valid(key, part):
    shared = layout(key)
    return shared[0]


def draw_place(key, part):
    shared = layout(key)
    return shared[1]


def draw_patches(key, part):
    key = jax.random.fold_in(key, 21)
    noise = jax.random.normal(jax.random.fold_in(key, 1), (PATCHES, D), jnp.float32)
    values = noise
    return jnp.clip(values, -6.0, 6.0).astype(jnp.bfloat16)


def draw_w_qkv(key, part):
    key = jax.random.fold_in(key, 22)
    noise = jax.random.normal(jax.random.fold_in(key, 1), (D, 3, D), jnp.float32)
    base = noise / math.sqrt(D)
    return jnp.clip(base, -1.0, 1.0).astype(jnp.bfloat16)


def block_scale(own_key, shape, split, smallest, largest):
    factor_of, own = 1.0, jax.random.fold_in(own_key, 6)
    for position, shards_of in split:
        heights = jnp.exp(jax.random.uniform(jax.random.fold_in(own, position), (shards_of,), jnp.float32, smallest / len(split), largest / len(split)))
        factor_of = factor_of * jnp.repeat(heights, shape[position] // shards_of).reshape([-1 if axis == position else 1 for axis in range(len(shape))])
    return factor_of


def gaussian(stream_key, dims, deviation, bound, pieces=(), held_as=jnp.bfloat16):
    drawn = jax.random.normal(stream_key, dims, jnp.float32) * deviation
    if len(pieces) > 0:
        drawn = block_scale(stream_key, dims, pieces, -0.22, 0.18) * drawn
    return jnp.clip(drawn, min=-bound, max=bound).astype(held_as)


def setup_inputs(seed: int = 0, part: int = 0) -> dict:
    key_list = jax.random.split(jax.random.key(seed), 8)
    own_keys = jax.random.split(jax.random.fold_in(key_list[7], part), 8)
    return {
        "patches": draw_patches(jax.random.fold_in(jax.random.fold_in(key_list[7], part), 71), part),
        "valid": draw_valid(jax.random.fold_in(jax.random.fold_in(key_list[7], part), 71), part),
        "place": draw_place(jax.random.fold_in(jax.random.fold_in(key_list[7], part), 71), part),
        "gain_attn": jnp.clip(1.0 + 0.15 * jax.random.normal(key_list[3], (D,), jnp.float32), 0.25, 1.75),
        "w_qkv": draw_w_qkv(jax.random.fold_in(key_list[7], 71), part),
        "w_proj": gaussian(key_list[5], (D, D), D ** -0.5, 0.15625, ((0, 4), (1, 4))),
        "gain_merge": jnp.clip(1.0 + 0.15 * jax.random.normal(key_list[6], (D,), jnp.float32), 0.25, 1.75),
    }


def normalize(tensor_in, gain):
    mean_sq = lax.optimization_barrier(jnp.mean(tensor_in * tensor_in, axis=-1, keepdims=True))
    return tensor_in * lax.rsqrt(mean_sq + 1e-06) * gain.astype(jnp.float32)

def reference(patches, valid, place, gain_attn, w_qkv, w_proj, gain_merge):
    windows = PATCHES // WIN
    hidden = normalize(patches.astype(jnp.float32), gain_attn).astype(jnp.bfloat16)
    projected = jnp.dot(hidden, w_qkv.reshape(D, 3 * D), preferred_element_type=jnp.float32)
    triple = projected.reshape(PATCHES, 3, HEADS, HD).astype(jnp.bfloat16)
    query_all = triple[:, 0].reshape(windows, WIN, HEADS, HD).astype(jnp.float32)
    key_all = triple[:, 1].reshape(windows, WIN, HEADS, HD).astype(jnp.float32)
    value_all = triple[:, 2].reshape(windows, WIN, HEADS, HD).astype(jnp.float32)
    scores = jnp.einsum('wqhd,wkhd->whqk', query_all, key_all) * HD ** (-0.5)
    key_mask = valid.reshape(windows, 1, 1, WIN) > 0
    scores = jnp.where(key_mask, scores, jnp.float32(-1e+30))
    peak = lax.optimization_barrier(jnp.max(scores, axis=-1, keepdims=True))
    exp_terms = jnp.exp(scores - peak)
    weights = (exp_terms / lax.optimization_barrier(jnp.sum(exp_terms, axis=-1, keepdims=True))).astype(jnp.bfloat16)
    mixed_heads = jnp.einsum('whqk,wkhd->wqhd', weights.astype(jnp.float32), value_all)
    mixed_heads = mixed_heads.reshape(PATCHES, D).astype(jnp.bfloat16)
    head_total = jnp.dot(mixed_heads, w_proj, preferred_element_type=jnp.float32)
    residual = patches.astype(jnp.float32) + head_total
    normed = normalize(residual, gain_merge).astype(jnp.bfloat16)
    merged = normed.reshape(MERGED, 4 * D)
    target = jnp.where(place >= 0, place, POSITIONS).astype(jnp.int32)
    canvas = jnp.zeros((POSITIONS + 1, 4 * D), jnp.bfloat16).at[target].set(merged)
    return canvas[:POSITIONS]
```

```python
import functools

import jax
import jax.numpy as jnp
from jax import lax
from jax.experimental import pallas as pl
from jax.experimental.pallas import tpu as pltpu
from jax.sharding import PartitionSpec as P

HD = 80
WIN = 64
PAIR = 2 * WIN
CHUNKS = 1
F32 = jnp.float32
BF16 = jnp.bfloat16
VMEM = pl.BlockSpec(memory_space=pltpu.VMEM)
SMEM = pl.BlockSpec(memory_space=pltpu.SMEM)


def params(mib):
    return pltpu.CompilerParams(vmem_limit_bytes=mib * 1024 * 1024)


def swap(x, axis, size, bit):
    return lax.ppermute(x, axis, [(i, i ^ bit) for i in range(size)])


def gather_xor(x, axis, size):
    blocks = {0: x}
    bit = size // 2
    while bit:
        for key in list(blocks):
            blocks[key ^ bit] = swap(blocks[key], axis, size, bit)
        bit //= 2
    return blocks


def norm_kernel(slot_ref, patches_ref, gain_ref, hidden_ref, own_ref):
    rows = patches_ref.shape[0]
    x = patches_ref[...]
    xf = x.astype(F32)
    mean_sq = jnp.mean(xf * xf, axis=-1, keepdims=True)
    hidden_ref[...] = (xf * lax.rsqrt(mean_sq + 1e-06) * gain_ref[...]).astype(BF16)
    step = 256
    pick = step // 4
    row = lax.broadcasted_iota(jnp.int32, (pick, step), 0)
    col = lax.broadcasted_iota(jnp.int32, (pick, step), 1)
    chosen = (col == 4 * row + slot_ref[0]).astype(F32).astype(BF16)
    for i in range(rows // step):
        own_ref[i * pick : (i + 1) * pick, :] = jnp.dot(
            chosen, x[i * step : (i + 1) * step], preferred_element_type=F32
        ).astype(BF16)


def attention_kernel(n_ctx, row0, rows, *refs):
    ctx_ref, hidden_ref, valid_ref = refs[:3]
    shards = refs[3 : 3 + n_ctx]
    out_ref, w_ref, q_ref, k_ref, v_ref, mix_ref = refs[3 + n_ctx :]
    depth = shards[0].shape[1]
    width = shards[0].shape[2]
    heads = width // HD
    me = ctx_ref[0]
    for key in range(n_ctx):
        at = pl.multiple_of((me ^ key) * depth, depth)
        for j in range(3):
            w_ref[j, pl.ds(at, depth), :] = shards[key][j]
    hidden = hidden_ref[row0 : row0 + rows, :]
    q_ref[...] = jnp.dot(hidden, w_ref[0], preferred_element_type=F32).astype(BF16)
    k_ref[...] = jnp.dot(hidden, w_ref[1], preferred_element_type=F32).astype(BF16)
    v_ref[...] = jnp.dot(hidden, w_ref[2], preferred_element_type=F32).astype(BF16)
    lane = lax.broadcasted_iota(jnp.int32, (1, width), 1)
    head_masks = [
        ((lane >= h * HD) & (lane < (h + 1) * HD)).astype(F32).astype(BF16) for h in range(heads)
    ]
    q_win = lax.broadcasted_iota(jnp.int32, (PAIR, PAIR), 0) // WIN
    k_win = lax.broadcasted_iota(jnp.int32, (PAIR, PAIR), 1) // WIN
    same = q_win == k_win
    for p in range(rows // PAIR):
        at = p * PAIR
        q = q_ref[at : at + PAIR, :]
        k = k_ref[at : at + PAIR, :]
        v = v_ref[at : at + PAIR, :]
        k_all = jnp.concatenate([k * m for m in head_masks], axis=0)
        v_all = jnp.concatenate([v * m for m in head_masks], axis=0)
        scores = lax.dot_general(q, k_all, (((1,), (1,)), ((), ())), preferred_element_type=F32)
        live = valid_ref[row0 // PAIR + p : row0 // PAIR + p + 1, :] > 0
        floor = jnp.where(same, F32(-1e30), F32(-3e38))
        weights = []
        for h in range(heads):
            s = scores[:, h * PAIR : (h + 1) * PAIR] * F32(HD ** (-0.5))
            s = jnp.where(same & live, s, floor)
            e = jnp.exp(s - jnp.max(s, axis=-1, keepdims=True))
            weights.append((e / jnp.sum(e, axis=-1, keepdims=True)).astype(BF16))
        w_all = jnp.concatenate(weights, axis=1)
        mix_ref[at : at + PAIR, :] = jnp.dot(w_all, v_all, preferred_element_type=F32).astype(BF16)
    step = 128
    pick = step // 4
    src = lax.broadcasted_iota(jnp.int32, (step, step), 1)
    dst = lax.broadcasted_iota(jnp.int32, (step, step), 0)
    order = (src == 4 * (dst % pick) + dst // pick).astype(F32).astype(BF16)
    for i in range(rows // step):
        sorted_rows = jnp.dot(
            order, mix_ref[i * step : (i + 1) * step, :], preferred_element_type=F32
        ).astype(BF16)
        for t in range(4):
            out_ref[t, i * pick : (i + 1) * pick, :] = sorted_rows[t * pick : (t + 1) * pick]


def project_kernel(row0, mix0, mix1, mix2, mix3, w_ref, own_ref, gain_ref, out_ref):
    width = mix0.shape[1]
    rows = mix0.shape[0]
    total = own_ref[row0 : row0 + rows, :].astype(F32)
    for s, mix in enumerate((mix0, mix1, mix2, mix3)):
        total = total + jnp.dot(
            mix[...], w_ref[s * width : (s + 1) * width, :], preferred_element_type=F32
        )
    mean_sq = jnp.mean(total * total, axis=-1, keepdims=True)
    out_ref[...] = (total * lax.rsqrt(mean_sq + 1e-06) * gain_ref[...]).astype(BF16)


def place_kernel(n_ctx, ctx_ref, *refs):
    place_refs = refs[:n_ctx]
    row_refs = refs[n_ctx:-1]
    out_ref = refs[-1]
    spots = out_ref.shape[0]
    chunks = len(row_refs) // n_ctx
    total = None
    for key in range(n_ctx):
        target = place_refs[key][...] - ctx_ref[0] * spots
        grid = lax.broadcasted_iota(jnp.int32, (spots, target.shape[1]), 0)
        chosen = (grid == target).astype(F32).astype(BF16)
        for r in range(chunks):
            block = row_refs[key * chunks + r]
            count = block.shape[0]
            part = jnp.dot(
                chosen[:, r * count : (r + 1) * count], block[...], preferred_element_type=F32
            )
            total = part if total is None else total + part
    out_ref[...] = total.astype(BF16)


def local(n_ctx, n_ten, patches, valid, place, gain_attn, w_qkv, w_proj, gain_merge):
    rows, feat = patches.shape
    width = w_qkv.shape[2]
    depth = w_qkv.shape[0]
    groups = rows // 4
    ctx = lax.axis_index("context").astype(jnp.int32).reshape(1)
    ten = lax.axis_index("tensor").astype(jnp.int32).reshape(1)

    w_blocks = gather_xor(jnp.transpose(w_qkv, (1, 0, 2)), "context", n_ctx)
    proj = jnp.stack([w_proj] + [swap(w_proj, "tensor", n_ten, s) for s in range(1, n_ten)])
    places = gather_xor(place.reshape(1, groups), "context", n_ctx)

    hidden, own_patches = pl.pallas_call(
        norm_kernel,
        out_shape=(
            jax.ShapeDtypeStruct((rows, feat), BF16),
            jax.ShapeDtypeStruct((groups, feat), BF16),
        ),
        in_specs=[SMEM, VMEM, VMEM],
        out_specs=(VMEM, VMEM),
        compiler_params=params(32),
        name="norm",
    )(ten, patches, gain_attn.reshape(1, feat))

    proj_blocks = gather_xor(proj, "context", n_ctx)
    col = proj.shape[2]
    by_key = jnp.stack([proj_blocks[k] for k in range(n_ctx)])
    order = ctx[0] ^ jnp.arange(n_ctx, dtype=jnp.int32)
    w_full = jnp.transpose(by_key[order], (1, 2, 0, 3)).reshape(n_ten * width, n_ctx * col)

    valid_pairs = valid.reshape(rows // PAIR, PAIR)
    part = rows // CHUNKS
    gain2 = gain_merge.reshape(1, feat)
    finished = []
    for r in range(CHUNKS):
        mixed = pl.pallas_call(
            functools.partial(attention_kernel, n_ctx, r * part, part),
            out_shape=jax.ShapeDtypeStruct((n_ten, part // 4, width), BF16),
            in_specs=[SMEM, VMEM, VMEM] + [VMEM] * n_ctx,
            out_specs=VMEM,
            scratch_shapes=[
                pltpu.VMEM((3, feat, width), BF16),
                pltpu.VMEM((part, width), BF16),
                pltpu.VMEM((part, width), BF16),
                pltpu.VMEM((part, width), BF16),
                pltpu.VMEM((part, width), BF16),
            ],
            compiler_params=params(32),
            name="attention",
        )(ctx, hidden, valid_pairs, *[w_blocks[k] for k in range(n_ctx)])
        pieces = []
        for s in range(n_ten):
            piece = lax.dynamic_index_in_dim(mixed, ten[0] ^ s, 0, keepdims=False)
            pieces.append(piece if s == 0 else swap(piece, "tensor", n_ten, s))
        finished.append(
            pl.pallas_call(
                functools.partial(project_kernel, r * (part // 4)),
                out_shape=jax.ShapeDtypeStruct((part // 4, feat), BF16),
                in_specs=[VMEM] * 7,
                out_specs=VMEM,
                compiler_params=params(32),
                name="project",
            )(*pieces, w_full, own_patches, gain2)
        )
    gathered = [gather_xor(block, "context", n_ctx) for block in finished]
    return pl.pallas_call(
        functools.partial(place_kernel, n_ctx),
        out_shape=jax.ShapeDtypeStruct((groups, feat), BF16),
        in_specs=[SMEM] + [VMEM] * (n_ctx + n_ctx * CHUNKS),
        out_specs=VMEM,
        compiler_params=params(32),
        name="placement",
    )(
        ctx,
        *[places[k] for k in range(n_ctx)],
        *[gathered[r][k] for k in range(n_ctx) for r in range(CHUNKS)],
    )


def solution(mesh):
    in_specs = (
        P(("dp", "context"), None),
        P(("dp", "context")),
        P(("dp", "context")),
        P(),
        P("context", None, "tensor"),
        P("tensor", "context"),
        P(),
    )
    out_specs = P(("dp", "context"), "tensor")
    body = functools.partial(local, mesh.shape["context"], mesh.shape["tensor"])
    return jax.shard_map(body, mesh=mesh, in_specs=in_specs, out_specs=out_specs, check_vma=False)
```

```python
import functools

import jax
import jax.numpy as jnp
from jax import lax
from jax.experimental import pallas as pl
from jax.experimental.pallas import tpu as pltpu
from jax.sharding import PartitionSpec as P

HD = 80
WIN = 64
PAIR = 2 * WIN
CHUNKS = 2
F32 = jnp.float32
BF16 = jnp.bfloat16
VMEM = pl.BlockSpec(memory_space=pltpu.VMEM)
SMEM = pl.BlockSpec(memory_space=pltpu.SMEM)


def params(mib):
    return pltpu.CompilerParams(vmem_limit_bytes=mib * 1024 * 1024)


def swap(x, axis, size, bit):
    return lax.ppermute(x, axis, [(i, i ^ bit) for i in range(size)])


def cross_keys(size):
    return range(2, size, 2)


def gather_cross(x, size):
    blocks = {0: x}
    bit = size // 2
    while bit > 1:
        for key in list(blocks):
            blocks[key ^ bit] = swap(blocks[key], "context", size, bit)
        bit //= 2
    return blocks


def gather_xor(x, size):
    blocks = gather_cross(x, size)
    for key in list(blocks):
        blocks[key ^ 1] = swap(blocks[key], "context", size, 1)
    return blocks


def one_hot(mask):
    return mask.astype(F32).astype(BF16)


def norm_kernel(n_ctx, index_ref, *refs):
    place_refs = refs[:n_ctx]
    patches_ref, gain_ref, hidden_ref, own_ref, chosen_ref = refs[n_ctx:]
    rows = patches_ref.shape[0]
    x = patches_ref[...]
    xf = x.astype(F32)
    mean_sq = jnp.mean(xf * xf, axis=-1, keepdims=True)
    hidden_ref[...] = (xf * lax.rsqrt(mean_sq + 1e-06) * gain_ref[...]).astype(BF16)
    step = 256
    pick = step // 4
    row = lax.broadcasted_iota(jnp.int32, (pick, step), 0)
    col = lax.broadcasted_iota(jnp.int32, (pick, step), 1)
    chosen = one_hot(col == 4 * row + index_ref[1])
    for i in range(rows // step):
        own_ref[i * pick : (i + 1) * pick, :] = jnp.dot(
            chosen, x[i * step : (i + 1) * step], preferred_element_type=F32
        ).astype(BF16)
    spots = chosen_ref.shape[1]
    for key in range(n_ctx):
        target = place_refs[key][...] - index_ref[0] * spots
        grid = lax.broadcasted_iota(jnp.int32, (spots, target.shape[1]), 0)
        chosen_ref[key] = one_hot(grid == target)


def attend(row0, hidden_ref, valid_ref, w_ref, out_ref, q_ref, k_ref, v_ref, mix_ref):
    rows = q_ref.shape[0]
    width = q_ref.shape[1]
    heads = width // HD
    hidden = hidden_ref[row0 : row0 + rows, :]
    for j, ref in enumerate((q_ref, k_ref, v_ref)):
        ref[...] = jnp.dot(hidden, w_ref[j], preferred_element_type=F32).astype(BF16)
    lane = lax.broadcasted_iota(jnp.int32, (1, width), 1)
    head_masks = [one_hot((lane >= h * HD) & (lane < (h + 1) * HD)) for h in range(heads)]
    q_win = lax.broadcasted_iota(jnp.int32, (PAIR, PAIR), 0) // WIN
    k_win = lax.broadcasted_iota(jnp.int32, (PAIR, PAIR), 1) // WIN
    same = q_win == k_win
    floor = jnp.where(same, F32(-1e30), F32(-3e38))
    for p in range(rows // PAIR):
        at = p * PAIR
        q = q_ref[at : at + PAIR, :]
        k = k_ref[at : at + PAIR, :]
        v = v_ref[at : at + PAIR, :]
        k_all = jnp.concatenate([k * m for m in head_masks], axis=0)
        v_all = jnp.concatenate([v * m for m in head_masks], axis=0)
        scores = lax.dot_general(q, k_all, (((1,), (1,)), ((), ())), preferred_element_type=F32)
        live = valid_ref[row0 // PAIR + p : row0 // PAIR + p + 1, :] > 0
        weights = []
        for h in range(heads):
            s = scores[:, h * PAIR : (h + 1) * PAIR] * F32(HD ** (-0.5))
            s = jnp.where(same & live, s, floor)
            e = jnp.exp(s - jnp.max(s, axis=-1, keepdims=True))
            weights.append((e / jnp.sum(e, axis=-1, keepdims=True)).astype(BF16))
        w_all = jnp.concatenate(weights, axis=1)
        mix_ref[at : at + PAIR, :] = jnp.dot(w_all, v_all, preferred_element_type=F32).astype(BF16)
    pick = PAIR // 4
    src = lax.broadcasted_iota(jnp.int32, (PAIR, PAIR), 1)
    dst = lax.broadcasted_iota(jnp.int32, (PAIR, PAIR), 0)
    order = one_hot(src == 4 * (dst % pick) + dst // pick)
    for i in range(rows // PAIR):
        sorted_rows = jnp.dot(
            order, mix_ref[i * PAIR : (i + 1) * PAIR, :], preferred_element_type=F32
        ).astype(BF16)
        for t in range(4):
            out_ref[t, i * pick : (i + 1) * pick, :] = sorted_rows[t * pick : (t + 1) * pick]


def first_attention_kernel(n_ctx, index_ref, hidden_ref, valid_ref, *refs):
    shards = list(refs[: 2 + 3 * (n_ctx - 2)])
    out_ref, w_ref, *scratch = refs[len(shards) :]
    depth = shards[0].shape[1]
    me = index_ref[0]
    part = index_ref[2]
    for key in range(n_ctx):
        at = pl.multiple_of((me ^ key) * depth, depth)
        if key < 2:
            block = shards.pop(0)
            for j in range(3):
                w_ref[j, pl.ds(at, depth), :] = block[j]
        else:
            for j in (part, 1 - part, 2):
                w_ref[j, pl.ds(at, depth), :] = shards.pop(0)[...]
    attend(0, hidden_ref, valid_ref, w_ref, out_ref, *scratch)


def next_attention_kernel(row0, hidden_ref, valid_ref, w_ref, out_ref, *scratch):
    attend(row0, hidden_ref, valid_ref, w_ref, out_ref, *scratch)


def project_kernel(n_ctx, row0, index_ref, *refs):
    mixes = [m[...] for m in refs[:4]]
    blocks = list(refs[4 : 4 + 2 + 2 * (n_ctx - 2)])
    own_ref, gain_ref, out_ref, part_ref = refs[4 + len(blocks) :]
    rows = out_ref.shape[0]
    me = index_ref[0]
    flip = index_ref[2] > 0
    low = jnp.concatenate(mixes[:2], axis=1)
    high = jnp.concatenate(mixes[2:], axis=1)
    first = jnp.where(flip, high, low)
    second = jnp.where(flip, low, high)
    col = blocks[0].shape[2]

    def times(mix, ref, at):
        w = ref[at : at + 2].reshape(mix.shape[1], col)
        return jnp.dot(mix, w, preferred_element_type=F32)

    for key in range(n_ctx):
        if key < 2:
            block = blocks.pop(0)
            part_ref[me ^ key] = times(low, block, 0) + times(high, block, 2)
        else:
            part_ref[me ^ key] = times(first, blocks.pop(0), 0) + times(second, blocks.pop(0), 0)
    total = jnp.concatenate([part_ref[i] for i in range(n_ctx)], axis=1)
    total = total + own_ref[row0 : row0 + rows, :].astype(F32)
    mean_sq = jnp.mean(total * total, axis=-1, keepdims=True)
    out_ref[...] = (total * lax.rsqrt(mean_sq + 1e-06) * gain_ref[...]).astype(BF16)


def place_kernel(n_ctx, chosen_ref, *refs):
    row_refs = refs[:-1]
    out_ref = refs[-1]
    chunks = len(row_refs) // n_ctx
    total = None
    for key in range(n_ctx):
        for r in range(chunks):
            block = row_refs[key * chunks + r]
            count = block.shape[0]
            part = jnp.dot(
                chosen_ref[key, :, r * count : (r + 1) * count],
                block[...],
                preferred_element_type=F32,
            )
            total = part if total is None else total + part
    out_ref[...] = total.astype(BF16)


def local(n_dp, n_ctx, n_ten, patches, valid, place, gain_attn, w_qkv, w_proj, gain_merge):
    rows, feat = patches.shape
    width = w_qkv.shape[2]
    groups = rows // 4
    ten = lax.axis_index("tensor")
    half = lax.axis_index("dp") % 2
    index = jnp.stack([lax.axis_index("context"), ten, half]).astype(jnp.int32)

    w3 = jnp.transpose(w_qkv, (1, 0, 2))
    near = gather_cross(lax.dynamic_index_in_dim(w3, half, 0, keepdims=False), n_ctx)
    last = gather_cross(w3[2], n_ctx)
    shards = {0: [w3], 1: [swap(w3, "context", n_ctx, 1)]}
    for key in cross_keys(n_ctx):
        shards[key] = [near[key], swap(near[key], "dp", n_dp, 1), last[key]]
        shards[key ^ 1] = [swap(x, "context", n_ctx, 1) for x in shards[key]]

    pieces = [w_proj] + [swap(w_proj, "tensor", n_ten, s) for s in range(1, n_ten)]
    proj = jnp.stack(pieces)
    mine = gather_cross(lax.dynamic_slice_in_dim(proj, half * 2, 2, 0), n_ctx)
    blocks = {0: [proj], 1: [swap(proj, "context", n_ctx, 1)]}
    for key in cross_keys(n_ctx):
        blocks[key] = [mine[key], swap(mine[key], "dp", n_dp, 1)]
        blocks[key ^ 1] = [swap(x, "context", n_ctx, 1) for x in blocks[key]]

    places = gather_xor(place.reshape(1, groups), n_ctx)
    hidden, own_patches, chosen = pl.pallas_call(
        functools.partial(norm_kernel, n_ctx),
        out_shape=(
            jax.ShapeDtypeStruct((rows, feat), BF16),
            jax.ShapeDtypeStruct((groups, feat), BF16),
            jax.ShapeDtypeStruct((n_ctx, groups, groups), BF16),
        ),
        in_specs=[SMEM] + [VMEM] * (n_ctx + 2),
        out_specs=(VMEM, VMEM, VMEM),
        compiler_params=params(32),
        name="norm",
    )(index, *[places[k] for k in range(n_ctx)], patches, gain_attn.reshape(1, feat))

    valid_pairs = valid.reshape(rows // PAIR, PAIR)
    part = rows // CHUNKS
    gain2 = gain_merge.reshape(1, feat)
    mix_shape = jax.ShapeDtypeStruct((n_ten, part // 4, width), BF16)
    scratch = [pltpu.VMEM((part, width), BF16)] * 4
    shard_list = [x for k in range(n_ctx) for x in shards[k]]
    block_list = [x for k in range(n_ctx) for x in blocks[k]]
    w_full = None
    gathered = []
    for r in range(CHUNKS):
        if r == 0:
            mixed, w_full = pl.pallas_call(
                functools.partial(first_attention_kernel, n_ctx),
                out_shape=(mix_shape, jax.ShapeDtypeStruct((3, feat, width), BF16)),
                in_specs=[SMEM] + [VMEM] * (2 + len(shard_list)),
                out_specs=(VMEM, VMEM),
                scratch_shapes=scratch,
                compiler_params=params(32),
                name="attention0",
            )(index, hidden, valid_pairs, *shard_list)
        else:
            mixed = pl.pallas_call(
                functools.partial(next_attention_kernel, r * part),
                out_shape=mix_shape,
                in_specs=[VMEM] * 3,
                out_specs=VMEM,
                scratch_shapes=scratch,
                compiler_params=params(32),
                name="attention" + str(r),
            )(hidden, valid_pairs, w_full)
        mixes = []
        for s in range(n_ten):
            piece = lax.dynamic_index_in_dim(mixed, ten ^ s, 0, keepdims=False)
            mixes.append(piece if s == 0 else swap(piece, "tensor", n_ten, s))
        done = pl.pallas_call(
            functools.partial(project_kernel, n_ctx, r * (part // 4)),
            out_shape=jax.ShapeDtypeStruct((part // 4, feat), BF16),
            in_specs=[SMEM] + [VMEM] * (n_ten + len(block_list) + 2),
            out_specs=VMEM,
            scratch_shapes=[pltpu.VMEM((n_ctx, part // 4, w_proj.shape[1]), F32)],
            compiler_params=params(32),
            name="project" + str(r),
        )(index, *mixes, *block_list, own_patches, gain2)
        gathered.append(gather_xor(done, n_ctx))
    return pl.pallas_call(
        functools.partial(place_kernel, n_ctx),
        out_shape=jax.ShapeDtypeStruct((groups, feat), BF16),
        in_specs=[VMEM] * (1 + n_ctx * CHUNKS),
        out_specs=VMEM,
        compiler_params=params(32),
        name="placement",
    )(chosen, *[gathered[r][k] for k in range(n_ctx) for r in range(CHUNKS)])


def solution(mesh):
    in_specs = (
        P(("dp", "context"), None),
        P(("dp", "context")),
        P(("dp", "context")),
        P(),
        P("context", None, "tensor"),
        P("tensor", "context"),
        P(),
    )
    out_specs = P(("dp", "context"), "tensor")
    sizes = [mesh.shape[name] for name in ("dp", "context", "tensor")]
    body = functools.partial(local, *sizes)
    return jax.shard_map(body, mesh=mesh, in_specs=in_specs, out_specs=out_specs, check_vma=False)
```

```python
import functools

import jax
import jax.numpy as jnp
from jax import lax
from jax.experimental import pallas as pl
from jax.experimental.pallas import tpu as pltpu
from jax.sharding import PartitionSpec as P

HD = 80
WIN = 64
PAIR = 2 * WIN
CHUNKS = 2
F32 = jnp.float32
BF16 = jnp.bfloat16
VMEM = pl.BlockSpec(memory_space=pltpu.VMEM)
SMEM = pl.BlockSpec(memory_space=pltpu.SMEM)


def params(mib):
    return pltpu.CompilerParams(vmem_limit_bytes=mib * 1024 * 1024)


def swap(x, axis, size, bit):
    return lax.ppermute(x, axis, [(i, i ^ bit) for i in range(size)])


def cross_keys(size):
    return range(2, size, 2)


def gather_cross(x, size):
    blocks = {0: x}
    bit = size // 2
    while bit > 1:
        for key in list(blocks):
            blocks[key ^ bit] = swap(blocks[key], "context", size, bit)
        bit //= 2
    return blocks


def gather_xor(x, size):
    blocks = gather_cross(x, size)
    for key in list(blocks):
        blocks[key ^ 1] = swap(blocks[key], "context", size, 1)
    return blocks


def one_hot(mask):
    return mask.astype(F32).astype(BF16)


def norm_kernel(index_ref, patches_ref, gain_ref, hidden_ref, own_ref):
    rows = patches_ref.shape[0]
    x = patches_ref[...]
    xf = x.astype(F32)
    mean_sq = jnp.mean(xf * xf, axis=-1, keepdims=True)
    hidden_ref[...] = (xf * lax.rsqrt(mean_sq + 1e-06) * gain_ref[...]).astype(BF16)
    step = 256
    pick = step // 4
    row = lax.broadcasted_iota(jnp.int32, (pick, step), 0)
    col = lax.broadcasted_iota(jnp.int32, (pick, step), 1)
    chosen = one_hot(col == 4 * row + index_ref[1])
    for i in range(rows // step):
        own_ref[i * pick : (i + 1) * pick, :] = jnp.dot(
            chosen, x[i * step : (i + 1) * step], preferred_element_type=F32
        ).astype(BF16)


def attend(row0, hidden_ref, valid_ref, w_ref, out_ref, q_ref, k_ref, v_ref, mix_ref):
    rows = q_ref.shape[0]
    width = q_ref.shape[1]
    heads = width // HD
    hidden = hidden_ref[row0 : row0 + rows, :]
    for j, ref in enumerate((q_ref, k_ref, v_ref)):
        ref[...] = jnp.dot(hidden, w_ref[j], preferred_element_type=F32).astype(BF16)
    lane = lax.broadcasted_iota(jnp.int32, (1, width), 1)
    head_masks = [one_hot((lane >= h * HD) & (lane < (h + 1) * HD)) for h in range(heads)]
    q_win = lax.broadcasted_iota(jnp.int32, (PAIR, PAIR), 0) // WIN
    k_win = lax.broadcasted_iota(jnp.int32, (PAIR, PAIR), 1) // WIN
    same = q_win == k_win
    floor = jnp.where(same, F32(-1e30), F32(-3e38))
    for p in range(rows // PAIR):
        at = p * PAIR
        q = q_ref[at : at + PAIR, :]
        k = k_ref[at : at + PAIR, :]
        v = v_ref[at : at + PAIR, :]
        k_all = jnp.concatenate([k * m for m in head_masks], axis=0)
        v_all = jnp.concatenate([v * m for m in head_masks], axis=0)
        scores = lax.dot_general(q, k_all, (((1,), (1,)), ((), ())), preferred_element_type=F32)
        live = valid_ref[row0 // PAIR + p : row0 // PAIR + p + 1, :] > 0
        weights = []
        for h in range(heads):
            s = scores[:, h * PAIR : (h + 1) * PAIR] * F32(HD ** (-0.5))
            s = jnp.where(same & live, s, floor)
            e = jnp.exp(s - jnp.max(s, axis=-1, keepdims=True))
            weights.append((e / jnp.sum(e, axis=-1, keepdims=True)).astype(BF16))
        w_all = jnp.concatenate(weights, axis=1)
        mix_ref[at : at + PAIR, :] = jnp.dot(w_all, v_all, preferred_element_type=F32).astype(BF16)
    pick = PAIR // 4
    src = lax.broadcasted_iota(jnp.int32, (PAIR, PAIR), 1)
    dst = lax.broadcasted_iota(jnp.int32, (PAIR, PAIR), 0)
    order = one_hot(src == 4 * (dst % pick) + dst // pick)
    for i in range(rows // PAIR):
        sorted_rows = jnp.dot(
            order, mix_ref[i * PAIR : (i + 1) * PAIR, :], preferred_element_type=F32
        ).astype(BF16)
        for t in range(4):
            out_ref[t, i * pick : (i + 1) * pick, :] = sorted_rows[t * pick : (t + 1) * pick]


def first_attention_kernel(n_ctx, index_ref, hidden_ref, valid_ref, *refs):
    shards = list(refs[: 2 + 3 * (n_ctx - 2)])
    out_ref, w_ref, *scratch = refs[len(shards) :]
    depth = shards[0].shape[1]
    me = index_ref[0]
    part = index_ref[2]
    for key in range(n_ctx):
        at = pl.multiple_of((me ^ key) * depth, depth)
        if key < 2:
            block = shards.pop(0)
            for j in range(3):
                w_ref[j, pl.ds(at, depth), :] = block[j]
        else:
            for j in (part, 1 - part, 2):
                w_ref[j, pl.ds(at, depth), :] = shards.pop(0)[...]
    attend(0, hidden_ref, valid_ref, w_ref, out_ref, *scratch)


def next_attention_kernel(row0, hidden_ref, valid_ref, w_ref, out_ref, *scratch):
    attend(row0, hidden_ref, valid_ref, w_ref, out_ref, *scratch)


def project_kernel(n_ctx, row0, index_ref, *refs):
    mixed = jnp.concatenate([m[...] for m in refs[:4]], axis=1)
    *blocks, own_ref, gain_ref, out_ref, part_ref = refs[4:]
    rows = out_ref.shape[0]
    me = index_ref[0]
    for key in range(n_ctx):
        count = (4, 1)[key] if key < 2 else 2
        pieces = []
        for ref in [blocks.pop(0) for _ in range(count)]:
            block = ref[...]
            pieces.append(block.reshape(-1, block.shape[-1]))
        part_ref[me ^ key] = jnp.dot(
            mixed, jnp.concatenate(pieces, axis=0), preferred_element_type=F32
        )
    total = jnp.concatenate([part_ref[i] for i in range(n_ctx)], axis=1)
    total = total + own_ref[row0 : row0 + rows, :].astype(F32)
    mean_sq = jnp.mean(total * total, axis=-1, keepdims=True)
    out_ref[...] = (total * lax.rsqrt(mean_sq + 1e-06) * gain_ref[...]).astype(BF16)


def place_kernel(n_ctx, index_ref, *refs):
    place_refs = refs[:n_ctx]
    row_refs = refs[n_ctx:-1]
    out_ref = refs[-1]
    spots = out_ref.shape[0]
    chunks = len(row_refs) // n_ctx
    total = None
    for key in range(n_ctx):
        target = place_refs[key][...] - index_ref[0] * spots
        grid = lax.broadcasted_iota(jnp.int32, (spots, target.shape[1]), 0)
        chosen = one_hot(grid == target)
        for r in range(chunks):
            block = row_refs[key * chunks + r]
            count = block.shape[0]
            part = jnp.dot(
                chosen[:, r * count : (r + 1) * count], block[...], preferred_element_type=F32
            )
            total = part if total is None else total + part
    out_ref[...] = total.astype(BF16)


def together(*values):
    return lax.optimization_barrier(values)


def local(n_dp, n_ctx, n_ten, patches, valid, place, gain_attn, w_qkv, w_proj, gain_merge):
    rows, feat = patches.shape
    width = w_qkv.shape[2]
    groups = rows // 4
    ten = lax.axis_index("tensor")
    half = lax.axis_index("dp") % 2
    index = jnp.stack([lax.axis_index("context"), ten, half]).astype(jnp.int32)
    cross = list(cross_keys(n_ctx))

    def over_dp(x):
        return swap(x, "dp", n_dp, 1)

    def over_core(x):
        return swap(x, "context", n_ctx, 1)

    w3 = jnp.transpose(w_qkv, (1, 0, 2))
    first = gather_cross(lax.dynamic_index_in_dim(w3, half, 0, keepdims=False), n_ctx)
    value = gather_cross(w3[2], n_ctx)
    twin = over_core(w3)
    by_one = swap(w_proj, "tensor", n_ten, 1)
    by_two = swap(w_proj, "tensor", n_ten, 2)
    hidden, own_patches = pl.pallas_call(
        norm_kernel,
        out_shape=(
            jax.ShapeDtypeStruct((rows, feat), BF16),
            jax.ShapeDtypeStruct((groups, feat), BF16),
        ),
        in_specs=[SMEM, VMEM, VMEM],
        out_specs=(VMEM, VMEM),
        compiler_params=params(32),
        name="norm",
    )(index, patches, gain_attn.reshape(1, feat))
    first, by_one, twin, hidden = together(first, by_one, twin, hidden)

    second = {k: over_dp(first[k]) for k in cross}
    first_twin = {k: over_core(first[k]) for k in cross}
    low = gather_cross(jnp.stack([w_proj, by_one]), n_ctx)
    second, value, first_twin, by_two, w_proj = together(second, value, first_twin, by_two, w_proj)

    second_twin = {k: over_core(second[k]) for k in cross}
    value_twin = {k: over_core(value[k]) for k in cross}
    by_three = swap(w_proj, "tensor", n_ten, 3)
    places = gather_cross(place.reshape(1, groups), n_ctx)

    shard_list = [w3, twin]
    for k in cross:
        shard_list += [first[k], second[k], value[k], first_twin[k], second_twin[k], value_twin[k]]

    valid_pairs = valid.reshape(rows // PAIR, PAIR)
    part = rows // CHUNKS
    gain2 = gain_merge.reshape(1, feat)
    mix_shape = jax.ShapeDtypeStruct((n_ten, part // 4, width), BF16)
    scratch = [pltpu.VMEM((part, width), BF16)] * 4
    mixed, w_full = pl.pallas_call(
        functools.partial(first_attention_kernel, n_ctx),
        out_shape=(mix_shape, jax.ShapeDtypeStruct((3, feat, width), BF16)),
        in_specs=[SMEM] + [VMEM] * (2 + len(shard_list)),
        out_specs=(VMEM, VMEM),
        scratch_shapes=scratch,
        compiler_params=params(32),
        name="attention0",
    )(index, hidden, valid_pairs, *shard_list)
    def by_tensor(mixed):
        return [lax.dynamic_index_in_dim(mixed, ten ^ s, 0, keepdims=False) for s in range(n_ten)]

    def exchange(pieces):
        return [pieces[0]] + [swap(pieces[s], "tensor", n_ten, s) for s in range(1, n_ten)]

    pieces = by_tensor(mixed)
    pieces, by_three, low, places, w_proj = together(pieces, by_three, low, places, w_proj)
    received = [exchange(pieces)]
    high = gather_cross(jnp.stack([by_two, by_three]), n_ctx)
    own_twin = over_core(jnp.stack([w_proj, by_one, by_two, by_three]))
    for r in range(1, CHUNKS):
        received[r - 1][1], hidden = together(received[r - 1][1], hidden)
        mixed = pl.pallas_call(
            functools.partial(next_attention_kernel, r * part),
            out_shape=mix_shape,
            in_specs=[VMEM] * 3,
            out_specs=VMEM,
            scratch_shapes=scratch,
            compiler_params=params(32),
            name="attention" + str(r),
        )(hidden, valid_pairs, w_full)
        pieces, received[r - 1], own_twin, low = together(
            by_tensor(mixed), received[r - 1], own_twin, low
        )
        received.append(exchange(pieces))
    high, received[-1][1] = together(high, received[-1][1])

    blocks = [w_proj, by_one, by_two, by_three, own_twin]
    for k in cross:
        blocks += [low[k], high[k], over_core(low[k]), over_core(high[k])]
    gathered = []
    for r in range(CHUNKS):
        if r > 0:
            received[r], done = together(received[r], done)
        done = pl.pallas_call(
            functools.partial(project_kernel, n_ctx, r * (part // 4)),
            out_shape=jax.ShapeDtypeStruct((part // 4, feat), BF16),
            in_specs=[SMEM] + [VMEM] * (n_ten + len(blocks) + 2),
            out_specs=VMEM,
            scratch_shapes=[pltpu.VMEM((n_ctx, part // 4, w_proj.shape[1]), F32)],
            compiler_params=params(32),
            name="project" + str(r),
        )(index, *received[r], *blocks, own_patches, gain2)
        gathered.append(gather_xor(done, n_ctx))
    place_twin = over_core(jnp.stack([places[k] for k in (0, *cross)]))
    place_list = []
    for i, k in enumerate((0, *cross)):
        place_list += [places[k], place_twin[i]]
    return pl.pallas_call(
        functools.partial(place_kernel, n_ctx),
        out_shape=jax.ShapeDtypeStruct((groups, feat), BF16),
        in_specs=[SMEM] + [VMEM] * (n_ctx + n_ctx * CHUNKS),
        out_specs=VMEM,
        compiler_params=params(32),
        name="placement",
    )(index, *place_list, *[gathered[r][k] for k in range(n_ctx) for r in range(CHUNKS)])


def solution(mesh):
    in_specs = (
        P(("dp", "context"), None),
        P(("dp", "context")),
        P(("dp", "context")),
        P(),
        P("context", None, "tensor"),
        P("tensor", "context"),
        P(),
    )
    out_specs = P(("dp", "context"), "tensor")
    sizes = [mesh.shape[name] for name in ("dp", "context", "tensor")]
    body = functools.partial(local, *sizes)
    return jax.shard_map(body, mesh=mesh, in_specs=in_specs, out_specs=out_specs, check_vma=False)
```

```python
import functools

import jax
import jax.numpy as jnp
from jax import lax
from jax.experimental import pallas as pl
from jax.experimental.pallas import tpu as pltpu
from jax.sharding import PartitionSpec as P

HD = 80
WIN = 64
PAIR = 2 * WIN
CHUNKS = 2
F32 = jnp.float32
BF16 = jnp.bfloat16
ANY = pl.BlockSpec(memory_space=pl.ANY)
VMEM = pl.BlockSpec(memory_space=pltpu.VMEM)
SMEM = pl.BlockSpec(memory_space=pltpu.SMEM)


def params(mib):
    return pltpu.CompilerParams(vmem_limit_bytes=mib * 1024 * 1024)


def swap(x, axis, size, bit):
    return lax.ppermute(x, axis, [(i, i ^ bit) for i in range(size)])


def cross_keys(size):
    return range(2, size, 2)


def gather_cross(x, size):
    blocks = {0: x}
    bit = size // 2
    while bit > 1:
        for key in list(blocks):
            blocks[key ^ bit] = swap(blocks[key], "context", size, bit)
        bit //= 2
    return blocks


def gather_xor(x, size):
    blocks = gather_cross(x, size)
    for key in list(blocks):
        blocks[key ^ 1] = swap(blocks[key], "context", size, 1)
    return blocks


def one_hot(mask):
    return mask.astype(F32).astype(BF16)


def norm_kernel(index_ref, patches_ref, gain_ref, hidden_ref, own_ref):
    rows = patches_ref.shape[0]
    x = patches_ref[...]
    xf = x.astype(F32)
    mean_sq = jnp.mean(xf * xf, axis=-1, keepdims=True)
    hidden_ref[...] = (xf * lax.rsqrt(mean_sq + 1e-06) * gain_ref[...]).astype(BF16)
    step = 256
    pick = step // 4
    row = lax.broadcasted_iota(jnp.int32, (pick, step), 0)
    col = lax.broadcasted_iota(jnp.int32, (pick, step), 1)
    chosen = one_hot(col == 4 * row + index_ref[1])
    for i in range(rows // step):
        own_ref[i * pick : (i + 1) * pick, :] = jnp.dot(
            chosen, x[i * step : (i + 1) * step], preferred_element_type=F32
        ).astype(BF16)


def attend(row0, hidden_ref, valid_ref, w_ref, out_ref, q_ref, k_ref, v_ref, mix_ref):
    rows = q_ref.shape[0]
    width = q_ref.shape[1]
    heads = width // HD
    hidden = hidden_ref[row0 : row0 + rows, :]
    for j, ref in enumerate((q_ref, k_ref, v_ref)):
        ref[...] = jnp.dot(hidden, w_ref[j], preferred_element_type=F32).astype(BF16)
    lane = lax.broadcasted_iota(jnp.int32, (1, width), 1)
    head_masks = [one_hot((lane >= h * HD) & (lane < (h + 1) * HD)) for h in range(heads)]
    q_win = lax.broadcasted_iota(jnp.int32, (PAIR, PAIR), 0) // WIN
    k_win = lax.broadcasted_iota(jnp.int32, (PAIR, PAIR), 1) // WIN
    same = q_win == k_win
    floor = jnp.where(same, F32(-1e30), F32(-3e38))
    for p in range(rows // PAIR):
        at = p * PAIR
        q = q_ref[at : at + PAIR, :]
        k = k_ref[at : at + PAIR, :]
        v = v_ref[at : at + PAIR, :]
        k_all = jnp.concatenate([k * m for m in head_masks], axis=0)
        v_all = jnp.concatenate([v * m for m in head_masks], axis=0)
        scores = lax.dot_general(q, k_all, (((1,), (1,)), ((), ())), preferred_element_type=F32)
        live = valid_ref[row0 // PAIR + p : row0 // PAIR + p + 1, :] > 0
        weights = []
        for h in range(heads):
            s = scores[:, h * PAIR : (h + 1) * PAIR] * F32(HD ** (-0.5))
            s = jnp.where(same & live, s, floor)
            e = jnp.exp(s - jnp.max(s, axis=-1, keepdims=True))
            weights.append((e / jnp.sum(e, axis=-1, keepdims=True)).astype(BF16))
        w_all = jnp.concatenate(weights, axis=1)
        mix_ref[at : at + PAIR, :] = jnp.dot(w_all, v_all, preferred_element_type=F32).astype(BF16)
    pick = PAIR // 4
    src = lax.broadcasted_iota(jnp.int32, (PAIR, PAIR), 1)
    dst = lax.broadcasted_iota(jnp.int32, (PAIR, PAIR), 0)
    order = one_hot(src == 4 * (dst % pick) + dst // pick)
    for i in range(rows // PAIR):
        sorted_rows = jnp.dot(
            order, mix_ref[i * PAIR : (i + 1) * PAIR, :], preferred_element_type=F32
        ).astype(BF16)
        for t in range(4):
            out_ref[t, i * pick : (i + 1) * pick, :] = sorted_rows[t * pick : (t + 1) * pick]


def first_attention_kernel(n_ctx, index_ref, hidden_ref, valid_ref, *refs):
    shards = list(refs[: 2 + 3 * (n_ctx - 2)])
    out_ref, w_ref, *scratch, sem = refs[len(shards) :]
    depth = shards[0].shape[1]
    copies = []

    def bring(src, dst):
        copies.append(pltpu.make_async_copy(src, dst, sem.at[len(copies)]))
        copies[-1].start()

    me = index_ref[0]
    part = index_ref[2]
    for key in range(n_ctx):
        at = pl.multiple_of((me ^ key) * depth, depth)
        if key < 2:
            block = shards.pop(0)
            for j in range(3):
                bring(block.at[j], w_ref.at[j, pl.ds(at, depth), :])
        else:
            for j in (part, 1 - part, 2):
                bring(shards.pop(0), w_ref.at[j, pl.ds(at, depth), :])
    for copy in copies:
        copy.wait()
    attend(0, hidden_ref, valid_ref, w_ref, out_ref, *scratch)


def next_attention_kernel(row0, hidden_ref, valid_ref, w_ref, out_ref, *scratch):
    attend(row0, hidden_ref, valid_ref, w_ref, out_ref, *scratch)


def project_kernel(n_ctx, row0, index_ref, *refs):
    mix_ref, *blocks, own_ref, gain_ref, out_ref, part_ref = refs
    mixed = jnp.concatenate([mix_ref[index_ref[1] ^ s] for s in range(4)], axis=1)
    rows = out_ref.shape[0]
    me = index_ref[0]
    for key in range(n_ctx):
        count = (4, 1)[key] if key < 2 else 2
        pieces = []
        for ref in [blocks.pop(0) for _ in range(count)]:
            block = ref[...]
            pieces.append(block.reshape(-1, block.shape[-1]))
        part_ref[me ^ key] = jnp.dot(
            mixed, jnp.concatenate(pieces, axis=0), preferred_element_type=F32
        )
    total = jnp.concatenate([part_ref[i] for i in range(n_ctx)], axis=1)
    total = total + own_ref[row0 : row0 + rows, :].astype(F32)
    mean_sq = jnp.mean(total * total, axis=-1, keepdims=True)
    out_ref[...] = (total * lax.rsqrt(mean_sq + 1e-06) * gain_ref[...]).astype(BF16)


def place_kernel(n_ctx, index_ref, *refs):
    place_refs = refs[:n_ctx]
    row_refs = refs[n_ctx:-1]
    out_ref = refs[-1]
    spots = out_ref.shape[0]
    chunks = len(row_refs) // n_ctx
    total = None
    for key in range(n_ctx):
        target = place_refs[key][...] - index_ref[0] * spots
        grid = lax.broadcasted_iota(jnp.int32, (spots, target.shape[1]), 0)
        chosen = one_hot(grid == target)
        for r in range(chunks):
            block = row_refs[key * chunks + r]
            count = block.shape[0]
            part = jnp.dot(
                chosen[:, r * count : (r + 1) * count], block[...], preferred_element_type=F32
            )
            total = part if total is None else total + part
    out_ref[...] = total.astype(BF16)


def together(*values):
    return lax.optimization_barrier(values)


def local(n_dp, n_ctx, n_ten, patches, valid, place, gain_attn, w_qkv, w_proj, gain_merge):
    rows, feat = patches.shape
    width = w_qkv.shape[2]
    groups = rows // 4
    ten = lax.axis_index("tensor")
    half = lax.axis_index("dp") % 2
    index = jnp.stack([lax.axis_index("context"), ten, half]).astype(jnp.int32)
    cross = list(cross_keys(n_ctx))

    def over_dp(x):
        return swap(x, "dp", n_dp, 1)

    def over_core(x):
        return swap(x, "context", n_ctx, 1)

    w3 = jnp.transpose(w_qkv, (1, 0, 2))
    third = lax.dynamic_index_in_dim(w3, half, 0, keepdims=False)
    third, last, w_proj = together(third, w3[2], w_proj)
    first = gather_cross(third, n_ctx)
    value = gather_cross(last, n_ctx)
    twin = over_core(w3)
    by_one = swap(w_proj, "tensor", n_ten, 1)
    by_two = swap(w_proj, "tensor", n_ten, 2)
    hidden, own_patches = pl.pallas_call(
        norm_kernel,
        out_shape=(
            jax.ShapeDtypeStruct((rows, feat), BF16),
            jax.ShapeDtypeStruct((groups, feat), BF16),
        ),
        in_specs=[SMEM, VMEM, VMEM],
        out_specs=(VMEM, VMEM),
        compiler_params=params(32),
        name="norm",
    )(index, patches, gain_attn.reshape(1, feat))
    first, by_one, twin, hidden = together(first, by_one, twin, hidden)

    second = {k: over_dp(first[k]) for k in cross}
    first_twin = {k: over_core(first[k]) for k in cross}
    low = gather_cross(jnp.stack([w_proj, by_one]), n_ctx)
    second, value, first_twin, by_two, w_proj = together(second, value, first_twin, by_two, w_proj)

    second_twin = {k: over_core(second[k]) for k in cross}
    value_twin = {k: over_core(value[k]) for k in cross}
    by_three = swap(w_proj, "tensor", n_ten, 3)
    places = gather_cross(place.reshape(1, groups), n_ctx)

    shard_list = [w3, twin]
    for k in cross:
        shard_list += [first[k], second[k], value[k], first_twin[k], second_twin[k], value_twin[k]]

    valid_pairs = valid.reshape(rows // PAIR, PAIR)
    part = rows // CHUNKS
    gain2 = gain_merge.reshape(1, feat)
    mix_shape = jax.ShapeDtypeStruct((n_ten, part // 4, width), BF16)
    scratch = [pltpu.VMEM((part, width), BF16)] * 4
    mixed, w_full = pl.pallas_call(
        functools.partial(first_attention_kernel, n_ctx),
        out_shape=(mix_shape, jax.ShapeDtypeStruct((3, feat, width), BF16)),
        in_specs=[SMEM, VMEM, VMEM] + [ANY] * len(shard_list),
        out_specs=(VMEM, VMEM),
        scratch_shapes=scratch + [pltpu.SemaphoreType.DMA((3 * n_ctx,))],
        compiler_params=params(32),
        name="attention0",
    )(index, hidden, valid_pairs, *shard_list)
    def exchange(mixed):
        return lax.all_to_all(mixed, "tensor", 0, 0, tiled=True)

    mixed, by_three, low, places, w_proj = together(mixed, by_three, low, places, w_proj)
    received = [exchange(mixed)]
    high = gather_cross(jnp.stack([by_two, by_three]), n_ctx)
    own_twin = over_core(jnp.stack([w_proj, by_one, by_two, by_three]))
    for r in range(1, CHUNKS):
        mixed = pl.pallas_call(
            functools.partial(next_attention_kernel, r * part),
            out_shape=mix_shape,
            in_specs=[VMEM] * 3,
            out_specs=VMEM,
            scratch_shapes=scratch,
            compiler_params=params(32),
            name="attention" + str(r),
        )(hidden, valid_pairs, w_full)
        mixed, own_twin, low = together(mixed, own_twin, low)
        received.append(exchange(mixed))

    place_twin = over_core(jnp.stack([places[k] for k in (0, *cross)]))
    received[0], place_twin = together(received[0], place_twin)
    blocks = [w_proj, by_one, by_two, by_three, own_twin]
    for k in cross:
        blocks += [low[k], high[k], over_core(low[k]), over_core(high[k])]
    gathered = []
    for r in range(CHUNKS):
        if r > 0:
            received[r], done = together(received[r], done)
        done = pl.pallas_call(
            functools.partial(project_kernel, n_ctx, r * (part // 4)),
            out_shape=jax.ShapeDtypeStruct((part // 4, feat), BF16),
            in_specs=[SMEM] + [VMEM] * (1 + len(blocks) + 2),
            out_specs=VMEM,
            scratch_shapes=[pltpu.VMEM((n_ctx, part // 4, w_proj.shape[1]), F32)],
            compiler_params=params(32),
            name="project" + str(r),
        )(index, received[r], *blocks, own_patches, gain2)
        gathered.append(gather_xor(done, n_ctx))
    place_list = []
    for i, k in enumerate((0, *cross)):
        place_list += [places[k], place_twin[i]]
    return pl.pallas_call(
        functools.partial(place_kernel, n_ctx),
        out_shape=jax.ShapeDtypeStruct((groups, feat), BF16),
        in_specs=[SMEM] + [VMEM] * (n_ctx + n_ctx * CHUNKS),
        out_specs=VMEM,
        compiler_params=params(32),
        name="placement",
    )(index, *place_list, *[gathered[r][k] for k in range(n_ctx) for r in range(CHUNKS)])


def solution(mesh):
    in_specs = (
        P(("dp", "context"), None),
        P(("dp", "context")),
        P(("dp", "context")),
        P(),
        P("context", None, "tensor"),
        P("tensor", "context"),
        P(),
    )
    out_specs = P(("dp", "context"), "tensor")
    sizes = [mesh.shape[name] for name in ("dp", "context", "tensor")]
    body = functools.partial(local, *sizes)
    return jax.shard_map(body, mesh=mesh, in_specs=in_specs, out_specs=out_specs, check_vma=False)
```

```python
import functools

import jax
import jax.numpy as jnp
from jax import lax
from jax.experimental import pallas as pl
from jax.experimental.pallas import tpu as pltpu
from jax.sharding import PartitionSpec as P

HD = 80
WIN = 64
PAIR = 2 * WIN
LANES = 128
CHUNKS = 2
F32 = jnp.float32
BF16 = jnp.bfloat16
VMEM = pl.BlockSpec(memory_space=pltpu.VMEM)
SMEM = pl.BlockSpec(memory_space=pltpu.SMEM)


def params(mib):
    return pltpu.CompilerParams(vmem_limit_bytes=mib * 1024 * 1024)


def swap(x, axis, size, bit):
    return lax.ppermute(x, axis, [(i, i ^ bit) for i in range(size)])


def cross_keys(size):
    return range(2, size, 2)


def gather_cross(x, size):
    blocks = {0: x}
    bit = size // 2
    while bit > 1:
        for key in list(blocks):
            blocks[key ^ bit] = swap(blocks[key], "context", size, bit)
        bit //= 2
    return blocks


def gather_xor(x, size):
    blocks = gather_cross(x, size)
    for key in list(blocks):
        blocks[key ^ 1] = swap(blocks[key], "context", size, 1)
    return blocks


def together(*values):
    return lax.optimization_barrier(values)


def one_hot(mask):
    return mask.astype(F32).astype(BF16)


def shape(*dims):
    return jax.ShapeDtypeStruct(dims, BF16)


def packs(rows, cols):
    return rows % 32 == 0 and cols == 2 * LANES + LANES // 2


def packed_shape(rows, cols):
    return (rows * 5 // 2, LANES) if packs(rows, cols) else (rows, cols)


def pack(x):
    rows, cols = x.shape
    if not packs(rows, cols):
        return x
    rest = x[:, 2 * LANES :]
    tail = jnp.concatenate([rest[: rows // 2], rest[rows // 2 :]], axis=1)
    return jnp.concatenate([x[:, :LANES], x[:, LANES : 2 * LANES], tail], axis=0)


def unpack(p, rows, cols):
    if not packs(rows, cols):
        return p[:, : 2 * LANES], p[:, 2 * LANES :]
    tail = p[2 * rows :]
    rest = jnp.concatenate([tail[:, : LANES // 2], tail[:, LANES // 2 :]], axis=0)
    return jnp.concatenate([p[:rows], p[rows : 2 * rows]], axis=1), rest


def pack_kernel(index_ref, qkv_ref, proj_ref, first_ref, value_ref, all_ref, proj_out_ref):
    for j in range(3):
        all_ref[j] = pack(qkv_ref[j])
    first_ref[...] = all_ref[index_ref[2]]
    value_ref[...] = all_ref[2]
    proj_out_ref[...] = pack(proj_ref[...])


def norm_kernel(index_ref, patches_ref, gain_ref, hidden_ref, own_ref):
    rows = patches_ref.shape[0]
    x = patches_ref[...]
    xf = x.astype(F32)
    mean_sq = jnp.mean(xf * xf, axis=-1, keepdims=True)
    hidden_ref[...] = (xf * lax.rsqrt(mean_sq + 1e-06) * gain_ref[...]).astype(BF16)
    step = 256
    pick = step // 4
    row = lax.broadcasted_iota(jnp.int32, (pick, step), 0)
    col = lax.broadcasted_iota(jnp.int32, (pick, step), 1)
    chosen = one_hot(col == 4 * row + index_ref[1])
    for i in range(rows // step):
        own_ref[i * pick : (i + 1) * pick, :] = jnp.dot(
            chosen, x[i * step : (i + 1) * step], preferred_element_type=F32
        ).astype(BF16)


def attend(row0, index_ref, hidden_ref, valid_ref, w_ref, out_refs, q_ref, k_ref, v_ref, mix_ref):
    rows, width = q_ref.shape
    heads = width // HD
    main = 2 * LANES
    rest = width - main
    qkv = jnp.dot(hidden_ref[row0 : row0 + rows, :], w_ref[...], preferred_element_type=F32)
    for j, ref in enumerate((q_ref, k_ref, v_ref)):
        ref[:, :main] = qkv[:, j * main : (j + 1) * main].astype(BF16)
        at = 3 * main + j * rest
        ref[:, main:] = qkv[:, at : at + rest].astype(BF16)
    lane = lax.broadcasted_iota(jnp.int32, (1, width), 1)
    head_masks = [one_hot((lane >= h * HD) & (lane < (h + 1) * HD)) for h in range(heads)]
    q_win = lax.broadcasted_iota(jnp.int32, (PAIR, PAIR), 0) // WIN
    k_win = lax.broadcasted_iota(jnp.int32, (PAIR, PAIR), 1) // WIN
    same = q_win == k_win
    floor = jnp.where(same, F32(-1e30), F32(-3e38))
    pick = PAIR // 4
    src = lax.broadcasted_iota(jnp.int32, (PAIR, PAIR), 1)
    dst = lax.broadcasted_iota(jnp.int32, (PAIR, PAIR), 0)
    order = one_hot(src == 4 * (dst % pick) + dst // pick)
    for p in range(rows // PAIR):
        at = p * PAIR
        q = q_ref[at : at + PAIR, :]
        k = k_ref[at : at + PAIR, :]
        v = v_ref[at : at + PAIR, :]
        k_all = jnp.concatenate([k * m for m in head_masks], axis=0)
        v_all = jnp.concatenate([v * m for m in head_masks], axis=0)
        scores = lax.dot_general(q, k_all, (((1,), (1,)), ((), ())), preferred_element_type=F32)
        live = valid_ref[row0 // PAIR + p : row0 // PAIR + p + 1, :] > 0
        weights = []
        for h in range(heads):
            s = scores[:, h * PAIR : (h + 1) * PAIR] * F32(HD ** (-0.5))
            s = jnp.where(same & live, s, floor)
            e = jnp.exp(s - jnp.max(s, axis=-1, keepdims=True))
            weights.append((e / jnp.sum(e, axis=-1, keepdims=True)).astype(BF16))
        w_all = jnp.concatenate(weights, axis=1)
        mixed = jnp.dot(w_all, v_all, preferred_element_type=F32).astype(BF16)
        mixed = jnp.dot(order, mixed, preferred_element_type=F32).astype(BF16)
        for t in range(4):
            mix_ref[t, p * pick : (p + 1) * pick, :] = mixed[t * pick : (t + 1) * pick]
    for s, out_ref in enumerate(out_refs):
        out_ref[...] = pack(mix_ref[index_ref[1] ^ s])


def first_attention_kernel(n_ctx, width, index_ref, hidden_ref, valid_ref, *refs):
    shards = list(refs[: 2 + 3 * (n_ctx - 2)])
    *out_refs, w_ref, q_ref, k_ref, v_ref, mix_ref = refs[len(shards) :]
    depth = w_ref.shape[0] // n_ctx
    me = index_ref[0]
    flip = index_ref[2] > 0
    main = 2 * LANES
    for key in range(n_ctx):
        rows = pl.ds(pl.multiple_of((me ^ key) * depth, depth), depth)
        if key < 2:
            block = shards.pop(0)
            thirds = [block[j] for j in range(3)]
        else:
            first, second, value = [shards.pop(0)[...] for _ in range(3)]
            thirds = [jnp.where(flip, second, first), jnp.where(flip, first, second), value]
        tails = []
        for j, third in enumerate(thirds):
            w_ref[rows, j * main : (j + 1) * main], tail = unpack(third, depth, width)
            tails.append(tail)
        w_ref[rows, 3 * main :] = jnp.concatenate(tails, axis=1)
    attend(0, index_ref, hidden_ref, valid_ref, w_ref, out_refs, q_ref, k_ref, v_ref, mix_ref)


def next_attention_kernel(row0, index_ref, hidden_ref, valid_ref, w_ref, *refs):
    *out_refs, q_ref, k_ref, v_ref, mix_ref = refs
    attend(row0, index_ref, hidden_ref, valid_ref, w_ref, out_refs, q_ref, k_ref, v_ref, mix_ref)


def project_kernel(n_ctx, row0, width, col, index_ref, *refs):
    mixes = [unpack(m[...], refs[-2].shape[0], width) for m in refs[:4]]
    *blocks, own_ref, gain_ref, out_ref, part_ref = refs[4:]
    rows = out_ref.shape[0]
    me = index_ref[0]
    main = 2 * LANES
    mixed = jnp.concatenate([m for m, _ in mixes] + [r for _, r in mixes], axis=1)
    mains = []
    rests = []
    for key in range(n_ctx):
        pieces = []
        for ref in [blocks.pop(0) for _ in range((4, 1)[key] if key < 2 else 2)]:
            pieces += [ref[...]] if len(ref.shape) == 2 else [ref[i] for i in range(ref.shape[0])]
        halves = [unpack(p, width, col) for p in pieces]
        both = []
        for half in ([h[0] for h in halves], [h[1] for h in halves]):
            both.append(jnp.concatenate([h[:main] for h in half] + [h[main:] for h in half], axis=0))
        mains.append(jnp.dot(mixed, both[0], preferred_element_type=F32))
        rests.append(both[1])
    if rests[0].shape[1]:
        rest = jnp.dot(mixed, jnp.concatenate(rests, axis=1), preferred_element_type=F32)
        count = rests[0].shape[1]
        mains = [
            jnp.concatenate([m, rest[:, key * count : (key + 1) * count]], axis=1)
            for key, m in enumerate(mains)
        ]
    for key in range(n_ctx):
        part_ref[me ^ key] = mains[key]
    total = jnp.concatenate([part_ref[i] for i in range(n_ctx)], axis=1)
    total = total + own_ref[row0 : row0 + rows, :].astype(F32)
    mean_sq = jnp.mean(total * total, axis=-1, keepdims=True)
    out_ref[...] = (total * lax.rsqrt(mean_sq + 1e-06) * gain_ref[...]).astype(BF16)


def place_kernel(n_ctx, index_ref, *refs):
    place_refs = refs[:n_ctx]
    row_refs = refs[n_ctx:-1]
    out_ref = refs[-1]
    spots = out_ref.shape[0]
    chosen = []
    for place_ref in place_refs:
        target = place_ref[...] - index_ref[0] * spots
        grid = lax.broadcasted_iota(jnp.int32, (spots, target.shape[1]), 0)
        chosen.append(one_hot(grid == target))
    out_ref[...] = jnp.dot(
        jnp.concatenate(chosen, axis=1),
        jnp.concatenate([ref[...] for ref in row_refs], axis=0),
        preferred_element_type=F32,
    ).astype(BF16)


def local(n_dp, n_ctx, n_ten, patches, valid, place, gain_attn, w_qkv, w_proj, gain_merge):
    rows, feat = patches.shape
    depth, _, width = w_qkv.shape
    col = w_proj.shape[1]
    groups = rows // 4
    ten = lax.axis_index("tensor")
    half = lax.axis_index("dp") % 2
    index = jnp.stack([lax.axis_index("context"), ten, half]).astype(jnp.int32)
    cross = list(cross_keys(n_ctx))

    def over_dp(x):
        return swap(x, "dp", n_dp, 1)

    def over_core(x):
        return swap(x, "context", n_ctx, 1)

    third = packed_shape(depth, width)
    piece = packed_shape(width, col)
    first, value, own, w_proj = pl.pallas_call(
        pack_kernel,
        out_shape=(shape(*third), shape(*third), shape(3, *third), shape(*piece)),
        in_specs=[SMEM, VMEM, VMEM],
        out_specs=(VMEM,) * 4,
        compiler_params=params(8),
        name="pack",
    )(index, jnp.transpose(w_qkv, (1, 0, 2)), w_proj)
    first = gather_cross(first, n_ctx)
    value = gather_cross(value, n_ctx)
    twin = over_core(own)
    by_one = swap(w_proj, "tensor", n_ten, 1)
    by_two = swap(w_proj, "tensor", n_ten, 2)
    hidden, own_patches = pl.pallas_call(
        norm_kernel,
        out_shape=(shape(rows, feat), shape(groups, feat)),
        in_specs=[SMEM, VMEM, VMEM],
        out_specs=(VMEM, VMEM),
        compiler_params=params(16),
        name="norm",
    )(index, patches, gain_attn.reshape(1, feat))
    first, twin, hidden = together(first, twin, hidden)

    second = {k: over_dp(first[k]) for k in cross}
    first_twin = {k: over_core(first[k]) for k in cross}
    by_one, first = together(by_one, first)
    low = gather_cross(jnp.stack([w_proj, by_one]), n_ctx)
    second, value, first_twin = together(second, value, first_twin)

    second_twin = {k: over_core(second[k]) for k in cross}
    value_twin = {k: over_core(value[k]) for k in cross}
    by_two, w_proj, place = together(by_two, w_proj, place, second, value)[:3]
    by_three = swap(w_proj, "tensor", n_ten, 3)
    places = gather_cross(place.reshape(1, groups), n_ctx)

    shard_list = [own, twin]
    for k in cross:
        shard_list += [first[k], second[k], value[k], first_twin[k], second_twin[k], value_twin[k]]

    valid_pairs = valid.reshape(rows // PAIR, PAIR)
    part = rows // CHUNKS
    gain2 = gain_merge.reshape(1, feat)
    mix_shapes = (shape(*packed_shape(part // 4, width)),) * n_ten
    scratch = [pltpu.VMEM((part, width), BF16)] * 3 + [pltpu.VMEM((4, part // 4, width), BF16)]
    *mixed, w_full = pl.pallas_call(
        functools.partial(first_attention_kernel, n_ctx, width),
        out_shape=mix_shapes + (shape(feat, 3 * width),),
        in_specs=[SMEM] + [VMEM] * (2 + len(shard_list)),
        out_specs=(VMEM,) * (n_ten + 1),
        scratch_shapes=scratch,
        compiler_params=params(16),
        name="attention0",
    )(index, hidden, valid_pairs, *shard_list)

    def exchange(pieces):
        return [pieces[0]] + [swap(pieces[s], "tensor", n_ten, s) for s in range(1, n_ten)]

    mixed, by_three, low, places = together(mixed, by_three, low, places)
    received = [exchange(mixed)]
    high = gather_cross(jnp.stack([by_two, by_three]), n_ctx)
    own_twin = over_core(jnp.stack([w_proj, by_one, by_two, by_three]))
    place_twin = over_core(jnp.stack([places[k] for k in (0, *cross)]))
    for r in range(1, CHUNKS):
        received[r - 1][1], hidden = together(received[r - 1][1], hidden)
        mixed = pl.pallas_call(
            functools.partial(next_attention_kernel, r * part),
            out_shape=mix_shapes,
            in_specs=[SMEM, VMEM, VMEM, VMEM],
            out_specs=(VMEM,) * n_ten,
            scratch_shapes=scratch,
            compiler_params=params(12),
            name="attention" + str(r),
        )(index, hidden, valid_pairs, w_full)
        mixed, received[r - 1], own_twin, low = together(mixed, received[r - 1], own_twin, low)
        received.append(exchange(mixed))
    high, received[-1][1], place_twin = together(high, received[-1][1], place_twin)

    blocks = [w_proj, by_one, by_two, by_three, own_twin]
    for k in cross:
        blocks += [low[k], high[k], over_core(low[k]), over_core(high[k])]
    gathered = []
    for r in range(CHUNKS):
        if r > 0:
            received[r], done = together(received[r], done)
        done = pl.pallas_call(
            functools.partial(project_kernel, n_ctx, r * (part // 4), width, col),
            out_shape=shape(part // 4, feat),
            in_specs=[SMEM] + [VMEM] * (n_ten + len(blocks) + 2),
            out_specs=VMEM,
            scratch_shapes=[pltpu.VMEM((n_ctx, part // 4, col), F32)],
            compiler_params=params(20),
            name="project" + str(r),
        )(index, *received[r], *blocks, own_patches, gain2)
        gathered.append(gather_xor(done, n_ctx))
    place_list = []
    for i, k in enumerate((0, *cross)):
        place_list += [places[k], place_twin[i]]
    return pl.pallas_call(
        functools.partial(place_kernel, n_ctx),
        out_shape=shape(groups, feat),
        in_specs=[SMEM] + [VMEM] * (n_ctx + n_ctx * CHUNKS),
        out_specs=VMEM,
        compiler_params=params(28),
        name="placement",
    )(index, *place_list, *[gathered[r][k] for k in range(n_ctx) for r in range(CHUNKS)])


def solution(mesh):
    in_specs = (
        P(("dp", "context"), None),
        P(("dp", "context")),
        P(("dp", "context")),
        P(),
        P("context", None, "tensor"),
        P("tensor", "context"),
        P(),
    )
    out_specs = P(("dp", "context"), "tensor")
    sizes = [mesh.shape[name] for name in ("dp", "context", "tensor")]
    body = functools.partial(local, *sizes)
    return jax.shard_map(body, mesh=mesh, in_specs=in_specs, out_specs=out_specs, check_vma=False)
```

```python
import functools

import jax
import jax.numpy as jnp
from jax import lax
from jax.experimental import pallas as pl
from jax.experimental.pallas import tpu as pltpu
from jax.sharding import PartitionSpec as P

HD = 80
WIN = 64
PAIR = 2 * WIN
LANES = 128
CHUNKS = 2
F32 = jnp.float32
BF16 = jnp.bfloat16
ANY = pl.BlockSpec(memory_space=pl.ANY)
VMEM = pl.BlockSpec(memory_space=pltpu.VMEM)
SMEM = pl.BlockSpec(memory_space=pltpu.SMEM)


def params(mib):
    return pltpu.CompilerParams(vmem_limit_bytes=mib * 1024 * 1024)


def cost(us):
    return pl.CostEstimate(flops=int(us * 1e9), bytes_accessed=int(us * 3.3e6), transcendentals=0)


def swap(x, axis, size, bit):
    return lax.ppermute(x, axis, [(i, i ^ bit) for i in range(size)])


def cross_keys(size):
    return range(2, size, 2)


def gather_cross(x, size):
    blocks = {0: x}
    bit = size // 2
    while bit > 1:
        for key in list(blocks):
            blocks[key ^ bit] = swap(blocks[key], "context", size, bit)
        bit //= 2
    return blocks


def gather_xor(x, size):
    blocks = gather_cross(x, size)
    for key in list(blocks):
        blocks[key ^ 1] = swap(blocks[key], "context", size, 1)
    return blocks


def together(*values):
    return lax.optimization_barrier(values)


def one_hot(mask):
    return mask.astype(F32).astype(BF16)


def shape(*dims):
    return jax.ShapeDtypeStruct(dims, BF16)


def packs(rows, cols):
    return rows % 32 == 0 and cols == 2 * LANES + LANES // 2


def packed_shape(rows, cols):
    return (rows * 5 // 2, LANES) if packs(rows, cols) else (rows, cols)


def pack(x):
    rows, cols = x.shape
    if not packs(rows, cols):
        return x
    rest = x[:, 2 * LANES :]
    tail = jnp.concatenate([rest[: rows // 2], rest[rows // 2 :]], axis=1)
    return jnp.concatenate([x[:, :LANES], x[:, LANES : 2 * LANES], tail], axis=0)


def unpack(p, rows, cols):
    if not packs(rows, cols):
        return p[:, : 2 * LANES], p[:, 2 * LANES :]
    tail = p[2 * rows :]
    rest = jnp.concatenate([tail[:, : LANES // 2], tail[:, LANES // 2 :]], axis=0)
    return jnp.concatenate([p[:rows], p[rows : 2 * rows]], axis=1), rest


def pack_kernel(
    index_ref, qkv_any, proj_any, first_ref, value_ref, all_ref, proj_out_ref, qkv_ref, proj_ref, sem
):
    copies = [pltpu.make_async_copy(qkv_any.at[j], qkv_ref.at[j], sem.at[j]) for j in range(3)]
    copies.append(pltpu.make_async_copy(proj_any, proj_ref, sem.at[3]))
    for copy in copies:
        copy.start()
    for j in range(3):
        copies[j].wait()
        all_ref[j] = pack(qkv_ref[j])
    first_ref[...] = all_ref[index_ref[2]]
    value_ref[...] = all_ref[2]
    copies[3].wait()
    proj_out_ref[...] = pack(proj_ref[...])


def norm_kernel(index_ref, patches_any, gain_ref, hidden_ref, own_ref, x_ref, sem):
    step = 256
    count = x_ref.shape[0] // step
    copies = []
    for i in range(count):
        rows = pl.ds(i * step, step)
        copies.append(pltpu.make_async_copy(patches_any.at[rows], x_ref.at[rows], sem.at[i]))
        copies[i].start()
    gain = gain_ref[...].reshape(1, -1)
    pick = step // 4
    row = lax.broadcasted_iota(jnp.int32, (pick, step), 0)
    col = lax.broadcasted_iota(jnp.int32, (pick, step), 1)
    chosen = one_hot(col == 4 * row + index_ref[1])
    for i in range(count):
        copies[i].wait()
        x = x_ref[i * step : (i + 1) * step, :]
        xf = x.astype(F32)
        mean_sq = jnp.mean(xf * xf, axis=-1, keepdims=True)
        hidden_ref[i * step : (i + 1) * step, :] = (
            xf * lax.rsqrt(mean_sq + 1e-06) * gain
        ).astype(BF16)
        own_ref[i * pick : (i + 1) * pick, :] = jnp.dot(
            chosen, x, preferred_element_type=F32
        ).astype(BF16)


def attend(row0, index_ref, hidden_ref, valid_ref, w_ref, out_refs, q_ref, k_ref, v_ref, mix_ref):
    rows, width = q_ref.shape
    heads = width // HD
    main = 2 * LANES
    rest = width - main
    qkv = jnp.dot(hidden_ref[row0 : row0 + rows, :], w_ref[...], preferred_element_type=F32)
    for j, ref in enumerate((q_ref, k_ref, v_ref)):
        ref[:, :main] = qkv[:, j * main : (j + 1) * main].astype(BF16)
        at = 3 * main + j * rest
        ref[:, main:] = qkv[:, at : at + rest].astype(BF16)
    lane = lax.broadcasted_iota(jnp.int32, (1, width), 1)
    head_masks = [one_hot((lane >= h * HD) & (lane < (h + 1) * HD)) for h in range(heads)]
    q_win = lax.broadcasted_iota(jnp.int32, (PAIR, PAIR), 0) // WIN
    k_win = lax.broadcasted_iota(jnp.int32, (PAIR, PAIR), 1) // WIN
    same = q_win == k_win
    floor = jnp.where(same, F32(-1e30), F32(-3e38))
    pick = PAIR // 4
    src = lax.broadcasted_iota(jnp.int32, (PAIR, PAIR), 1)
    dst = lax.broadcasted_iota(jnp.int32, (PAIR, PAIR), 0)
    order = one_hot(src == 4 * (dst % pick) + dst // pick)
    for p in range(rows // PAIR):
        at = p * PAIR
        q = q_ref[at : at + PAIR, :]
        k = k_ref[at : at + PAIR, :]
        v = v_ref[at : at + PAIR, :]
        k_all = jnp.concatenate([k * m for m in head_masks], axis=0)
        v_all = jnp.concatenate([v * m for m in head_masks], axis=0)
        scores = lax.dot_general(q, k_all, (((1,), (1,)), ((), ())), preferred_element_type=F32)
        live = valid_ref[row0 // PAIR + p : row0 // PAIR + p + 1, :] > 0
        weights = []
        for h in range(heads):
            s = scores[:, h * PAIR : (h + 1) * PAIR] * F32(HD ** (-0.5))
            s = jnp.where(same & live, s, floor)
            e = jnp.exp(s - jnp.max(s, axis=-1, keepdims=True))
            weights.append((e / jnp.sum(e, axis=-1, keepdims=True)).astype(BF16))
        w_all = jnp.concatenate(weights, axis=1)
        mixed = jnp.dot(w_all, v_all, preferred_element_type=F32).astype(BF16)
        mixed = jnp.dot(order, mixed, preferred_element_type=F32).astype(BF16)
        for t in range(4):
            mix_ref[t, p * pick : (p + 1) * pick, :] = mixed[t * pick : (t + 1) * pick]
    for s, out_ref in enumerate(out_refs):
        out_ref[...] = pack(mix_ref[index_ref[1] ^ s])


def first_attention_kernel(n_ctx, width, index_ref, hidden_ref, valid_ref, *refs):
    shards = list(refs[: 2 + 3 * (n_ctx - 2)])
    *out_refs, w_ref, q_ref, k_ref, v_ref, mix_ref = refs[len(shards) :]
    depth = w_ref.shape[0] // n_ctx
    me = index_ref[0]
    flip = index_ref[2] > 0
    main = 2 * LANES
    for key in range(n_ctx):
        rows = pl.ds(pl.multiple_of((me ^ key) * depth, depth), depth)
        if key < 2:
            block = shards.pop(0)
            thirds = [block[j] for j in range(3)]
        else:
            first, second, value = [shards.pop(0)[...] for _ in range(3)]
            thirds = [jnp.where(flip, second, first), jnp.where(flip, first, second), value]
        tails = []
        for j, third in enumerate(thirds):
            w_ref[rows, j * main : (j + 1) * main], tail = unpack(third, depth, width)
            tails.append(tail)
        w_ref[rows, 3 * main :] = jnp.concatenate(tails, axis=1)
    attend(0, index_ref, hidden_ref, valid_ref, w_ref, out_refs, q_ref, k_ref, v_ref, mix_ref)


def next_attention_kernel(row0, index_ref, hidden_ref, valid_ref, w_ref, *refs):
    *out_refs, q_ref, k_ref, v_ref, mix_ref = refs
    attend(row0, index_ref, hidden_ref, valid_ref, w_ref, out_refs, q_ref, k_ref, v_ref, mix_ref)


def project_kernel(n_ctx, row0, width, col, index_ref, *refs):
    mixes = [unpack(m[...], refs[-2].shape[0], width) for m in refs[:4]]
    flip = index_ref[2] > 0
    mixes[2:] = [
        [jnp.where(flip, b, a) for a, b in zip(mixes[2], mixes[3])],
        [jnp.where(flip, a, b) for a, b in zip(mixes[2], mixes[3])],
    ]
    *blocks, own_ref, gain_ref, out_ref, part_ref = refs[4:]
    rows = out_ref.shape[0]
    me = index_ref[0]
    main = 2 * LANES
    mixed = jnp.concatenate([m for m, _ in mixes] + [r for _, r in mixes], axis=1)
    mains = []
    rests = []
    for key in range(n_ctx):
        pieces = []
        for ref in [blocks.pop(0) for _ in range((4, 1)[key] if key < 2 else 2)]:
            pieces += [ref[...]] if len(ref.shape) == 2 else [ref[i] for i in range(ref.shape[0])]
        halves = [unpack(p, width, col) for p in pieces]
        both = []
        for half in ([h[0] for h in halves], [h[1] for h in halves]):
            both.append(jnp.concatenate([h[:main] for h in half] + [h[main:] for h in half], axis=0))
        mains.append(jnp.dot(mixed, both[0], preferred_element_type=F32))
        rests.append(both[1])
    if rests[0].shape[1]:
        rest = jnp.dot(mixed, jnp.concatenate(rests, axis=1), preferred_element_type=F32)
        count = rests[0].shape[1]
        mains = [
            jnp.concatenate([m, rest[:, key * count : (key + 1) * count]], axis=1)
            for key, m in enumerate(mains)
        ]
    for key in range(n_ctx):
        part_ref[me ^ key] = mains[key]
    total = jnp.concatenate([part_ref[i] for i in range(n_ctx)], axis=1)
    total = total + own_ref[row0 : row0 + rows, :].astype(F32)
    mean_sq = jnp.mean(total * total, axis=-1, keepdims=True)
    out_ref[...] = (total * lax.rsqrt(mean_sq + 1e-06) * gain_ref[...].reshape(1, -1)).astype(BF16)


def place_kernel(n_ctx, index_ref, *refs):
    place_refs = refs[:n_ctx]
    row_refs = refs[n_ctx:-1]
    out_ref = refs[-1]
    spots = out_ref.shape[0]
    chosen = []
    for place_ref in place_refs:
        target = place_ref[...] - index_ref[0] * spots
        grid = lax.broadcasted_iota(jnp.int32, (spots, target.shape[1]), 0)
        chosen.append(one_hot(grid == target))
    out_ref[...] = jnp.dot(
        jnp.concatenate(chosen, axis=1),
        jnp.concatenate([ref[...] for ref in row_refs], axis=0),
        preferred_element_type=F32,
    ).astype(BF16)


def local(n_dp, n_ctx, n_ten, patches, valid, place, gain_attn, w_qkv, w_proj, gain_merge):
    rows, feat = patches.shape
    depth, _, width = w_qkv.shape
    col = w_proj.shape[1]
    groups = rows // 4
    ten = lax.axis_index("tensor")
    half = lax.axis_index("dp") % 2
    index = jnp.stack([lax.axis_index("context"), ten, half]).astype(jnp.int32)
    cross = list(cross_keys(n_ctx))

    def over_dp(x):
        return swap(x, "dp", n_dp, 1)

    def over_core(x):
        return swap(x, "context", n_ctx, 1)

    third = packed_shape(depth, width)
    piece = packed_shape(width, col)
    first, value, own, w_proj = pl.pallas_call(
        pack_kernel,
        out_shape=(shape(*third), shape(*third), shape(3, *third), shape(*piece)),
        in_specs=[SMEM, ANY, ANY],
        out_specs=(VMEM,) * 4,
        scratch_shapes=[
            pltpu.VMEM((3, depth, width), BF16),
            pltpu.VMEM((width, col), BF16),
            pltpu.SemaphoreType.DMA((4,)),
        ],
        compiler_params=params(8),
        cost_estimate=cost(1),
        name="pack",
    )(index, jnp.transpose(w_qkv, (1, 0, 2)), w_proj)
    first = gather_cross(first, n_ctx)
    value = gather_cross(value, n_ctx)
    twin = over_core(own)
    far = lax.ppermute(
        w_proj,
        ("dp", "tensor"),
        [
            (d * n_ten + t, d * n_ten + (t ^ (2 + d % 2)))
            for d in range(n_dp)
            for t in range(n_ten)
        ],
    )
    by_one = swap(w_proj, "tensor", n_ten, 1)
    first, twin, patches = together(first, twin, patches)

    second = {k: over_dp(first[k]) for k in cross}
    first_twin = {k: over_core(first[k]) for k in cross}
    hidden, own_patches = pl.pallas_call(
        norm_kernel,
        out_shape=(shape(rows, feat), shape(groups, feat)),
        in_specs=[SMEM, ANY, VMEM],
        out_specs=(VMEM, VMEM),
        scratch_shapes=[pltpu.VMEM((rows, feat), BF16), pltpu.SemaphoreType.DMA((rows // 256,))],
        compiler_params=params(16),
        cost_estimate=cost(2),
        name="norm",
    )(index, patches, gain_attn)
    low = gather_cross(jnp.stack([w_proj, by_one]), n_ctx)
    second, value, first_twin = together(second, value, first_twin)

    second_twin = {k: over_core(second[k]) for k in cross}
    value_twin = {k: over_core(value[k]) for k in cross}
    far2 = over_dp(far)

    shard_list = [own, twin]
    for k in cross:
        shard_list += [first[k], second[k], value[k], first_twin[k], second_twin[k], value_twin[k]]

    valid_pairs = valid.reshape(rows // PAIR, PAIR)
    part = rows // CHUNKS
    mix_shapes = (shape(*packed_shape(part // 4, width)),) * n_ten
    scratch = [pltpu.VMEM((part, width), BF16)] * 3 + [pltpu.VMEM((4, part // 4, width), BF16)]
    *mixed, w_full = pl.pallas_call(
        functools.partial(first_attention_kernel, n_ctx, width),
        out_shape=mix_shapes + (shape(feat, 3 * width),),
        in_specs=[SMEM] + [VMEM] * (2 + len(shard_list)),
        out_specs=(VMEM,) * (n_ten + 1),
        scratch_shapes=scratch,
        compiler_params=params(16),
        cost_estimate=cost(5),
        name="attention0",
    )(index, hidden, valid_pairs, *shard_list)

    def exchange(pieces):
        return [pieces[0]] + [swap(pieces[s], "tensor", n_ten, s) for s in range(1, n_ten)]

    mixed, far, far2, low = together(mixed, far, far2, low)
    received = [exchange(mixed)]
    high = gather_cross(jnp.stack([far, far2]), n_ctx)
    own_twin = None
    for r in range(1, CHUNKS):
        received[r - 1][1], hidden = together(received[r - 1][1], hidden)
        mixed = pl.pallas_call(
            functools.partial(next_attention_kernel, r * part),
            out_shape=mix_shapes,
            in_specs=[SMEM, VMEM, VMEM, VMEM],
            out_specs=(VMEM,) * n_ten,
            scratch_shapes=scratch,
            compiler_params=params(12),
            cost_estimate=cost(4),
        name="attention" + str(r),
        )(index, hidden, valid_pairs, w_full)
        mixed, received[r - 1], low, w_proj = together(mixed, received[r - 1], low, w_proj)
        received.append(exchange(mixed))
        if own_twin is None:
            own_twin = over_core(jnp.stack([w_proj, by_one, far, far2]))

    blocks = [w_proj, by_one, far, far2, own_twin]
    for k in cross:
        blocks += [low[k], high[k], over_core(low[k]), over_core(high[k])]
    gathered = []
    for r in range(CHUNKS):
        if r > 0:
            received[r], gathered[0][1], place = together(received[r], gathered[0][1], place)
        done = pl.pallas_call(
            functools.partial(project_kernel, n_ctx, r * (part // 4), width, col),
            out_shape=shape(part // 4, feat),
            in_specs=[SMEM] + [VMEM] * (n_ten + len(blocks) + 2),
            out_specs=VMEM,
            scratch_shapes=[pltpu.VMEM((n_ctx, part // 4, col), F32)],
            compiler_params=params(20),
            cost_estimate=cost(2),
        name="project" + str(r),
        )(index, *received[r], *blocks, own_patches, gain_merge)
        gathered.append(gather_xor(done, n_ctx))
    places = gather_cross(place.reshape(1, groups), n_ctx)
    place_twin = over_core(jnp.stack([places[k] for k in (0, *cross)]))
    place_list = []
    for i, k in enumerate((0, *cross)):
        place_list += [places[k], place_twin[i]]
    return pl.pallas_call(
        functools.partial(place_kernel, n_ctx),
        out_shape=shape(groups, feat),
        in_specs=[SMEM] + [VMEM] * (n_ctx + n_ctx * CHUNKS),
        out_specs=VMEM,
        compiler_params=params(28),
        cost_estimate=cost(2),
        name="placement",
    )(index, *place_list, *[gathered[r][k] for k in range(n_ctx) for r in range(CHUNKS)])


def solution(mesh):
    in_specs = (
        P(("dp", "context"), None),
        P(("dp", "context")),
        P(("dp", "context")),
        P(),
        P("context", None, "tensor"),
        P("tensor", "context"),
        P(),
    )
    out_specs = P(("dp", "context"), "tensor")
    sizes = [mesh.shape[name] for name in ("dp", "context", "tensor")]
    body = functools.partial(local, *sizes)
    return jax.shard_map(body, mesh=mesh, in_specs=in_specs, out_specs=out_specs, check_vma=False)
```

```python
import functools

import jax
import jax.numpy as jnp
from jax import lax
from jax.experimental import pallas as pl
from jax.experimental.pallas import tpu as pltpu
from jax.sharding import PartitionSpec as P

HD = 80
WIN = 64
PAIR = 2 * WIN
LANES = 128
CHUNKS = 2
F32 = jnp.float32
BF16 = jnp.bfloat16
VMEM = pl.BlockSpec(memory_space=pltpu.VMEM)
SMEM = pl.BlockSpec(memory_space=pltpu.SMEM)


def params(mib):
    return pltpu.CompilerParams(vmem_limit_bytes=mib * 1024 * 1024)


def swap(x, axis, size, bit):
    return lax.ppermute(x, axis, [(i, i ^ bit) for i in range(size)])


def cross_keys(size):
    return range(2, size, 2)


def gather_cross(x, size):
    blocks = {0: x}
    bit = size // 2
    while bit > 1:
        for key in list(blocks):
            blocks[key ^ bit] = swap(blocks[key], "context", size, bit)
        bit //= 2
    return blocks


def gather_xor(x, size):
    blocks = gather_cross(x, size)
    for key in list(blocks):
        blocks[key ^ 1] = swap(blocks[key], "context", size, 1)
    return blocks


def together(*values):
    return lax.optimization_barrier(values)


def one_hot(mask):
    return mask.astype(F32).astype(BF16)


def shape(*dims):
    return jax.ShapeDtypeStruct(dims, BF16)


def packs(rows, cols):
    return rows % 32 == 0 and cols == 2 * LANES + LANES // 2


def packed_shape(rows, cols):
    return (rows * 5 // 2, LANES) if packs(rows, cols) else (rows, cols)


def pack(x):
    rows, cols = x.shape
    if not packs(rows, cols):
        return x
    rest = x[:, 2 * LANES :]
    tail = jnp.concatenate([rest[: rows // 2], rest[rows // 2 :]], axis=1)
    return jnp.concatenate([x[:, :LANES], x[:, LANES : 2 * LANES], tail], axis=0)


def unpack(p, rows, cols):
    if not packs(rows, cols):
        return p[:, : 2 * LANES], p[:, 2 * LANES :]
    tail = p[2 * rows :]
    rest = jnp.concatenate([tail[:, : LANES // 2], tail[:, LANES // 2 :]], axis=0)
    return jnp.concatenate([p[:rows], p[rows : 2 * rows]], axis=1), rest


def pack_kernel(index_ref, qkv_ref, first_ref, value_ref, all_ref):
    for j in range(3):
        all_ref[j] = pack(qkv_ref[j])
    first_ref[...] = all_ref[index_ref[2]]
    value_ref[...] = all_ref[2]


def pack_proj_kernel(proj_ref, out_ref):
    out_ref[...] = pack(proj_ref[...])


def norm_kernel(index_ref, patches_ref, gain_ref, hidden_ref, own_ref):
    rows = patches_ref.shape[0]
    x = patches_ref[...]
    xf = x.astype(F32)
    mean_sq = jnp.mean(xf * xf, axis=-1, keepdims=True)
    gain = gain_ref[...].reshape(1, -1)
    hidden_ref[...] = (xf * lax.rsqrt(mean_sq + 1e-06) * gain).astype(BF16)
    step = 256
    pick = step // 4
    row = lax.broadcasted_iota(jnp.int32, (pick, step), 0)
    col = lax.broadcasted_iota(jnp.int32, (pick, step), 1)
    chosen = one_hot(col == 4 * row + index_ref[1])
    for i in range(rows // step):
        own_ref[i * pick : (i + 1) * pick, :] = jnp.dot(
            chosen, x[i * step : (i + 1) * step], preferred_element_type=F32
        ).astype(BF16)


def attend(row0, index_ref, hidden_ref, valid_ref, w_ref, out_refs, q_ref, k_ref, v_ref, mix_ref):
    rows, width = q_ref.shape
    heads = width // HD
    main = 2 * LANES
    rest = width - main
    qkv = jnp.dot(hidden_ref[row0 : row0 + rows, :], w_ref[...], preferred_element_type=F32)
    for j, ref in enumerate((q_ref, k_ref, v_ref)):
        ref[:, :main] = qkv[:, j * main : (j + 1) * main].astype(BF16)
        at = 3 * main + j * rest
        ref[:, main:] = qkv[:, at : at + rest].astype(BF16)
    lane = lax.broadcasted_iota(jnp.int32, (1, width), 1)
    head_masks = [one_hot((lane >= h * HD) & (lane < (h + 1) * HD)) for h in range(heads)]
    q_win = lax.broadcasted_iota(jnp.int32, (PAIR, PAIR), 0) // WIN
    k_win = lax.broadcasted_iota(jnp.int32, (PAIR, PAIR), 1) // WIN
    same = q_win == k_win
    floor = jnp.where(same, F32(-1e30), F32(-3e38))
    pick = PAIR // 4
    src = lax.broadcasted_iota(jnp.int32, (PAIR, PAIR), 1)
    dst = lax.broadcasted_iota(jnp.int32, (PAIR, PAIR), 0)
    order = one_hot(src == 4 * (dst % pick) + dst // pick)
    for p in range(rows // PAIR):
        at = p * PAIR
        q = q_ref[at : at + PAIR, :]
        k = k_ref[at : at + PAIR, :]
        v = v_ref[at : at + PAIR, :]
        k_all = jnp.concatenate([k * m for m in head_masks], axis=0)
        v_all = jnp.concatenate([v * m for m in head_masks], axis=0)
        scores = lax.dot_general(q, k_all, (((1,), (1,)), ((), ())), preferred_element_type=F32)
        live = valid_ref[row0 // PAIR + p : row0 // PAIR + p + 1, :] > 0
        weights = []
        for h in range(heads):
            s = scores[:, h * PAIR : (h + 1) * PAIR] * F32(HD ** (-0.5))
            s = jnp.where(same & live, s, floor)
            e = jnp.exp(s - jnp.max(s, axis=-1, keepdims=True))
            weights.append((e / jnp.sum(e, axis=-1, keepdims=True)).astype(BF16))
        w_all = jnp.concatenate(weights, axis=1)
        mixed = jnp.dot(w_all, v_all, preferred_element_type=F32).astype(BF16)
        mixed = jnp.dot(order, mixed, preferred_element_type=F32).astype(BF16)
        for t in range(4):
            mix_ref[t, p * pick : (p + 1) * pick, :] = mixed[t * pick : (t + 1) * pick]
    for s, out_ref in enumerate(out_refs):
        out_ref[...] = pack(mix_ref[index_ref[1] ^ s])


def first_attention_kernel(n_ctx, width, index_ref, hidden_ref, valid_ref, *refs):
    shards = list(refs[: 2 + 3 * (n_ctx - 2)])
    *out_refs, w_ref, q_ref, k_ref, v_ref, mix_ref = refs[len(shards) :]
    depth = w_ref.shape[0] // n_ctx
    me = index_ref[0]
    flip = index_ref[2] > 0
    main = 2 * LANES
    for key in range(n_ctx):
        rows = pl.ds(pl.multiple_of((me ^ key) * depth, depth), depth)
        if key < 2:
            block = shards.pop(0)
            thirds = [block[j] for j in range(3)]
        else:
            first, second, value = [shards.pop(0)[...] for _ in range(3)]
            thirds = [jnp.where(flip, second, first), jnp.where(flip, first, second), value]
        tails = []
        for j, third in enumerate(thirds):
            w_ref[rows, j * main : (j + 1) * main], tail = unpack(third, depth, width)
            tails.append(tail)
        w_ref[rows, 3 * main :] = jnp.concatenate(tails, axis=1)
    attend(0, index_ref, hidden_ref, valid_ref, w_ref, out_refs, q_ref, k_ref, v_ref, mix_ref)


def next_attention_kernel(row0, index_ref, hidden_ref, valid_ref, w_ref, *refs):
    *out_refs, q_ref, k_ref, v_ref, mix_ref = refs
    attend(row0, index_ref, hidden_ref, valid_ref, w_ref, out_refs, q_ref, k_ref, v_ref, mix_ref)


def project_kernel(n_ctx, row0, width, col, index_ref, *refs):
    mixes = [unpack(m[...], refs[-2].shape[0], width) for m in refs[:4]]
    flip = index_ref[2] > 0
    mixes[2:] = [
        [jnp.where(flip, b, a) for a, b in zip(mixes[2], mixes[3])],
        [jnp.where(flip, a, b) for a, b in zip(mixes[2], mixes[3])],
    ]
    *blocks, own_ref, gain_ref, out_ref, part_ref = refs[4:]
    rows = out_ref.shape[0]
    me = index_ref[0]
    main = 2 * LANES
    mixed = jnp.concatenate([m for m, _ in mixes] + [r for _, r in mixes], axis=1)
    mains = []
    rests = []
    for key in range(n_ctx):
        pieces = []
        for ref in [blocks.pop(0) for _ in range((4, 1)[key] if key < 2 else 2)]:
            pieces += [ref[...]] if len(ref.shape) == 2 else [ref[i] for i in range(ref.shape[0])]
        halves = [unpack(p, width, col) for p in pieces]
        both = []
        for half in ([h[0] for h in halves], [h[1] for h in halves]):
            both.append(jnp.concatenate([h[:main] for h in half] + [h[main:] for h in half], axis=0))
        mains.append(jnp.dot(mixed, both[0], preferred_element_type=F32))
        rests.append(both[1])
    if rests[0].shape[1]:
        rest = jnp.dot(mixed, jnp.concatenate(rests, axis=1), preferred_element_type=F32)
        count = rests[0].shape[1]
        mains = [
            jnp.concatenate([m, rest[:, key * count : (key + 1) * count]], axis=1)
            for key, m in enumerate(mains)
        ]
    for key in range(n_ctx):
        part_ref[me ^ key] = mains[key]
    total = jnp.concatenate([part_ref[i] for i in range(n_ctx)], axis=1)
    total = total + own_ref[row0 : row0 + rows, :].astype(F32)
    mean_sq = jnp.mean(total * total, axis=-1, keepdims=True)
    out_ref[...] = (total * lax.rsqrt(mean_sq + 1e-06) * gain_ref[...].reshape(1, -1)).astype(BF16)


def place_kernel(n_ctx, index_ref, *refs):
    place_refs = refs[:n_ctx]
    row_refs = refs[n_ctx:-1]
    out_ref = refs[-1]
    spots = out_ref.shape[0]
    chosen = []
    for place_ref in place_refs:
        target = place_ref[...] - index_ref[0] * spots
        grid = lax.broadcasted_iota(jnp.int32, (spots, target.shape[1]), 0)
        chosen.append(one_hot(grid == target))
    out_ref[...] = jnp.dot(
        jnp.concatenate(chosen, axis=1),
        jnp.concatenate([ref[...] for ref in row_refs], axis=0),
        preferred_element_type=F32,
    ).astype(BF16)


def local(n_dp, n_ctx, n_ten, patches, valid, place, gain_attn, w_qkv, w_proj, gain_merge):
    rows, feat = patches.shape
    depth, _, width = w_qkv.shape
    col = w_proj.shape[1]
    groups = rows // 4
    ten = lax.axis_index("tensor")
    half = lax.axis_index("dp") % 2
    index = jnp.stack([lax.axis_index("context"), ten, half]).astype(jnp.int32)
    cross = list(cross_keys(n_ctx))

    def over_dp(x):
        return swap(x, "dp", n_dp, 1)

    def over_core(x):
        return swap(x, "context", n_ctx, 1)

    third = packed_shape(depth, width)
    piece = packed_shape(width, col)
    first, value, own = pl.pallas_call(
        pack_kernel,
        out_shape=(shape(*third), shape(*third), shape(3, *third)),
        in_specs=[SMEM, VMEM],
        out_specs=(VMEM,) * 3,
        compiler_params=params(8),
        name="pack",
    )(index, jnp.transpose(w_qkv, (1, 0, 2)))
    w_proj = pl.pallas_call(
        pack_proj_kernel,
        out_shape=shape(*piece),
        in_specs=[VMEM],
        out_specs=VMEM,
        compiler_params=params(8),
        name="pack_proj",
    )(w_proj)
    first = gather_cross(first, n_ctx)
    value = gather_cross(value, n_ctx)
    twin = over_core(own)
    far = lax.ppermute(
        w_proj,
        ("dp", "tensor"),
        [
            (d * n_ten + t, d * n_ten + (t ^ (2 + d % 2)))
            for d in range(n_dp)
            for t in range(n_ten)
        ],
    )
    by_one = swap(w_proj, "tensor", n_ten, 1)
    first, twin, patches = together(first, twin, patches)

    second = {k: over_dp(first[k]) for k in cross}
    first_twin = {k: over_core(first[k]) for k in cross}
    hidden, own_patches = pl.pallas_call(
        norm_kernel,
        out_shape=(shape(rows, feat), shape(groups, feat)),
        in_specs=[SMEM, VMEM, VMEM],
        out_specs=(VMEM, VMEM),
        compiler_params=params(16),
        name="norm",
    )(index, patches, gain_attn)
    low = gather_cross(jnp.stack([w_proj, by_one]), n_ctx)
    second, value, first_twin, hidden = together(second, value, first_twin, hidden)

    second_twin = {k: over_core(second[k]) for k in cross}
    value_twin = {k: over_core(value[k]) for k in cross}
    far2 = over_dp(far)

    shard_list = [own, twin]
    for k in cross:
        shard_list += [first[k], second[k], value[k], first_twin[k], second_twin[k], value_twin[k]]

    valid_pairs = valid.reshape(rows // PAIR, PAIR)
    part = rows // CHUNKS
    mix_shapes = (shape(*packed_shape(part // 4, width)),) * n_ten
    scratch = [pltpu.VMEM((part, width), BF16)] * 3 + [pltpu.VMEM((4, part // 4, width), BF16)]
    *mixed, w_full = pl.pallas_call(
        functools.partial(first_attention_kernel, n_ctx, width),
        out_shape=mix_shapes + (shape(feat, 3 * width),),
        in_specs=[SMEM] + [VMEM] * (2 + len(shard_list)),
        out_specs=(VMEM,) * (n_ten + 1),
        scratch_shapes=scratch,
        compiler_params=params(16),
        name="attention0",
    )(index, hidden, valid_pairs, *shard_list)

    def exchange(pieces):
        return [pieces[0]] + [swap(pieces[s], "tensor", n_ten, s) for s in range(1, n_ten)]

    mixed, far, far2, low = together(mixed, far, far2, low)
    received = [exchange(mixed)]
    high = gather_cross(jnp.stack([far, far2]), n_ctx)
    own_twin = None
    for r in range(1, CHUNKS):
        received[r - 1][1], hidden = together(received[r - 1][1], hidden)
        mixed = pl.pallas_call(
            functools.partial(next_attention_kernel, r * part),
            out_shape=mix_shapes,
            in_specs=[SMEM, VMEM, VMEM, VMEM],
            out_specs=(VMEM,) * n_ten,
            scratch_shapes=scratch,
            compiler_params=params(12),
            name="attention" + str(r),
        )(index, hidden, valid_pairs, w_full)
        mixed, received[r - 1], low, w_proj = together(mixed, received[r - 1], low, w_proj)
        received.append(exchange(mixed))
        if own_twin is None:
            own_twin = over_core(jnp.stack([w_proj, by_one, far, far2]))

    high, received[-1][1] = together(high, received[-1][1])

    blocks = [w_proj, by_one, far, far2, own_twin]
    for k in cross:
        blocks += [low[k], high[k], over_core(low[k]), over_core(high[k])]
    gathered = []
    for r in range(CHUNKS):
        if r > 0:
            received[r], done = together(received[r], done)
        done = pl.pallas_call(
            functools.partial(project_kernel, n_ctx, r * (part // 4), width, col),
            out_shape=shape(part // 4, feat),
            in_specs=[SMEM] + [VMEM] * (n_ten + len(blocks) + 2),
            out_specs=VMEM,
            scratch_shapes=[pltpu.VMEM((n_ctx, part // 4, col), F32)],
            compiler_params=params(20),
            name="project" + str(r),
        )(index, *received[r], *blocks, own_patches, gain_merge)
        crossed = gather_cross(done, n_ctx)
        if r > 0:
            for k in cross:
                crossed[k], gathered[r - 1][k ^ 1] = together(crossed[k], gathered[r - 1][k ^ 1])
        for k in list(crossed):
            crossed[k ^ 1] = over_core(crossed[k])
        gathered.append(crossed)
    places = gather_cross(place.reshape(1, groups), n_ctx)
    place_twin = over_core(jnp.stack([places[k] for k in (0, *cross)]))
    place_list = []
    for i, k in enumerate((0, *cross)):
        place_list += [places[k], place_twin[i]]
    return pl.pallas_call(
        functools.partial(place_kernel, n_ctx),
        out_shape=shape(groups, feat),
        in_specs=[SMEM] + [VMEM] * (n_ctx + n_ctx * CHUNKS),
        out_specs=VMEM,
        compiler_params=params(28),
        name="placement",
    )(index, *place_list, *[gathered[r][k] for k in range(n_ctx) for r in range(CHUNKS)])


def solution(mesh):
    in_specs = (
        P(("dp", "context"), None),
        P(("dp", "context")),
        P(("dp", "context")),
        P(),
        P("context", None, "tensor"),
        P("tensor", "context"),
        P(),
    )
    out_specs = P(("dp", "context"), "tensor")
    sizes = [mesh.shape[name] for name in ("dp", "context", "tensor")]
    body = functools.partial(local, *sizes)
    return jax.shard_map(body, mesh=mesh, in_specs=in_specs, out_specs=out_specs, check_vma=False)
```

```python
import functools

import jax
import jax.numpy as jnp
from jax import lax
from jax.experimental import pallas as pl
from jax.experimental.pallas import tpu as pltpu
from jax.sharding import PartitionSpec as P

HD = 80
WIN = 64
PAIR = 2 * WIN
LANES = 128
HALVES = 2
F32 = jnp.float32
BF16 = jnp.bfloat16
VMEM = pl.BlockSpec(memory_space=pltpu.VMEM)
SMEM = pl.BlockSpec(memory_space=pltpu.SMEM)


def params(mib):
    return pltpu.CompilerParams(vmem_limit_bytes=mib * 1024 * 1024)


def swap(x, axis, size, bit):
    return lax.ppermute(x, axis, [(i, i ^ bit) for i in range(size)])


def cross_keys(size):
    return range(2, size, 2)


def gather_cross(x, size):
    blocks = {0: x}
    bit = size // 2
    while bit > 1:
        for key in list(blocks):
            blocks[key ^ bit] = swap(blocks[key], "context", size, bit)
        bit //= 2
    return blocks


def gather_xor(x, size):
    blocks = gather_cross(x, size)
    for key in list(blocks):
        blocks[key ^ 1] = swap(blocks[key], "context", size, 1)
    return blocks


def together(*values):
    return lax.optimization_barrier(values)


def one_hot(mask):
    return mask.astype(F32).astype(BF16)


def shape(*dims):
    return jax.ShapeDtypeStruct(dims, BF16)


def packs(rows, cols):
    return rows % 32 == 0 and cols == 2 * LANES + LANES // 2


def packed_shape(rows, cols):
    return (rows * 5 // 2, LANES) if packs(rows, cols) else (rows, cols)


def pack(x):
    rows, cols = x.shape
    if not packs(rows, cols):
        return x
    rest = x[:, 2 * LANES :]
    tail = jnp.concatenate([rest[: rows // 2], rest[rows // 2 :]], axis=1)
    return jnp.concatenate([x[:, :LANES], x[:, LANES : 2 * LANES], tail], axis=0)


def unpack(p, rows, cols):
    if not packs(rows, cols):
        return p[:, : 2 * LANES], p[:, 2 * LANES :]
    tail = p[2 * rows :]
    rest = jnp.concatenate([tail[:, : LANES // 2], tail[:, LANES // 2 :]], axis=0)
    return jnp.concatenate([p[:rows], p[rows : 2 * rows]], axis=1), rest


def pack_kernel(index_ref, qkv_ref, first_ref, value_ref, all_ref):
    for j in range(3):
        all_ref[j] = pack(qkv_ref[j])
    first_ref[...] = all_ref[index_ref[2]]
    value_ref[...] = all_ref[2]


def pack_proj_kernel(proj_ref, out_ref):
    out_ref[...] = pack(proj_ref[...])


def norm_kernel(index_ref, patches_ref, gain_ref, hidden_ref, own_ref):
    rows = patches_ref.shape[0]
    x = patches_ref[...]
    xf = x.astype(F32)
    mean_sq = jnp.mean(xf * xf, axis=-1, keepdims=True)
    gain = gain_ref[...].reshape(1, -1)
    hidden_ref[...] = (xf * lax.rsqrt(mean_sq + 1e-06) * gain).astype(BF16)
    step = 256
    pick = step // 4
    row = lax.broadcasted_iota(jnp.int32, (pick, step), 0)
    col = lax.broadcasted_iota(jnp.int32, (pick, step), 1)
    chosen = one_hot(col == 4 * row + index_ref[1])
    for i in range(rows // step):
        own_ref[i * pick : (i + 1) * pick, :] = jnp.dot(
            chosen, x[i * step : (i + 1) * step], preferred_element_type=F32
        ).astype(BF16)


def attend(index_ref, hidden_ref, valid_ref, w_ref, out_refs, q_ref, k_ref, v_ref, mix_ref):
    rows, width = q_ref.shape
    heads = width // HD
    main = 2 * LANES
    rest = width - main
    qkv = jnp.dot(hidden_ref[...], w_ref[...], preferred_element_type=F32)
    for j, ref in enumerate((q_ref, k_ref, v_ref)):
        ref[:, :main] = qkv[:, j * main : (j + 1) * main].astype(BF16)
        at = 3 * main + j * rest
        ref[:, main:] = qkv[:, at : at + rest].astype(BF16)
    lane = lax.broadcasted_iota(jnp.int32, (1, width), 1)
    head_masks = [one_hot((lane >= h * HD) & (lane < (h + 1) * HD)) for h in range(heads)]
    q_win = lax.broadcasted_iota(jnp.int32, (PAIR, PAIR), 0) // WIN
    k_win = lax.broadcasted_iota(jnp.int32, (PAIR, PAIR), 1) // WIN
    same = q_win == k_win
    floor = jnp.where(same, F32(-1e30), F32(-3e38))
    pick = PAIR // 4
    src = lax.broadcasted_iota(jnp.int32, (PAIR, PAIR), 1)
    dst = lax.broadcasted_iota(jnp.int32, (PAIR, PAIR), 0)
    order = one_hot(src == 4 * (dst % pick) + dst // pick)
    for p in range(rows // PAIR):
        at = p * PAIR
        q = q_ref[at : at + PAIR, :]
        k = k_ref[at : at + PAIR, :]
        v = v_ref[at : at + PAIR, :]
        k_all = jnp.concatenate([k * m for m in head_masks], axis=0)
        v_all = jnp.concatenate([v * m for m in head_masks], axis=0)
        scores = lax.dot_general(q, k_all, (((1,), (1,)), ((), ())), preferred_element_type=F32)
        live = valid_ref[p : p + 1, :] > 0
        weights = []
        for h in range(heads):
            s = scores[:, h * PAIR : (h + 1) * PAIR] * F32(HD ** (-0.5))
            s = jnp.where(same & live, s, floor)
            e = jnp.exp(s - jnp.max(s, axis=-1, keepdims=True))
            weights.append((e / jnp.sum(e, axis=-1, keepdims=True)).astype(BF16))
        w_all = jnp.concatenate(weights, axis=1)
        mixed = jnp.dot(w_all, v_all, preferred_element_type=F32).astype(BF16)
        mixed = jnp.dot(order, mixed, preferred_element_type=F32).astype(BF16)
        for t in range(4):
            mix_ref[t, p * pick : (p + 1) * pick, :] = mixed[t * pick : (t + 1) * pick]
    for s, out_ref in enumerate(out_refs):
        out_ref[...] = pack(mix_ref[index_ref[1] ^ s])


def attention_kernel(n_ctx, width, index_ref, hidden_ref, valid_ref, *refs):
    shards = list(refs[: 2 + 3 * (n_ctx - 2)])
    *out_refs, w_ref, q_ref, k_ref, v_ref, mix_ref = refs[len(shards) :]
    depth = w_ref.shape[0] // n_ctx
    me = index_ref[0]
    flip = index_ref[2] > 0
    main = 2 * LANES
    for key in range(n_ctx):
        rows = pl.ds(pl.multiple_of((me ^ key) * depth, depth), depth)
        if key < 2:
            block = shards.pop(0)
            thirds = [block[j] for j in range(3)]
        else:
            first, second, value = [shards.pop(0)[...] for _ in range(3)]
            thirds = [jnp.where(flip, second, first), jnp.where(flip, first, second), value]
        tails = []
        for j, third in enumerate(thirds):
            w_ref[rows, j * main : (j + 1) * main], tail = unpack(third, depth, width)
            tails.append(tail)
        w_ref[rows, 3 * main :] = jnp.concatenate(tails, axis=1)
    attend(index_ref, hidden_ref, valid_ref, w_ref, out_refs, q_ref, k_ref, v_ref, mix_ref)


def project_kernel(n_ctx, width, col, index_ref, *refs):
    *blocks, own_ref, gain_ref = refs[4 : -HALVES - 1]
    *out_refs, part_ref = refs[-HALVES - 1 :]
    rows = own_ref.shape[0]
    mixes = [unpack(m[...], rows, width) for m in refs[:4]]
    flip = index_ref[2] > 0
    mixes[2:] = [
        [jnp.where(flip, b, a) for a, b in zip(mixes[2], mixes[3])],
        [jnp.where(flip, a, b) for a, b in zip(mixes[2], mixes[3])],
    ]
    me = index_ref[0]
    main = 2 * LANES
    mixed = jnp.concatenate([m for m, _ in mixes] + [r for _, r in mixes], axis=1)
    mains = []
    rests = []
    for key in range(n_ctx):
        pieces = []
        for ref in [blocks.pop(0) for _ in range((4, 1)[key] if key < 2 else 2)]:
            pieces += [ref[...]] if len(ref.shape) == 2 else [ref[i] for i in range(ref.shape[0])]
        halves = [unpack(p, width, col) for p in pieces]
        both = []
        for half in ([h[0] for h in halves], [h[1] for h in halves]):
            both.append(jnp.concatenate([h[:main] for h in half] + [h[main:] for h in half], axis=0))
        mains.append(jnp.dot(mixed, both[0], preferred_element_type=F32))
        rests.append(both[1])
    if rests[0].shape[1]:
        rest = jnp.dot(mixed, jnp.concatenate(rests, axis=1), preferred_element_type=F32)
        count = rests[0].shape[1]
        mains = [
            jnp.concatenate([m, rest[:, key * count : (key + 1) * count]], axis=1)
            for key, m in enumerate(mains)
        ]
    for key in range(n_ctx):
        part_ref[me ^ key] = mains[key]
    total = jnp.concatenate([part_ref[i] for i in range(n_ctx)], axis=1)
    total = total + own_ref[...].astype(F32)
    mean_sq = jnp.mean(total * total, axis=-1, keepdims=True)
    normed = (total * lax.rsqrt(mean_sq + 1e-06) * gain_ref[...].reshape(1, -1)).astype(BF16)
    count = rows // HALVES
    for i, out_ref in enumerate(out_refs):
        out_ref[...] = normed[i * count : (i + 1) * count]


def place_kernel(n_ctx, index_ref, *refs):
    place_refs = refs[:n_ctx]
    row_refs = refs[n_ctx:-1]
    out_ref = refs[-1]
    spots = out_ref.shape[0]
    chosen = []
    for place_ref in place_refs:
        target = place_ref[...] - index_ref[0] * spots
        grid = lax.broadcasted_iota(jnp.int32, (spots, target.shape[1]), 0)
        chosen.append(one_hot(grid == target))
    out_ref[...] = jnp.dot(
        jnp.concatenate(chosen, axis=1),
        jnp.concatenate([ref[...] for ref in row_refs], axis=0),
        preferred_element_type=F32,
    ).astype(BF16)


def local(n_dp, n_ctx, n_ten, patches, valid, place, gain_attn, w_qkv, w_proj, gain_merge):
    rows, feat = patches.shape
    depth, _, width = w_qkv.shape
    col = w_proj.shape[1]
    groups = rows // 4
    ten = lax.axis_index("tensor")
    half = lax.axis_index("dp") % 2
    index = jnp.stack([lax.axis_index("context"), ten, half]).astype(jnp.int32)
    cross = list(cross_keys(n_ctx))

    def over_dp(x):
        return swap(x, "dp", n_dp, 1)

    def over_core(x):
        return swap(x, "context", n_ctx, 1)

    third = packed_shape(depth, width)
    piece = packed_shape(width, col)
    first, value, own = pl.pallas_call(
        pack_kernel,
        out_shape=(shape(*third), shape(*third), shape(3, *third)),
        in_specs=[SMEM, VMEM],
        out_specs=(VMEM,) * 3,
        compiler_params=params(8),
        name="pack",
    )(index, jnp.transpose(w_qkv, (1, 0, 2)))
    w_proj = pl.pallas_call(
        pack_proj_kernel,
        out_shape=shape(*piece),
        in_specs=[VMEM],
        out_specs=VMEM,
        compiler_params=params(8),
        name="pack_proj",
    )(w_proj)
    first = gather_cross(first, n_ctx)
    value = gather_cross(value, n_ctx)
    twin = over_core(own)
    far = lax.ppermute(
        w_proj,
        ("dp", "tensor"),
        [
            (d * n_ten + t, d * n_ten + (t ^ (2 + d % 2)))
            for d in range(n_dp)
            for t in range(n_ten)
        ],
    )
    by_one = swap(w_proj, "tensor", n_ten, 1)
    first, twin, patches = together(first, twin, patches)

    second = {k: over_dp(first[k]) for k in cross}
    first_twin = {k: over_core(first[k]) for k in cross}
    hidden, own_patches = pl.pallas_call(
        norm_kernel,
        out_shape=(shape(rows, feat), shape(groups, feat)),
        in_specs=[SMEM, VMEM, VMEM],
        out_specs=(VMEM, VMEM),
        compiler_params=params(16),
        name="norm",
    )(index, patches, gain_attn)
    by_one, hidden = together(by_one, hidden)
    low = gather_cross(jnp.stack([w_proj, by_one]), n_ctx)
    second, value, first_twin, hidden = together(second, value, first_twin, hidden)

    second_twin = {k: over_core(second[k]) for k in cross}
    value_twin = {k: over_core(value[k]) for k in cross}
    far, *_ = together(far, *second.values())
    far2 = over_dp(far)

    shard_list = [own, twin]
    for k in cross:
        shard_list += [first[k], second[k], value[k], first_twin[k], second_twin[k], value_twin[k]]

    mix_shapes = (shape(*packed_shape(groups, width)),) * n_ten
    mixed = pl.pallas_call(
        functools.partial(attention_kernel, n_ctx, width),
        out_shape=mix_shapes,
        in_specs=[SMEM] + [VMEM] * (2 + len(shard_list)),
        out_specs=(VMEM,) * n_ten,
        scratch_shapes=[pltpu.VMEM((feat, 3 * width), BF16)]
        + [pltpu.VMEM((rows, width), BF16)] * 3
        + [pltpu.VMEM((4, groups, width), BF16)],
        compiler_params=params(20),
        name="attention",
    )(index, hidden, valid.reshape(rows // PAIR, PAIR), *shard_list)

    mixed, far, far2, low = together(mixed, far, far2, low)
    mixed = [mixed[0]] + [swap(mixed[s], "tensor", n_ten, s) for s in range(1, n_ten)]
    high = gather_cross(jnp.stack([far, far2]), n_ctx)
    blocks = [w_proj, by_one, far, far2, over_core(jnp.stack([w_proj, by_one, far, far2]))]
    low_twin = {k: over_core(low[k]) for k in cross}
    mixed, high = together(mixed, high)
    for k in cross:
        blocks += [low[k], high[k], low_twin[k], over_core(high[k])]
    done = pl.pallas_call(
        functools.partial(project_kernel, n_ctx, width, col),
        out_shape=(shape(groups // HALVES, feat),) * HALVES,
        in_specs=[SMEM] + [VMEM] * (n_ten + len(blocks) + 2),
        out_specs=(VMEM,) * HALVES,
        scratch_shapes=[pltpu.VMEM((n_ctx, groups, col), F32)],
        compiler_params=params(24),
        name="project",
    )(index, *mixed, *blocks, own_patches, gain_merge)

    gathered = []
    for r in range(HALVES):
        crossed = gather_cross(done[r], n_ctx)
        if r == 0:
            place, crossed[0] = together(place, crossed[0])
            places = gather_cross(place.reshape(1, groups), n_ctx)
            place_twin = over_core(jnp.stack([places[k] for k in (0, *cross)]))
        else:
            for k in cross:
                crossed[k], gathered[r - 1][k ^ 1], place_twin = together(
                    crossed[k], gathered[r - 1][k ^ 1], place_twin
                )
        for k in list(crossed):
            crossed[k ^ 1] = over_core(crossed[k])
        gathered.append(crossed)
    place_list = []
    for i, k in enumerate((0, *cross)):
        place_list += [places[k], place_twin[i]]
    return pl.pallas_call(
        functools.partial(place_kernel, n_ctx),
        out_shape=shape(groups, feat),
        in_specs=[SMEM] + [VMEM] * (n_ctx + n_ctx * HALVES),
        out_specs=VMEM,
        compiler_params=params(28),
        name="placement",
    )(index, *place_list, *[gathered[r][k] for k in range(n_ctx) for r in range(HALVES)])


def solution(mesh):
    in_specs = (
        P(("dp", "context"), None),
        P(("dp", "context")),
        P(("dp", "context")),
        P(),
        P("context", None, "tensor"),
        P("tensor", "context"),
        P(),
    )
    out_specs = P(("dp", "context"), "tensor")
    sizes = [mesh.shape[name] for name in ("dp", "context", "tensor")]
    body = functools.partial(local, *sizes)
    return jax.shard_map(body, mesh=mesh, in_specs=in_specs, out_specs=out_specs, check_vma=False)
```

```python
import functools
import math

import jax
import jax.numpy as jnp
from jax import lax
from jax.experimental import pallas as pl
from jax.experimental.pallas import tpu as pltpu
from jax.sharding import PartitionSpec as P

HD = 80
WIN = 64
PAIR = 2 * WIN
LANES = 128
HALVES = 2
F32 = jnp.float32
BF16 = jnp.bfloat16
VMEM = pl.BlockSpec(memory_space=pltpu.VMEM)
SMEM = pl.BlockSpec(memory_space=pltpu.SMEM)


def params(mib):
    return pltpu.CompilerParams(vmem_limit_bytes=mib * 1024 * 1024)


def swap(x, axis, size, bit):
    return lax.ppermute(x, axis, [(i, i ^ bit) for i in range(size)])


def cross_keys(size):
    return range(2, size, 2)


def gather_cross(x, size):
    blocks = {0: x}
    bit = size // 2
    while bit > 1:
        for key in list(blocks):
            blocks[key ^ bit] = swap(blocks[key], "context", size, bit)
        bit //= 2
    return blocks


def gather_xor(x, size):
    blocks = gather_cross(x, size)
    for key in list(blocks):
        blocks[key ^ 1] = swap(blocks[key], "context", size, 1)
    return blocks


def together(*values):
    return lax.optimization_barrier(values)


def one_hot(mask):
    return mask.astype(F32).astype(BF16)


def shape(*dims):
    return jax.ShapeDtypeStruct(dims, BF16)


def packs(rows, cols):
    return rows % 32 == 0 and cols == 2 * LANES + LANES // 2


def packed_shape(rows, cols):
    return (rows * 5 // 2, LANES) if packs(rows, cols) else (rows, cols)


def pack(x):
    rows, cols = x.shape
    if not packs(rows, cols):
        return x
    rest = x[:, 2 * LANES :]
    tail = jnp.concatenate([rest[: rows // 2], rest[rows // 2 :]], axis=1)
    return jnp.concatenate([x[:, :LANES], x[:, LANES : 2 * LANES], tail], axis=0)


def unpack(p, rows, cols):
    if not packs(rows, cols):
        return p[:, : 2 * LANES], p[:, 2 * LANES :]
    tail = p[2 * rows :]
    rest = jnp.concatenate([tail[:, : LANES // 2], tail[:, LANES // 2 :]], axis=0)
    return jnp.concatenate([p[:rows], p[rows : 2 * rows]], axis=1), rest


def pack_kernel(qkv_ref, all_ref, *third_refs):
    for j, ref in enumerate(third_refs):
        all_ref[j] = pack(qkv_ref[j])
        ref[...] = all_ref[j]


def pack_proj_kernel(proj_ref, all_ref, low_ref, high_ref):
    half = low_ref.shape[0]
    for t in range(2 * half):
        all_ref[t] = pack(proj_ref[t])
    low_ref[...] = all_ref[:half]
    high_ref[...] = all_ref[half:]


def norm_kernel(index_ref, patches_ref, gain_ref, hidden_ref, own_ref):
    rows = patches_ref.shape[0]
    x = patches_ref[...]
    xf = x.astype(F32)
    mean_sq = jnp.mean(xf * xf, axis=-1, keepdims=True)
    gain = gain_ref[...].reshape(1, -1)
    hidden_ref[...] = (xf * lax.rsqrt(mean_sq + 1e-06) * gain).astype(BF16)
    step = 256
    pick = step // 4
    row = lax.broadcasted_iota(jnp.int32, (pick, step), 0)
    col = lax.broadcasted_iota(jnp.int32, (pick, step), 1)
    chosen = one_hot(col == 4 * row + index_ref[1])
    for i in range(rows // step):
        own_ref[i * pick : (i + 1) * pick, :] = jnp.dot(
            chosen, x[i * step : (i + 1) * step], preferred_element_type=F32
        ).astype(BF16)


def load_weights(me, depth, width, count, blocks, w_ref):
    main = 2 * LANES
    for key, thirds in enumerate(blocks):
        rows = pl.ds(pl.multiple_of((me ^ key) * depth, depth), depth)
        tails = []
        for j, third in enumerate(thirds):
            w_ref[rows, j * main : (j + 1) * main], tail = unpack(third, depth, width)
            tails.append(tail)
        w_ref[rows, count * main :] = tails[0] if count == 1 else jnp.concatenate(tails, axis=1)


def score_kernel(n_ctx, width, index_ref, hidden_ref, valid_ref, *refs):
    own_ref, twin_ref = refs[:2]
    others = refs[2 : 2 + 2 * (n_ctx - 2)]
    out_ref, w_ref, q_ref, k_ref = refs[2 + len(others) :]
    rows, feat = hidden_ref.shape
    heads = width // HD
    main = 2 * LANES
    rest = width - main
    blocks = [[own_ref[0], own_ref[1]], [twin_ref[0], twin_ref[1]]]
    for key in range(2, n_ctx):
        blocks.append([others[2 * key - 4][...], others[2 * key - 3][...]])
    load_weights(index_ref[0], feat // n_ctx, width, 2, blocks, w_ref)
    qk = jnp.dot(hidden_ref[...], w_ref[...], preferred_element_type=F32)
    for j, ref in enumerate((q_ref, k_ref)):
        ref[:, :main] = qk[:, j * main : (j + 1) * main].astype(BF16)
        at = 2 * main + j * rest
        ref[:, main:] = qk[:, at : at + rest].astype(BF16)
    q_win = lax.broadcasted_iota(jnp.int32, (PAIR, PAIR), 0) // WIN
    k_win = lax.broadcasted_iota(jnp.int32, (PAIR, PAIR), 1) // WIN
    same = q_win == k_win
    floor = jnp.where(same, F32(-1e30), F32(-3e38))
    zero = jnp.zeros((HD, PAIR), BF16)
    factor = F32(HD ** (-0.5) * math.log2(math.e))
    for p in range(rows // PAIR):
        at = p * PAIR
        turned = k_ref[at : at + PAIR, :].T
        k_all = jnp.concatenate(
            [
                jnp.concatenate(
                    [turned[h * HD : (h + 1) * HD] if i == h else zero for i in range(heads)], axis=1
                )
                for h in range(heads)
            ],
            axis=0,
        )
        scores = jnp.dot(q_ref[at : at + PAIR, :], k_all, preferred_element_type=F32)
        seen = same & (valid_ref[p : p + 1, :] > 0)
        for h in range(heads):
            s = jnp.where(seen, scores[:, h * PAIR : (h + 1) * PAIR], floor)
            e = jnp.exp2((s - jnp.max(s, axis=-1, keepdims=True)) * factor)
            out_ref[at : at + PAIR, h * PAIR : (h + 1) * PAIR] = e.astype(BF16)


def mix_kernel(n_ctx, width, index_ref, hidden_ref, exps_ref, *refs):
    own_ref, twin_ref = refs[:2]
    others = refs[2:n_ctx]
    *out_refs, w_ref, v_ref, mix_ref = refs[n_ctx:]
    rows, feat = hidden_ref.shape
    heads = width // HD
    blocks = [[own_ref[2]], [twin_ref[2]]] + [[ref[...]] for ref in others]
    load_weights(index_ref[0], feat // n_ctx, width, 1, blocks, w_ref)
    v_ref[...] = jnp.dot(hidden_ref[...], w_ref[...], preferred_element_type=F32).astype(BF16)
    lane = lax.broadcasted_iota(jnp.int32, (1, width), 1)
    head_masks = [one_hot((lane >= h * HD) & (lane < (h + 1) * HD)) for h in range(heads)]
    ones = jnp.concatenate([jnp.broadcast_to(m, (PAIR, width)) for m in head_masks], axis=0)
    pick = PAIR // 4
    src = lax.broadcasted_iota(jnp.int32, (PAIR, PAIR), 1)
    dst = lax.broadcasted_iota(jnp.int32, (PAIR, PAIR), 0)
    order = one_hot(src == 4 * (dst % pick) + dst // pick)
    for p in range(rows // PAIR):
        at = p * PAIR
        exps = exps_ref[at : at + PAIR, :]
        v = v_ref[at : at + PAIR, :]
        v_all = jnp.concatenate([v * m for m in head_masks], axis=0)
        mixed = jnp.dot(exps, v_all, preferred_element_type=F32)
        total = jnp.dot(exps, ones, preferred_element_type=F32)
        mixed = (mixed / total).astype(BF16)
        mixed = jnp.dot(order, mixed, preferred_element_type=F32).astype(BF16)
        for t in range(4):
            mix_ref[t, p * pick : (p + 1) * pick, :] = mixed[t * pick : (t + 1) * pick]
    for s, out_ref in enumerate(out_refs):
        out_ref[...] = pack(mix_ref[index_ref[1] ^ s])


def project_kernel(n_ctx, width, col, index_ref, *refs):
    *blocks, own_ref, gain_ref = refs[4 : -HALVES - 2]
    *out_refs, part_ref, mix_ref = refs[-HALVES - 2 :]
    rows = own_ref.shape[0]
    for s in range(4):
        mix_ref[index_ref[1] ^ s] = refs[s][...]
    mixes = [unpack(mix_ref[t], rows, width) for t in range(4)]
    me = index_ref[0]
    main = 2 * LANES
    mixed = jnp.concatenate([m for m, _ in mixes] + [r for _, r in mixes], axis=1)
    mains = []
    rests = []
    for key in range(n_ctx):
        pieces = []
        for ref in [blocks.pop(0) for _ in range(1 if key < 2 else 2)]:
            pieces += [ref[i] for i in range(ref.shape[0])]
        halves = [unpack(p, width, col) for p in pieces]
        both = []
        for half in ([h[0] for h in halves], [h[1] for h in halves]):
            both.append(jnp.concatenate([h[:main] for h in half] + [h[main:] for h in half], axis=0))
        mains.append(jnp.dot(mixed, both[0], preferred_element_type=F32))
        rests.append(both[1])
    if rests[0].shape[1]:
        rest = jnp.dot(mixed, jnp.concatenate(rests, axis=1), preferred_element_type=F32)
        count = rests[0].shape[1]
        mains = [
            jnp.concatenate([m, rest[:, key * count : (key + 1) * count]], axis=1)
            for key, m in enumerate(mains)
        ]
    for key in range(n_ctx):
        part_ref[me ^ key] = mains[key]
    total = jnp.concatenate([part_ref[i] for i in range(n_ctx)], axis=1)
    total = total + own_ref[...].astype(F32)
    mean_sq = jnp.mean(total * total, axis=-1, keepdims=True)
    normed = (total * lax.rsqrt(mean_sq + 1e-06) * gain_ref[...].reshape(1, -1)).astype(BF16)
    count = rows // HALVES
    for i, out_ref in enumerate(out_refs):
        out_ref[...] = normed[i * count : (i + 1) * count]


def place_kernel(n_ctx, index_ref, *refs):
    place_refs = refs[:n_ctx]
    row_refs = refs[n_ctx:-1]
    out_ref = refs[-1]
    spots = out_ref.shape[0]
    chosen = []
    for place_ref in place_refs:
        target = place_ref[...] - index_ref[0] * spots
        grid = lax.broadcasted_iota(jnp.int32, (spots, target.shape[1]), 0)
        chosen.append(one_hot(grid == target))
    out_ref[...] = jnp.dot(
        jnp.concatenate(chosen, axis=1),
        jnp.concatenate([ref[...] for ref in row_refs], axis=0),
        preferred_element_type=F32,
    ).astype(BF16)


def local(n_dp, n_ctx, n_ten, patches, valid, place, gain_attn, w_qkv, w_proj, gain_merge):
    rows, feat = patches.shape
    depth, _, width = w_qkv.shape
    col = w_proj.shape[1]
    groups = rows // 4
    ten = lax.axis_index("tensor")
    half = lax.axis_index("dp") % 2
    index = jnp.stack([lax.axis_index("context"), ten, half]).astype(jnp.int32)
    cross = list(cross_keys(n_ctx))

    def over_dp(x):
        return swap(x, "dp", n_dp, 1)

    def over_core(x):
        return swap(x, "context", n_ctx, 1)

    third = packed_shape(depth, width)
    piece = packed_shape(width, col)
    own, *thirds = pl.pallas_call(
        pack_kernel,
        out_shape=(shape(3, *third),) + (shape(*third),) * 3,
        in_specs=[VMEM],
        out_specs=(VMEM,) * 4,
        compiler_params=params(8),
        name="pack",
    )(jnp.transpose(w_qkv, (1, 0, 2)))
    proj = lax.all_gather(w_proj, "tensor")
    query = gather_cross(thirds[0], n_ctx)
    key = gather_cross(thirds[1], n_ctx)
    value = gather_cross(thirds[2], n_ctx)
    query, patches = together(query, patches)
    query_twin = {k: over_core(query[k]) for k in cross}
    hidden, own_patches = pl.pallas_call(
        norm_kernel,
        out_shape=(shape(rows, feat), shape(groups, feat)),
        in_specs=[SMEM, VMEM, VMEM],
        out_specs=(VMEM, VMEM),
        compiler_params=params(16),
        name="norm",
    )(index, patches, gain_attn)
    key, hidden = together(key, hidden)
    twin = over_core(own)
    key_twin = {k: over_core(key[k]) for k in cross}

    shard_list = [own, twin]
    for k in cross:
        shard_list += [query[k], key[k], query_twin[k], key_twin[k]]
    exps = pl.pallas_call(
        functools.partial(score_kernel, n_ctx, width),
        out_shape=shape(rows, width // HD * PAIR),
        in_specs=[SMEM] + [VMEM] * (2 + len(shard_list)),
        out_specs=VMEM,
        scratch_shapes=[pltpu.VMEM((feat, 2 * width), BF16)] + [pltpu.VMEM((rows, width), BF16)] * 2,
        compiler_params=params(20),
        name="scores",
    )(index, hidden, valid.reshape(rows // PAIR, PAIR), *shard_list)
    exps, value, proj = together(exps, value, proj)
    value_twin = {k: over_core(value[k]) for k in cross}
    proj, proj_low, proj_high = pl.pallas_call(
        pack_proj_kernel,
        out_shape=(shape(n_ten, *piece), shape(n_ten // 2, *piece), shape(n_ten // 2, *piece)),
        in_specs=[VMEM],
        out_specs=(VMEM,) * 3,
        compiler_params=params(12),
        name="pack_proj",
    )(proj)
    low = gather_cross(proj_low, n_ctx)
    high = gather_cross(proj_high, n_ctx)
    value_list = []
    for k in cross:
        value_list += [value[k], value_twin[k]]
    mixed = pl.pallas_call(
        functools.partial(mix_kernel, n_ctx, width),
        out_shape=(shape(*packed_shape(groups, width)),) * n_ten,
        in_specs=[SMEM] + [VMEM] * (2 + n_ctx),
        out_specs=(VMEM,) * n_ten,
        scratch_shapes=[
            pltpu.VMEM((feat, width), BF16),
            pltpu.VMEM((rows, width), BF16),
            pltpu.VMEM((4, groups, width), BF16),
        ],
        compiler_params=params(16),
        name="mix",
    )(index, hidden, exps, own, twin, *value_list)

    received = {s: swap(mixed[s], "tensor", n_ten, s) for s in (2, 3, 1)}
    mixed = [mixed[0]] + [received[s] for s in range(1, n_ten)]
    proj_twin = over_core(proj)
    mixed, low, high = together(mixed, low, high)
    blocks = [proj, proj_twin]
    for k in cross:
        blocks += [low[k], high[k], over_core(low[k]), over_core(high[k])]
    done = pl.pallas_call(
        functools.partial(project_kernel, n_ctx, width, col),
        out_shape=(shape(groups // HALVES, feat),) * HALVES,
        in_specs=[SMEM] + [VMEM] * (n_ten + len(blocks) + 2),
        out_specs=(VMEM,) * HALVES,
        scratch_shapes=[
            pltpu.VMEM((n_ctx, groups, col), F32),
            pltpu.VMEM((n_ten, *packed_shape(groups, width)), BF16),
        ],
        compiler_params=params(24),
        name="project",
    )(index, *mixed, *blocks, own_patches, gain_merge)

    gathered = []
    for r in range(HALVES):
        crossed = gather_cross(done[r], n_ctx)
        if r == 0:
            place, crossed[0] = together(place, crossed[0])
            places = gather_cross(place.reshape(1, groups), n_ctx)
            place_twin = over_core(jnp.stack([places[k] for k in (0, *cross)]))
        else:
            for k in cross:
                crossed[k], gathered[r - 1][k ^ 1], place_twin = together(
                    crossed[k], gathered[r - 1][k ^ 1], place_twin
                )
        for k in list(crossed):
            crossed[k ^ 1] = over_core(crossed[k])
        gathered.append(crossed)
    place_list = []
    for i, k in enumerate((0, *cross)):
        place_list += [places[k], place_twin[i]]
    return pl.pallas_call(
        functools.partial(place_kernel, n_ctx),
        out_shape=shape(groups, feat),
        in_specs=[SMEM] + [VMEM] * (n_ctx + n_ctx * HALVES),
        out_specs=VMEM,
        compiler_params=params(28),
        name="placement",
    )(index, *place_list, *[gathered[r][k] for k in range(n_ctx) for r in range(HALVES)])


def solution(mesh):
    in_specs = (
        P(("dp", "context"), None),
        P(("dp", "context")),
        P(("dp", "context")),
        P(),
        P("context", None, "tensor"),
        P("tensor", "context"),
        P(),
    )
    out_specs = P(("dp", "context"), "tensor")
    sizes = [mesh.shape[name] for name in ("dp", "context", "tensor")]
    body = functools.partial(local, *sizes)
    return jax.shard_map(body, mesh=mesh, in_specs=in_specs, out_specs=out_specs, check_vma=False)
```

```python
import functools
import math

import jax
import jax.numpy as jnp
from jax import lax
from jax.experimental import pallas as pl
from jax.experimental.pallas import tpu as pltpu
from jax.sharding import PartitionSpec as P

HD = 80
WIN = 64
PAIR = 2 * WIN
LANES = 128
HALVES = 2
F32 = jnp.float32
BF16 = jnp.bfloat16
VMEM = pl.BlockSpec(memory_space=pltpu.VMEM)
SMEM = pl.BlockSpec(memory_space=pltpu.SMEM)


def params(mib):
    return pltpu.CompilerParams(vmem_limit_bytes=mib * 1024 * 1024)


def cost(us):
    return pl.CostEstimate(flops=0, bytes_accessed=int(us * 3.3e6), transcendentals=0)


def swap(x, axis, size, bit):
    return lax.ppermute(x, axis, [(i, i ^ bit) for i in range(size)])


def cross_keys(size):
    return range(2, size, 2)


def gather_cross(x, size):
    blocks = {0: x}
    bit = size // 2
    while bit > 1:
        for key in list(blocks):
            blocks[key ^ bit] = swap(blocks[key], "context", size, bit)
        bit //= 2
    return blocks


def gather_xor(x, size):
    blocks = gather_cross(x, size)
    for key in list(blocks):
        blocks[key ^ 1] = swap(blocks[key], "context", size, 1)
    return blocks


def together(*values):
    return lax.optimization_barrier(values)


def one_hot(mask):
    return mask.astype(F32).astype(BF16)


def shape(*dims):
    return jax.ShapeDtypeStruct(dims, BF16)


def packs(rows, cols):
    return rows % 32 == 0 and cols == 2 * LANES + LANES // 2


def packed_shape(rows, cols):
    return (rows * 5 // 2, LANES) if packs(rows, cols) else (rows, cols)


def pack(x):
    rows, cols = x.shape
    if not packs(rows, cols):
        return x
    rest = x[:, 2 * LANES :]
    tail = jnp.concatenate([rest[: rows // 2], rest[rows // 2 :]], axis=1)
    return jnp.concatenate([x[:, :LANES], x[:, LANES : 2 * LANES], tail], axis=0)


def unpack(p, rows, cols):
    if not packs(rows, cols):
        return p[:, : 2 * LANES], p[:, 2 * LANES :]
    tail = p[2 * rows :]
    rest = jnp.concatenate([tail[:, : LANES // 2], tail[:, LANES // 2 :]], axis=0)
    return jnp.concatenate([p[:rows], p[rows : 2 * rows]], axis=1), rest


def pack_kernel(qkv_ref, all_ref, *third_refs):
    for j, ref in enumerate(third_refs):
        all_ref[j] = pack(qkv_ref[j])
        ref[...] = all_ref[j]


def pack_proj_kernel(own_ref, next_ref, far_ref, all_ref, far_out_ref):
    for i, ref in enumerate((own_ref, next_ref, far_ref)):
        all_ref[i] = pack(ref[...])
    far_out_ref[...] = all_ref[2]


def norm_kernel(index_ref, patches_ref, gain_ref, hidden_ref, own_ref):
    rows = patches_ref.shape[0]
    x = patches_ref[...]
    xf = x.astype(F32)
    mean_sq = jnp.mean(xf * xf, axis=-1, keepdims=True)
    gain = gain_ref[...].reshape(1, -1)
    hidden_ref[...] = (xf * lax.rsqrt(mean_sq + 1e-06) * gain).astype(BF16)
    step = 256
    pick = step // 4
    row = lax.broadcasted_iota(jnp.int32, (pick, step), 0)
    col = lax.broadcasted_iota(jnp.int32, (pick, step), 1)
    chosen = one_hot(col == 4 * row + index_ref[1])
    for i in range(rows // step):
        own_ref[i * pick : (i + 1) * pick, :] = jnp.dot(
            chosen, x[i * step : (i + 1) * step], preferred_element_type=F32
        ).astype(BF16)


def load_weights(me, depth, width, count, blocks, w_ref):
    main = 2 * LANES
    for key, thirds in enumerate(blocks):
        rows = pl.ds(pl.multiple_of((me ^ key) * depth, depth), depth)
        tails = []
        for j, third in enumerate(thirds):
            w_ref[rows, j * main : (j + 1) * main], tail = unpack(third, depth, width)
            tails.append(tail)
        w_ref[rows, count * main :] = tails[0] if count == 1 else jnp.concatenate(tails, axis=1)


def score_kernel(n_ctx, width, index_ref, hidden_ref, valid_ref, *refs):
    own_ref, twin_ref = refs[:2]
    others = refs[2 : 2 + 2 * (n_ctx - 2)]
    out_ref, w_ref, q_ref, k_ref = refs[2 + len(others) :]
    rows, feat = hidden_ref.shape
    heads = width // HD
    main = 2 * LANES
    rest = width - main
    blocks = [[own_ref[0], own_ref[1]], [twin_ref[0], twin_ref[1]]]
    for key in range(2, n_ctx):
        blocks.append([others[2 * key - 4][...], others[2 * key - 3][...]])
    load_weights(index_ref[0], feat // n_ctx, width, 2, blocks, w_ref)
    qk = jnp.dot(hidden_ref[...], w_ref[...], preferred_element_type=F32)
    for j, ref in enumerate((q_ref, k_ref)):
        ref[:, :main] = qk[:, j * main : (j + 1) * main].astype(BF16)
        at = 2 * main + j * rest
        ref[:, main:] = qk[:, at : at + rest].astype(BF16)
    q_win = lax.broadcasted_iota(jnp.int32, (PAIR, PAIR), 0) // WIN
    k_win = lax.broadcasted_iota(jnp.int32, (PAIR, PAIR), 1) // WIN
    same = q_win == k_win
    floor = jnp.where(same, F32(-1e30), F32(-3e38))
    zero = jnp.zeros((HD, PAIR), BF16)
    factor = F32(HD ** (-0.5) * math.log2(math.e))
    for p in range(rows // PAIR):
        at = p * PAIR
        turned = k_ref[at : at + PAIR, :].T
        k_all = jnp.concatenate(
            [
                jnp.concatenate(
                    [turned[h * HD : (h + 1) * HD] if i == h else zero for i in range(heads)], axis=1
                )
                for h in range(heads)
            ],
            axis=0,
        )
        scores = jnp.dot(q_ref[at : at + PAIR, :], k_all, preferred_element_type=F32)
        seen = same & (valid_ref[p : p + 1, :] > 0)
        for h in range(heads):
            s = jnp.where(seen, scores[:, h * PAIR : (h + 1) * PAIR], floor)
            e = jnp.exp2((s - jnp.max(s, axis=-1, keepdims=True)) * factor)
            out_ref[at : at + PAIR, h * PAIR : (h + 1) * PAIR] = e.astype(BF16)


def mix_kernel(n_ctx, width, index_ref, hidden_ref, exps_ref, *refs):
    own_ref, twin_ref = refs[:2]
    others = refs[2:n_ctx]
    *out_refs, w_ref, v_ref, mix_ref = refs[n_ctx:]
    rows, feat = hidden_ref.shape
    heads = width // HD
    blocks = [[own_ref[2]], [twin_ref[2]]] + [[ref[...]] for ref in others]
    load_weights(index_ref[0], feat // n_ctx, width, 1, blocks, w_ref)
    v_ref[...] = jnp.dot(hidden_ref[...], w_ref[...], preferred_element_type=F32).astype(BF16)
    lane = lax.broadcasted_iota(jnp.int32, (1, width), 1)
    head_masks = [one_hot((lane >= h * HD) & (lane < (h + 1) * HD)) for h in range(heads)]
    ones = jnp.concatenate([jnp.broadcast_to(m, (PAIR, width)) for m in head_masks], axis=0)
    pick = PAIR // 4
    src = lax.broadcasted_iota(jnp.int32, (PAIR, PAIR), 1)
    dst = lax.broadcasted_iota(jnp.int32, (PAIR, PAIR), 0)
    order = one_hot(src == 4 * (dst % pick) + dst // pick)
    for p in range(rows // PAIR):
        at = p * PAIR
        exps = exps_ref[at : at + PAIR, :]
        v = v_ref[at : at + PAIR, :]
        v_all = jnp.concatenate([v * m for m in head_masks], axis=0)
        mixed = jnp.dot(exps, v_all, preferred_element_type=F32)
        total = jnp.dot(exps, ones, preferred_element_type=F32)
        mixed = (mixed / total).astype(BF16)
        mixed = jnp.dot(order, mixed, preferred_element_type=F32).astype(BF16)
        for t in range(4):
            mix_ref[t, p * pick : (p + 1) * pick, :] = mixed[t * pick : (t + 1) * pick]
    for s, out_ref in enumerate(out_refs):
        out_ref[...] = pack(mix_ref[index_ref[1] ^ s])


def project_kernel(n_ctx, width, col, index_ref, *refs):
    *blocks, own_ref, gain_ref = refs[4 : -HALVES - 1]
    *out_refs, part_ref = refs[-HALVES - 1 :]
    rows = own_ref.shape[0]
    mixes = [unpack(m[...], rows, width) for m in refs[:4]]
    flip = index_ref[2] > 0
    mixes[2:] = [
        [jnp.where(flip, b, a) for a, b in zip(mixes[2], mixes[3])],
        [jnp.where(flip, a, b) for a, b in zip(mixes[2], mixes[3])],
    ]
    me = index_ref[0]
    main = 2 * LANES
    mixed = jnp.concatenate([m for m, _ in mixes] + [r for _, r in mixes], axis=1)
    mains = []
    rests = []
    for key in range(n_ctx):
        pieces = []
        for ref in [blocks.pop(0) for _ in range(2)]:
            pieces += [ref[...]] if len(ref.shape) == 2 else [ref[i] for i in range(ref.shape[0])]
        halves = [unpack(p, width, col) for p in pieces]
        both = []
        for half in ([h[0] for h in halves], [h[1] for h in halves]):
            both.append(jnp.concatenate([h[:main] for h in half] + [h[main:] for h in half], axis=0))
        mains.append(jnp.dot(mixed, both[0], preferred_element_type=F32))
        rests.append(both[1])
    if rests[0].shape[1]:
        rest = jnp.dot(mixed, jnp.concatenate(rests, axis=1), preferred_element_type=F32)
        count = rests[0].shape[1]
        mains = [
            jnp.concatenate([m, rest[:, key * count : (key + 1) * count]], axis=1)
            for key, m in enumerate(mains)
        ]
    for key in range(n_ctx):
        part_ref[me ^ key] = mains[key]
    total = jnp.concatenate([part_ref[i] for i in range(n_ctx)], axis=1)
    total = total + own_ref[...].astype(F32)
    mean_sq = jnp.mean(total * total, axis=-1, keepdims=True)
    normed = (total * lax.rsqrt(mean_sq + 1e-06) * gain_ref[...].reshape(1, -1)).astype(BF16)
    count = rows // HALVES
    for i, out_ref in enumerate(out_refs):
        out_ref[...] = normed[i * count : (i + 1) * count]


def place_kernel(n_ctx, index_ref, *refs):
    place_refs = refs[:n_ctx]
    row_refs = refs[n_ctx:-1]
    out_ref = refs[-1]
    spots = out_ref.shape[0]
    chosen = []
    for place_ref in place_refs:
        target = place_ref[...] - index_ref[0] * spots
        grid = lax.broadcasted_iota(jnp.int32, (spots, target.shape[1]), 0)
        chosen.append(one_hot(grid == target))
    out_ref[...] = jnp.dot(
        jnp.concatenate(chosen, axis=1),
        jnp.concatenate([ref[...] for ref in row_refs], axis=0),
        preferred_element_type=F32,
    ).astype(BF16)


def local(n_dp, n_ctx, n_ten, patches, valid, place, gain_attn, w_qkv, w_proj, gain_merge):
    rows, feat = patches.shape
    depth, _, width = w_qkv.shape
    col = w_proj.shape[1]
    groups = rows // 4
    ten = lax.axis_index("tensor")
    half = lax.axis_index("dp") % 2
    index = jnp.stack([lax.axis_index("context"), ten, half]).astype(jnp.int32)
    cross = list(cross_keys(n_ctx))

    def over_dp(x):
        return swap(x, "dp", n_dp, 1)

    def over_core(x):
        return swap(x, "context", n_ctx, 1)

    third = packed_shape(depth, width)
    piece = packed_shape(width, col)
    own, *thirds = pl.pallas_call(
        pack_kernel,
        out_shape=(shape(3, *third),) + (shape(*third),) * 3,
        in_specs=[VMEM],
        out_specs=(VMEM,) * 4,
        compiler_params=params(8),
        name="pack",
    )(jnp.transpose(w_qkv, (1, 0, 2)))
    query = gather_cross(thirds[0], n_ctx)
    key = gather_cross(thirds[1], n_ctx)
    value = gather_cross(thirds[2], n_ctx)
    by_one = swap(w_proj, "tensor", n_ten, 1)
    far = lax.ppermute(
        w_proj,
        ("dp", "tensor"),
        [
            (d * n_ten + t, d * n_ten + (t ^ (2 + d % 2)))
            for d in range(n_dp)
            for t in range(n_ten)
        ],
    )
    near, far = pl.pallas_call(
        pack_proj_kernel,
        out_shape=(shape(3, *piece), shape(*piece)),
        in_specs=[VMEM] * 3,
        out_specs=(VMEM, VMEM),
        compiler_params=params(8),
        cost_estimate=cost(5),
        name="pack_proj",
    )(w_proj, by_one, far)
    hidden, own_patches = pl.pallas_call(
        norm_kernel,
        out_shape=(shape(rows, feat), shape(groups, feat)),
        in_specs=[SMEM, VMEM, VMEM],
        out_specs=(VMEM, VMEM),
        compiler_params=params(16),
        name="norm",
    )(index, patches, gain_attn)
    twin = over_core(own)
    query, key, hidden, near, far = together(query, key, hidden, near, far)

    query_twin = {k: over_core(query[k]) for k in cross}
    key_twin = {k: over_core(key[k]) for k in cross}
    far2 = over_dp(far)

    shard_list = [own, twin]
    for k in cross:
        shard_list += [query[k], key[k], query_twin[k], key_twin[k]]
    exps = pl.pallas_call(
        functools.partial(score_kernel, n_ctx, width),
        out_shape=shape(rows, width // HD * PAIR),
        in_specs=[SMEM] + [VMEM] * (2 + len(shard_list)),
        out_specs=VMEM,
        scratch_shapes=[pltpu.VMEM((feat, 2 * width), BF16)] + [pltpu.VMEM((rows, width), BF16)] * 2,
        compiler_params=params(20),
        name="scores",
    )(index, hidden, valid.reshape(rows // PAIR, PAIR), *shard_list)
    exps, value = together(exps, value)
    value_twin = {k: over_core(value[k]) for k in cross}
    near, far2 = together(near, far2, exps)[:2]
    low = gather_cross(near, n_ctx)
    high = gather_cross(far2, n_ctx)
    near_twin = over_core(near)
    far2_twin = over_core(far2)
    value_list = []
    for k in cross:
        value_list += [value[k], value_twin[k]]
    mixed = pl.pallas_call(
        functools.partial(mix_kernel, n_ctx, width),
        out_shape=(shape(*packed_shape(groups, width)),) * n_ten,
        in_specs=[SMEM] + [VMEM] * (2 + n_ctx),
        out_specs=(VMEM,) * n_ten,
        scratch_shapes=[
            pltpu.VMEM((feat, width), BF16),
            pltpu.VMEM((rows, width), BF16),
            pltpu.VMEM((4, groups, width), BF16),
        ],
        compiler_params=params(16),
        name="mix",
    )(index, hidden, exps, own, twin, *value_list)

    received = {s: swap(mixed[s], "tensor", n_ten, s) for s in (2, 3, 1)}
    mixed = [mixed[0]] + [received[s] for s in range(1, n_ten)]
    blocks = [near, far2, near_twin, far2_twin]
    mixed, low, high = together(mixed, low, high)
    for k in cross:
        blocks += [low[k], high[k], over_core(low[k]), over_core(high[k])]
    done = pl.pallas_call(
        functools.partial(project_kernel, n_ctx, width, col),
        out_shape=(shape(groups // HALVES, feat),) * HALVES,
        in_specs=[SMEM] + [VMEM] * (n_ten + len(blocks) + 2),
        out_specs=(VMEM,) * HALVES,
        scratch_shapes=[pltpu.VMEM((n_ctx, groups, col), F32)],
        compiler_params=params(24),
        name="project",
    )(index, *mixed, *blocks, own_patches, gain_merge)

    gathered = []
    for r in range(HALVES):
        crossed = gather_cross(done[r], n_ctx)
        if r == 0:
            place, crossed[0] = together(place, crossed[0])
            places = gather_cross(place.reshape(1, groups), n_ctx)
            place_twin = over_core(jnp.stack([places[k] for k in (0, *cross)]))
        else:
            for k in cross:
                crossed[k], gathered[r - 1][k ^ 1], place_twin = together(
                    crossed[k], gathered[r - 1][k ^ 1], place_twin
                )
        for k in list(crossed):
            crossed[k ^ 1] = over_core(crossed[k])
        gathered.append(crossed)
    place_list = []
    for i, k in enumerate((0, *cross)):
        place_list += [places[k], place_twin[i]]
    return pl.pallas_call(
        functools.partial(place_kernel, n_ctx),
        out_shape=shape(groups, feat),
        in_specs=[SMEM] + [VMEM] * (n_ctx + n_ctx * HALVES),
        out_specs=VMEM,
        compiler_params=params(28),
        name="placement",
    )(index, *place_list, *[gathered[r][k] for k in range(n_ctx) for r in range(HALVES)])


def solution(mesh):
    in_specs = (
        P(("dp", "context"), None),
        P(("dp", "context")),
        P(("dp", "context")),
        P(),
        P("context", None, "tensor"),
        P("tensor", "context"),
        P(),
    )
    out_specs = P(("dp", "context"), "tensor")
    sizes = [mesh.shape[name] for name in ("dp", "context", "tensor")]
    body = functools.partial(local, *sizes)
    return jax.shard_map(body, mesh=mesh, in_specs=in_specs, out_specs=out_specs, check_vma=False)
```

```python
import functools
import math

import jax
import jax.numpy as jnp
from jax import lax
from jax.experimental import pallas as pl
from jax.experimental.pallas import tpu as pltpu
from jax.sharding import PartitionSpec as P

HD = 80
WIN = 64
PAIR = 2 * WIN
LANES = 128
HALVES = 2
F32 = jnp.float32
BF16 = jnp.bfloat16
VMEM = pl.BlockSpec(memory_space=pltpu.VMEM)
SMEM = pl.BlockSpec(memory_space=pltpu.SMEM)


def params(mib):
    return pltpu.CompilerParams(vmem_limit_bytes=mib * 1024 * 1024)


def cost(us):
    return pl.CostEstimate(flops=0, bytes_accessed=int(us * 3.3e6), transcendentals=0)


def swap(x, axis, size, bit):
    return lax.ppermute(x, axis, [(i, i ^ bit) for i in range(size)])


def cross_keys(size):
    return range(2, size, 2)


def gather_cross(x, size):
    blocks = {0: x}
    bit = size // 2
    while bit > 1:
        for key in list(blocks):
            blocks[key ^ bit] = swap(blocks[key], "context", size, bit)
        bit //= 2
    return blocks


def gather_xor(x, size):
    blocks = gather_cross(x, size)
    for key in list(blocks):
        blocks[key ^ 1] = swap(blocks[key], "context", size, 1)
    return blocks


def together(*values):
    return lax.optimization_barrier(values)


def one_hot(mask):
    return mask.astype(F32).astype(BF16)


def shape(*dims):
    return jax.ShapeDtypeStruct(dims, BF16)


def packs(rows, cols):
    return rows % 32 == 0 and cols == 2 * LANES + LANES // 2


def packed_shape(rows, cols):
    return (rows * 5 // 2, LANES) if packs(rows, cols) else (rows, cols)


def pack(x):
    rows, cols = x.shape
    if not packs(rows, cols):
        return x
    rest = x[:, 2 * LANES :]
    tail = jnp.concatenate([rest[: rows // 2], rest[rows // 2 :]], axis=1)
    return jnp.concatenate([x[:, :LANES], x[:, LANES : 2 * LANES], tail], axis=0)


def unpack(p, rows, cols):
    if not packs(rows, cols):
        return p[:, : 2 * LANES], p[:, 2 * LANES :]
    tail = p[2 * rows :]
    rest = jnp.concatenate([tail[:, : LANES // 2], tail[:, LANES // 2 :]], axis=0)
    return jnp.concatenate([p[:rows], p[rows : 2 * rows]], axis=1), rest


def pack_kernel(qkv_ref, *out_refs):
    for j, out_ref in enumerate(out_refs):
        out_ref[...] = pack(qkv_ref[j])


def pack_proj_kernel(own_ref, next_ref, far_ref, all_ref, far_out_ref):
    for i, ref in enumerate((own_ref, next_ref, far_ref)):
        all_ref[i] = pack(ref[...])
    far_out_ref[...] = all_ref[2]


def norm_kernel(index_ref, patches_ref, gain_ref, hidden_ref, own_ref):
    rows = patches_ref.shape[0]
    x = patches_ref[...]
    xf = x.astype(F32)
    mean_sq = jnp.mean(xf * xf, axis=-1, keepdims=True)
    gain = gain_ref[...].reshape(1, -1)
    hidden_ref[...] = (xf * lax.rsqrt(mean_sq + 1e-06) * gain).astype(BF16)
    step = 256
    pick = step // 4
    row = lax.broadcasted_iota(jnp.int32, (pick, step), 0)
    col = lax.broadcasted_iota(jnp.int32, (pick, step), 1)
    chosen = one_hot(col == 4 * row + index_ref[1])
    for i in range(rows // step):
        own_ref[i * pick : (i + 1) * pick, :] = jnp.dot(
            chosen, x[i * step : (i + 1) * step], preferred_element_type=F32
        ).astype(BF16)


def load_weights(me, depth, width, count, blocks, w_ref):
    main = 2 * LANES
    for key, thirds in enumerate(blocks):
        rows = pl.ds(pl.multiple_of((me ^ key) * depth, depth), depth)
        tails = []
        for j, third in enumerate(thirds):
            w_ref[rows, j * main : (j + 1) * main], tail = unpack(third, depth, width)
            tails.append(tail)
        w_ref[rows, count * main :] = tails[0] if count == 1 else jnp.concatenate(tails, axis=1)


def bias_kernel(valid_ref, out_ref):
    q_win = lax.broadcasted_iota(jnp.int32, (PAIR, PAIR), 0) // WIN
    k_win = lax.broadcasted_iota(jnp.int32, (PAIR, PAIR), 1) // WIN
    same = q_win == k_win
    floor = jnp.where(same, F32(-1e30), F32(-3e38))
    for p in range(valid_ref.shape[0]):
        seen = same & (valid_ref[p : p + 1, :] > 0)
        out_ref[p * PAIR : (p + 1) * PAIR, :] = jnp.where(seen, F32(0), floor)


def score_kernel(n_ctx, width, index_ref, hidden_ref, bias_ref, *refs):
    count = n_ctx // 2
    *shards, query_ref, key_ref = refs[: n_ctx + 2]
    out_ref, w_ref, q_ref, k_ref = refs[n_ctx + 2 :]
    rows, feat = hidden_ref.shape
    heads = width // HD
    main = 2 * LANES
    rest = width - main
    blocks = []
    for i in range(count):
        blocks.append([shards[i][...], shards[count + i][...]])
        blocks.append([query_ref[i], key_ref[i]])
    load_weights(index_ref[0], feat // n_ctx, width, 2, blocks, w_ref)
    qk = jnp.dot(hidden_ref[...], w_ref[...], preferred_element_type=F32)
    for j, ref in enumerate((q_ref, k_ref)):
        ref[:, :main] = qk[:, j * main : (j + 1) * main].astype(BF16)
        at = 2 * main + j * rest
        ref[:, main:] = qk[:, at : at + rest].astype(BF16)
    zero = jnp.zeros((HD, PAIR), BF16)
    factor = F32(HD ** (-0.5) * math.log2(math.e))
    for p in range(rows // PAIR):
        at = p * PAIR
        turned = k_ref[at : at + PAIR, :].T
        k_all = jnp.concatenate(
            [
                jnp.concatenate(
                    [turned[h * HD : (h + 1) * HD] if i == h else zero for i in range(heads)], axis=1
                )
                for h in range(heads)
            ],
            axis=0,
        )
        scores = jnp.dot(q_ref[at : at + PAIR, :], k_all, preferred_element_type=F32)
        bias = bias_ref[at : at + PAIR, :]
        for h in range(heads):
            s = scores[:, h * PAIR : (h + 1) * PAIR] + bias
            e = jnp.exp2((s - jnp.max(s, axis=-1, keepdims=True)) * factor)
            out_ref[at : at + PAIR, h * PAIR : (h + 1) * PAIR] = e.astype(BF16)


def mix_kernel(n_ctx, width, index_ref, hidden_ref, exps_ref, *refs):
    twin_ref, *own_refs = refs[: n_ctx // 2 + 1]
    *out_refs, w_ref, v_ref, mix_ref = refs[n_ctx // 2 + 1 :]
    rows, feat = hidden_ref.shape
    heads = width // HD
    blocks = []
    for i, ref in enumerate(own_refs):
        blocks += [[ref[...]], [twin_ref[i]]]
    load_weights(index_ref[0], feat // n_ctx, width, 1, blocks, w_ref)
    v_ref[...] = jnp.dot(hidden_ref[...], w_ref[...], preferred_element_type=F32).astype(BF16)
    lane = lax.broadcasted_iota(jnp.int32, (1, width), 1)
    head_masks = [one_hot((lane >= h * HD) & (lane < (h + 1) * HD)) for h in range(heads)]
    ones = jnp.concatenate([jnp.broadcast_to(m, (PAIR, width)) for m in head_masks], axis=0)
    pick = PAIR // 4
    src = lax.broadcasted_iota(jnp.int32, (PAIR, PAIR), 1)
    dst = lax.broadcasted_iota(jnp.int32, (PAIR, PAIR), 0)
    order = one_hot(src == 4 * (dst % pick) + dst // pick)
    for p in range(rows // PAIR):
        at = p * PAIR
        exps = exps_ref[at : at + PAIR, :]
        v = v_ref[at : at + PAIR, :]
        v_all = jnp.concatenate([v * m for m in head_masks], axis=0)
        mixed = jnp.dot(exps, v_all, preferred_element_type=F32)
        total = jnp.dot(exps, ones, preferred_element_type=F32)
        mixed = (mixed / total).astype(BF16)
        mixed = jnp.dot(order, mixed, preferred_element_type=F32).astype(BF16)
        for t in range(4):
            mix_ref[t, p * pick : (p + 1) * pick, :] = mixed[t * pick : (t + 1) * pick]
    for s, out_ref in enumerate(out_refs):
        out_ref[...] = pack(mix_ref[index_ref[1] ^ s])


def project_kernel(n_ctx, width, col, index_ref, *refs):
    *blocks, own_ref, gain_ref = refs[4 : -HALVES - 1]
    *out_refs, part_ref = refs[-HALVES - 1 :]
    rows = own_ref.shape[0]
    mixes = [unpack(m[...], rows, width) for m in refs[:4]]
    flip = index_ref[2] > 0
    mixes[2:] = [
        [jnp.where(flip, b, a) for a, b in zip(mixes[2], mixes[3])],
        [jnp.where(flip, a, b) for a, b in zip(mixes[2], mixes[3])],
    ]
    me = index_ref[0]
    main = 2 * LANES
    mixed = jnp.concatenate([m for m, _ in mixes] + [r for _, r in mixes], axis=1)
    mains = []
    rests = []
    for key in range(n_ctx):
        three, one = blocks.pop(0), blocks.pop(0)
        pieces = [three[0], three[1], three[2], one[...]]
        halves = [unpack(p, width, col) for p in pieces]
        both = []
        for half in ([h[0] for h in halves], [h[1] for h in halves]):
            both.append(jnp.concatenate([h[:main] for h in half] + [h[main:] for h in half], axis=0))
        mains.append(jnp.dot(mixed, both[0], preferred_element_type=F32))
        rests.append(both[1])
    if rests[0].shape[1]:
        rest = jnp.dot(mixed, jnp.concatenate(rests, axis=1), preferred_element_type=F32)
        count = rests[0].shape[1]
        mains = [
            jnp.concatenate([m, rest[:, key * count : (key + 1) * count]], axis=1)
            for key, m in enumerate(mains)
        ]
    for key in range(n_ctx):
        part_ref[me ^ key] = mains[key]
    total = jnp.concatenate([part_ref[i] for i in range(n_ctx)], axis=1)
    total = total + own_ref[...].astype(F32)
    mean_sq = jnp.mean(total * total, axis=-1, keepdims=True)
    normed = (total * lax.rsqrt(mean_sq + 1e-06) * gain_ref[...].reshape(1, -1)).astype(BF16)
    count = rows // HALVES
    for i, out_ref in enumerate(out_refs):
        out_ref[...] = normed[i * count : (i + 1) * count]


def place_kernel(n_ctx, index_ref, *refs):
    place_refs = refs[:n_ctx]
    row_refs = refs[n_ctx:-1]
    out_ref = refs[-1]
    spots = out_ref.shape[0]
    chosen = []
    for place_ref in place_refs:
        target = place_ref[...] - index_ref[0] * spots
        grid = lax.broadcasted_iota(jnp.int32, (spots, target.shape[1]), 0)
        chosen.append(one_hot(grid == target))
    out_ref[...] = jnp.dot(
        jnp.concatenate(chosen, axis=1),
        jnp.concatenate([ref[...] for ref in row_refs], axis=0),
        preferred_element_type=F32,
    ).astype(BF16)


def local(n_dp, n_ctx, n_ten, patches, valid, place, gain_attn, w_qkv, w_proj, gain_merge):
    rows, feat = patches.shape
    depth, _, width = w_qkv.shape
    col = w_proj.shape[1]
    groups = rows // 4
    ten = lax.axis_index("tensor")
    half = lax.axis_index("dp") % 2
    index = jnp.stack([lax.axis_index("context"), ten, half]).astype(jnp.int32)
    cross = list(cross_keys(n_ctx))

    def over_dp(x):
        return swap(x, "dp", n_dp, 1)

    def over_core(x):
        return swap(x, "context", n_ctx, 1)

    third = packed_shape(depth, width)
    piece = packed_shape(width, col)
    query, key, value = pl.pallas_call(
        pack_kernel,
        out_shape=(shape(*third),) * 3,
        in_specs=[VMEM],
        out_specs=(VMEM,) * 3,
        compiler_params=params(8),
        name="pack",
    )(jnp.transpose(w_qkv, (1, 0, 2)))
    query = gather_cross(query, n_ctx)
    key = gather_cross(key, n_ctx)
    value = gather_cross(value, n_ctx)
    by_one = swap(w_proj, "tensor", n_ten, 1)
    far = lax.ppermute(
        w_proj,
        ("dp", "tensor"),
        [
            (d * n_ten + t, d * n_ten + (t ^ (2 + d % 2)))
            for d in range(n_dp)
            for t in range(n_ten)
        ],
    )
    hidden, own_patches = pl.pallas_call(
        norm_kernel,
        out_shape=(shape(rows, feat), shape(groups, feat)),
        in_specs=[SMEM, VMEM, VMEM],
        out_specs=(VMEM, VMEM),
        compiler_params=params(16),
        name="norm",
    )(index, patches, gain_attn)
    by_one, far, hidden = together(by_one, far, hidden)
    near, far = pl.pallas_call(
        pack_proj_kernel,
        out_shape=(shape(3, *piece), shape(*piece)),
        in_specs=[VMEM] * 3,
        out_specs=(VMEM, VMEM),
        compiler_params=params(8),
        cost_estimate=cost(1000),
        name="pack_proj",
    )(w_proj, by_one, far)
    query, key, hidden, near, far = together(query, key, hidden, near, far)

    low = gather_cross(near[0], n_ctx)
    shard_list = [x[k] for x in (query, key) for k in (0, *cross)]
    count = len(shard_list) // 2
    shard_list += [over_core(jnp.stack(shard_list[:count])), over_core(jnp.stack(shard_list[count:]))]
    bias = pl.pallas_call(
        bias_kernel,
        out_shape=jax.ShapeDtypeStruct((rows, PAIR), F32),
        in_specs=[VMEM],
        out_specs=VMEM,
        compiler_params=params(8),
        name="bias",
    )(valid.reshape(rows // PAIR, PAIR))

    exps = pl.pallas_call(
        functools.partial(score_kernel, n_ctx, width),
        out_shape=shape(rows, width // HD * PAIR),
        in_specs=[SMEM] + [VMEM] * (2 + len(shard_list)),
        out_specs=VMEM,
        scratch_shapes=[pltpu.VMEM((feat, 2 * width), BF16)] + [pltpu.VMEM((rows, width), BF16)] * 2,
        compiler_params=params(20),
        name="scores",
    )(index, hidden, bias, *shard_list)
    exps, value, far = together(exps, value, far)
    values = [value[k] for k in (0, *cross)]
    value_twin = over_core(jnp.stack(values))
    far2 = over_dp(far)
    middle = gather_cross(near[1:], n_ctx)
    near_twin = over_core(near)
    mixed = pl.pallas_call(
        functools.partial(mix_kernel, n_ctx, width),
        out_shape=(shape(*packed_shape(groups, width)),) * n_ten,
        in_specs=[SMEM] + [VMEM] * (3 + len(values)),
        out_specs=(VMEM,) * n_ten,
        scratch_shapes=[
            pltpu.VMEM((feat, width), BF16),
            pltpu.VMEM((rows, width), BF16),
            pltpu.VMEM((4, groups, width), BF16),
        ],
        compiler_params=params(16),
        name="mix",
    )(index, hidden, exps, value_twin, *values)

    mixed, far2, near_twin = together(mixed, far2, near_twin)
    received = {s: swap(mixed[s], "tensor", n_ten, s) for s in (2, 3, 1)}
    mixed = [mixed[0]] + [received[s] for s in range(1, n_ten)]
    high = gather_cross(far2, n_ctx)
    mixed, low, middle, high = together(mixed, low, middle, high)
    high_twin = over_core(jnp.stack([far2] + [high[k] for k in cross]))
    blocks = [near, far2, near_twin, high_twin[0]]
    for i, k in enumerate(cross):
        three = jnp.concatenate([low[k][None], middle[k]], axis=0)
        blocks += [three, high[k], over_core(three), high_twin[1 + i]]
    done = pl.pallas_call(
        functools.partial(project_kernel, n_ctx, width, col),
        out_shape=(shape(groups // HALVES, feat),) * HALVES,
        in_specs=[SMEM] + [VMEM] * (n_ten + len(blocks) + 2),
        out_specs=(VMEM,) * HALVES,
        scratch_shapes=[pltpu.VMEM((n_ctx, groups, col), F32)],
        compiler_params=params(24),
        name="project",
    )(index, *mixed, *blocks, own_patches, gain_merge)

    gathered = []
    for r in range(HALVES):
        crossed = gather_cross(done[r], n_ctx)
        if r == 0:
            place, crossed[0] = together(place, crossed[0])
            places = gather_cross(place.reshape(1, groups), n_ctx)
            place_twin = over_core(jnp.stack([places[k] for k in (0, *cross)]))
        else:
            for k in cross:
                crossed[k], gathered[r - 1][k ^ 1], place_twin = together(
                    crossed[k], gathered[r - 1][k ^ 1], place_twin
                )
        for k in list(crossed):
            crossed[k ^ 1] = over_core(crossed[k])
        gathered.append(crossed)
    place_list = []
    for i, k in enumerate((0, *cross)):
        place_list += [places[k], place_twin[i]]
    return pl.pallas_call(
        functools.partial(place_kernel, n_ctx),
        out_shape=shape(groups, feat),
        in_specs=[SMEM] + [VMEM] * (n_ctx + n_ctx * HALVES),
        out_specs=VMEM,
        compiler_params=params(28),
        name="placement",
    )(index, *place_list, *[gathered[r][k] for k in range(n_ctx) for r in range(HALVES)])


def solution(mesh):
    in_specs = (
        P(("dp", "context"), None),
        P(("dp", "context")),
        P(("dp", "context")),
        P(),
        P("context", None, "tensor"),
        P("tensor", "context"),
        P(),
    )
    out_specs = P(("dp", "context"), "tensor")
    sizes = [mesh.shape[name] for name in ("dp", "context", "tensor")]
    body = functools.partial(local, *sizes)
    return jax.shard_map(body, mesh=mesh, in_specs=in_specs, out_specs=out_specs, check_vma=False)
```

```python
import functools
import math

import jax
import jax.numpy as jnp
from jax import lax
from jax.experimental import pallas as pl
from jax.experimental.pallas import tpu as pltpu
from jax.sharding import PartitionSpec as P

HD = 80
WIN = 64
PAIR = 2 * WIN
LANES = 128
HALVES = 2
F32 = jnp.float32
BF16 = jnp.bfloat16
VMEM = pl.BlockSpec(memory_space=pltpu.VMEM)
SMEM = pl.BlockSpec(memory_space=pltpu.SMEM)


def params(mib):
    return pltpu.CompilerParams(vmem_limit_bytes=mib * 1024 * 1024)


def swap(x, axis, size, bit):
    return lax.ppermute(x, axis, [(i, i ^ bit) for i in range(size)])


def cross_keys(size):
    return range(2, size, 2)


def gather_cross(x, size):
    blocks = {0: x}
    bit = size // 2
    while bit > 1:
        for key in list(blocks):
            blocks[key ^ bit] = swap(blocks[key], "context", size, bit)
        bit //= 2
    return blocks


def gather_xor(x, size):
    blocks = gather_cross(x, size)
    for key in list(blocks):
        blocks[key ^ 1] = swap(blocks[key], "context", size, 1)
    return blocks


def together(*values):
    return lax.optimization_barrier(values)


def one_hot(mask):
    return mask.astype(F32).astype(BF16)


def shape(*dims):
    return jax.ShapeDtypeStruct(dims, BF16)


def packs(rows, cols):
    return rows % 32 == 0 and cols == 2 * LANES + LANES // 2


def packed_shape(rows, cols):
    return (rows * 5 // 2, LANES) if packs(rows, cols) else (rows, cols)


def pack(x):
    rows, cols = x.shape
    if not packs(rows, cols):
        return x
    rest = x[:, 2 * LANES :]
    tail = jnp.concatenate([rest[: rows // 2], rest[rows // 2 :]], axis=1)
    return jnp.concatenate([x[:, :LANES], x[:, LANES : 2 * LANES], tail], axis=0)


def unpack(p, rows, cols):
    if not packs(rows, cols):
        return p[:, : 2 * LANES], p[:, 2 * LANES :]
    tail = p[2 * rows :]
    rest = jnp.concatenate([tail[:, : LANES // 2], tail[:, LANES // 2 :]], axis=0)
    return jnp.concatenate([p[:rows], p[rows : 2 * rows]], axis=1), rest


def pack_kernel(qkv_ref, all_ref, *third_refs):
    for j, ref in enumerate(third_refs):
        all_ref[j] = pack(qkv_ref[j])
        ref[...] = all_ref[j]


def pack_proj_kernel(proj_ref, out_ref):
    block = pack(proj_ref[...])
    rows = block.shape[0]
    out_ref[:rows, :] = block
    if out_ref.shape[0] > rows:
        out_ref[rows:, :] = jnp.zeros((out_ref.shape[0] - rows, block.shape[1]), BF16)


def split_proj_kernel(proj_ref, all_ref, low_ref, high_ref):
    half, rows = low_ref.shape[:2]
    all_ref[...] = proj_ref[:, :rows, :]
    low_ref[...] = all_ref[:half]
    high_ref[...] = all_ref[half:]


def norm_kernel(index_ref, patches_ref, gain_ref, hidden_ref, own_ref):
    rows = patches_ref.shape[0]
    x = patches_ref[...]
    xf = x.astype(F32)
    mean_sq = jnp.mean(xf * xf, axis=-1, keepdims=True)
    gain = gain_ref[...].reshape(1, -1)
    hidden_ref[...] = (xf * lax.rsqrt(mean_sq + 1e-06) * gain).astype(BF16)
    step = 256
    pick = step // 4
    row = lax.broadcasted_iota(jnp.int32, (pick, step), 0)
    col = lax.broadcasted_iota(jnp.int32, (pick, step), 1)
    chosen = one_hot(col == 4 * row + index_ref[1])
    for i in range(rows // step):
        own_ref[i * pick : (i + 1) * pick, :] = jnp.dot(
            chosen, x[i * step : (i + 1) * step], preferred_element_type=F32
        ).astype(BF16)


def load_weights(me, depth, width, count, blocks, w_ref):
    main = 2 * LANES
    for key, thirds in enumerate(blocks):
        rows = pl.ds(pl.multiple_of((me ^ key) * depth, depth), depth)
        tails = []
        for j, third in enumerate(thirds):
            w_ref[rows, j * main : (j + 1) * main], tail = unpack(third, depth, width)
            tails.append(tail)
        w_ref[rows, count * main :] = tails[0] if count == 1 else jnp.concatenate(tails, axis=1)


def score_kernel(n_ctx, width, index_ref, hidden_ref, valid_ref, *refs):
    own_ref, twin_ref = refs[:2]
    others = refs[2 : 2 + 2 * (n_ctx - 2)]
    out_ref, w_ref, q_ref, k_ref = refs[2 + len(others) :]
    rows, feat = hidden_ref.shape
    heads = width // HD
    main = 2 * LANES
    rest = width - main
    blocks = [[own_ref[0], own_ref[1]], [twin_ref[0], twin_ref[1]]]
    for key in range(2, n_ctx):
        blocks.append([others[2 * key - 4][...], others[2 * key - 3][...]])
    load_weights(index_ref[0], feat // n_ctx, width, 2, blocks, w_ref)
    qk = jnp.dot(hidden_ref[...], w_ref[...], preferred_element_type=F32)
    for j, ref in enumerate((q_ref, k_ref)):
        ref[:, :main] = qk[:, j * main : (j + 1) * main].astype(BF16)
        at = 2 * main + j * rest
        ref[:, main:] = qk[:, at : at + rest].astype(BF16)
    q_win = lax.broadcasted_iota(jnp.int32, (PAIR, PAIR), 0) // WIN
    k_win = lax.broadcasted_iota(jnp.int32, (PAIR, PAIR), 1) // WIN
    same = q_win == k_win
    floor = jnp.where(same, F32(-1e30), F32(-3e38))
    zero = jnp.zeros((HD, PAIR), BF16)
    factor = F32(HD ** (-0.5) * math.log2(math.e))
    for p in range(rows // PAIR):
        at = p * PAIR
        turned = k_ref[at : at + PAIR, :].T
        k_all = jnp.concatenate(
            [
                jnp.concatenate(
                    [turned[h * HD : (h + 1) * HD] if i == h else zero for i in range(heads)], axis=1
                )
                for h in range(heads)
            ],
            axis=0,
        )
        scores = jnp.dot(q_ref[at : at + PAIR, :], k_all, preferred_element_type=F32)
        seen = same & (valid_ref[p : p + 1, :] > 0)
        for h in range(heads):
            s = jnp.where(seen, scores[:, h * PAIR : (h + 1) * PAIR], floor)
            e = jnp.exp2((s - jnp.max(s, axis=-1, keepdims=True)) * factor)
            out_ref[at : at + PAIR, h * PAIR : (h + 1) * PAIR] = e.astype(BF16)


def mix_kernel(n_ctx, width, index_ref, hidden_ref, exps_ref, *refs):
    own_ref, twin_ref = refs[:2]
    others = refs[2:n_ctx]
    *out_refs, w_ref, v_ref, mix_ref = refs[n_ctx:]
    rows, feat = hidden_ref.shape
    heads = width // HD
    blocks = [[own_ref[2]], [twin_ref[2]]] + [[ref[...]] for ref in others]
    load_weights(index_ref[0], feat // n_ctx, width, 1, blocks, w_ref)
    v_ref[...] = jnp.dot(hidden_ref[...], w_ref[...], preferred_element_type=F32).astype(BF16)
    lane = lax.broadcasted_iota(jnp.int32, (1, width), 1)
    head_masks = [one_hot((lane >= h * HD) & (lane < (h + 1) * HD)) for h in range(heads)]
    ones = jnp.concatenate([jnp.broadcast_to(m, (PAIR, width)) for m in head_masks], axis=0)
    pick = PAIR // 4
    src = lax.broadcasted_iota(jnp.int32, (PAIR, PAIR), 1)
    dst = lax.broadcasted_iota(jnp.int32, (PAIR, PAIR), 0)
    order = one_hot(src == 4 * (dst % pick) + dst // pick)
    for p in range(rows // PAIR):
        at = p * PAIR
        exps = exps_ref[at : at + PAIR, :]
        v = v_ref[at : at + PAIR, :]
        v_all = jnp.concatenate([v * m for m in head_masks], axis=0)
        mixed = jnp.dot(exps, v_all, preferred_element_type=F32)
        total = jnp.dot(exps, ones, preferred_element_type=F32)
        mixed = (mixed / total).astype(BF16)
        mixed = jnp.dot(order, mixed, preferred_element_type=F32).astype(BF16)
        for t in range(4):
            mix_ref[t, p * pick : (p + 1) * pick, :] = mixed[t * pick : (t + 1) * pick]
    for s, out_ref in enumerate(out_refs):
        out_ref[...] = pack(mix_ref[index_ref[1] ^ s])


def project_kernel(n_ctx, width, col, index_ref, *refs):
    *blocks, own_ref, gain_ref = refs[4 : -HALVES - 2]
    *out_refs, part_ref, mix_ref = refs[-HALVES - 2 :]
    rows = own_ref.shape[0]
    for s in range(4):
        mix_ref[index_ref[1] ^ s] = refs[s][...]
    mixes = [unpack(mix_ref[t], rows, width) for t in range(4)]
    me = index_ref[0]
    main = 2 * LANES
    mixed = jnp.concatenate([m for m, _ in mixes] + [r for _, r in mixes], axis=1)
    mains = []
    rests = []
    for key in range(n_ctx):
        pieces = []
        for ref in [blocks.pop(0) for _ in range(1 if key < 2 else 2)]:
            pieces += [ref[i] for i in range(ref.shape[0])]
        halves = [unpack(p, width, col) for p in pieces]
        both = []
        for half in ([h[0] for h in halves], [h[1] for h in halves]):
            both.append(jnp.concatenate([h[:main] for h in half] + [h[main:] for h in half], axis=0))
        mains.append(jnp.dot(mixed, both[0], preferred_element_type=F32))
        rests.append(both[1])
    if rests[0].shape[1]:
        rest = jnp.dot(mixed, jnp.concatenate(rests, axis=1), preferred_element_type=F32)
        count = rests[0].shape[1]
        mains = [
            jnp.concatenate([m, rest[:, key * count : (key + 1) * count]], axis=1)
            for key, m in enumerate(mains)
        ]
    for key in range(n_ctx):
        part_ref[me ^ key] = mains[key]
    total = jnp.concatenate([part_ref[i] for i in range(n_ctx)], axis=1)
    total = total + own_ref[...].astype(F32)
    mean_sq = jnp.mean(total * total, axis=-1, keepdims=True)
    normed = (total * lax.rsqrt(mean_sq + 1e-06) * gain_ref[...].reshape(1, -1)).astype(BF16)
    count = rows // HALVES
    for i, out_ref in enumerate(out_refs):
        out_ref[...] = normed[i * count : (i + 1) * count]


def place_kernel(n_ctx, index_ref, *refs):
    place_refs = refs[:n_ctx]
    row_refs = refs[n_ctx:-1]
    out_ref = refs[-1]
    spots = out_ref.shape[0]
    chosen = []
    for place_ref in place_refs:
        target = place_ref[...] - index_ref[0] * spots
        grid = lax.broadcasted_iota(jnp.int32, (spots, target.shape[1]), 0)
        chosen.append(one_hot(grid == target))
    out_ref[...] = jnp.dot(
        jnp.concatenate(chosen, axis=1),
        jnp.concatenate([ref[...] for ref in row_refs], axis=0),
        preferred_element_type=F32,
    ).astype(BF16)


def local(n_dp, n_ctx, n_ten, patches, valid, place, gain_attn, w_qkv, w_proj, gain_merge):
    rows, feat = patches.shape
    depth, _, width = w_qkv.shape
    col = w_proj.shape[1]
    groups = rows // 4
    ten = lax.axis_index("tensor")
    half = lax.axis_index("dp") % 2
    index = jnp.stack([lax.axis_index("context"), ten, half]).astype(jnp.int32)
    cross = list(cross_keys(n_ctx))

    def over_dp(x):
        return swap(x, "dp", n_dp, 1)

    def over_core(x):
        return swap(x, "context", n_ctx, 1)

    third = packed_shape(depth, width)
    piece = packed_shape(width, col)
    own, *thirds = pl.pallas_call(
        pack_kernel,
        out_shape=(shape(3, *third),) + (shape(*third),) * 3,
        in_specs=[VMEM],
        out_specs=(VMEM,) * 4,
        compiler_params=params(8),
        name="pack",
    )(jnp.transpose(w_qkv, (1, 0, 2)))
    w_proj, own = together(w_proj, own)
    spare = 256 if packs(width, col) else 0
    proj = pl.pallas_call(
        pack_proj_kernel,
        out_shape=shape(piece[0] + spare, piece[1]),
        in_specs=[VMEM],
        out_specs=VMEM,
        compiler_params=params(8),
        name="pack_proj",
    )(w_proj)
    proj = lax.all_gather(proj, "tensor")
    query = gather_cross(thirds[0], n_ctx)
    key = gather_cross(thirds[1], n_ctx)
    value = gather_cross(thirds[2], n_ctx)
    query, patches = together(query, patches)
    query_twin = {k: over_core(query[k]) for k in cross}
    hidden, own_patches = pl.pallas_call(
        norm_kernel,
        out_shape=(shape(rows, feat), shape(groups, feat)),
        in_specs=[SMEM, VMEM, VMEM],
        out_specs=(VMEM, VMEM),
        compiler_params=params(16),
        name="norm",
    )(index, patches, gain_attn)
    key, hidden = together(key, hidden)
    twin = over_core(own)
    key_twin = {k: over_core(key[k]) for k in cross}

    shard_list = [own, twin]
    for k in cross:
        shard_list += [query[k], key[k], query_twin[k], key_twin[k]]
    exps = pl.pallas_call(
        functools.partial(score_kernel, n_ctx, width),
        out_shape=shape(rows, width // HD * PAIR),
        in_specs=[SMEM] + [VMEM] * (2 + len(shard_list)),
        out_specs=VMEM,
        scratch_shapes=[pltpu.VMEM((feat, 2 * width), BF16)] + [pltpu.VMEM((rows, width), BF16)] * 2,
        compiler_params=params(20),
        name="scores",
    )(index, hidden, valid.reshape(rows // PAIR, PAIR), *shard_list)
    exps, value, proj = together(exps, value, proj)
    value_twin = {k: over_core(value[k]) for k in cross}
    proj, proj_low, proj_high = pl.pallas_call(
        split_proj_kernel,
        out_shape=(shape(n_ten, *piece), shape(n_ten // 2, *piece), shape(n_ten // 2, *piece)),
        in_specs=[VMEM],
        out_specs=(VMEM,) * 3,
        compiler_params=params(12),
        name="split_proj",
    )(proj)
    low = gather_cross(proj_low, n_ctx)
    high = gather_cross(proj_high, n_ctx)
    value_list = []
    for k in cross:
        value_list += [value[k], value_twin[k]]
    mixed = pl.pallas_call(
        functools.partial(mix_kernel, n_ctx, width),
        out_shape=(shape(*packed_shape(groups, width)),) * n_ten,
        in_specs=[SMEM] + [VMEM] * (2 + n_ctx),
        out_specs=(VMEM,) * n_ten,
        scratch_shapes=[
            pltpu.VMEM((feat, width), BF16),
            pltpu.VMEM((rows, width), BF16),
            pltpu.VMEM((4, groups, width), BF16),
        ],
        compiler_params=params(16),
        name="mix",
    )(index, hidden, exps, own, twin, *value_list)

    proj_twin = over_core(proj)
    mixed, proj_twin = together(mixed, proj_twin)
    received = {s: swap(mixed[s], "tensor", n_ten, s) for s in (2, 3, 1)}
    mixed = [mixed[0]] + [received[s] for s in range(1, n_ten)]
    mixed, low, high, place = together(mixed, low, high, place)
    places = gather_cross(place.reshape(1, groups), n_ctx)
    blocks = [proj, proj_twin]
    for k in cross:
        blocks += [low[k], high[k], over_core(low[k]), over_core(high[k])]
    done = pl.pallas_call(
        functools.partial(project_kernel, n_ctx, width, col),
        out_shape=(shape(groups // HALVES, feat),) * HALVES,
        in_specs=[SMEM] + [VMEM] * (n_ten + len(blocks) + 2),
        out_specs=(VMEM,) * HALVES,
        scratch_shapes=[
            pltpu.VMEM((n_ctx, groups, col), F32),
            pltpu.VMEM((n_ten, *packed_shape(groups, width)), BF16),
        ],
        compiler_params=params(24),
        name="project",
    )(index, *mixed, *blocks, own_patches, gain_merge)

    done, place_group = together(done, jnp.stack([places[k] for k in (0, *cross)]))
    gathered = []
    for r in range(HALVES):
        crossed = gather_cross(done[r], n_ctx)
        if r == 0:
            place_twin = over_core(place_group)
        else:
            for k in cross:
                crossed[k], gathered[r - 1][k ^ 1], place_twin = together(
                    crossed[k], gathered[r - 1][k ^ 1], place_twin
                )
        for k in list(crossed):
            crossed[k ^ 1] = over_core(crossed[k])
        gathered.append(crossed)
    place_list = []
    for i, k in enumerate((0, *cross)):
        place_list += [places[k], place_twin[i]]
    return pl.pallas_call(
        functools.partial(place_kernel, n_ctx),
        out_shape=shape(groups, feat),
        in_specs=[SMEM] + [VMEM] * (n_ctx + n_ctx * HALVES),
        out_specs=VMEM,
        compiler_params=params(28),
        name="placement",
    )(index, *place_list, *[gathered[r][k] for k in range(n_ctx) for r in range(HALVES)])


def solution(mesh):
    in_specs = (
        P(("dp", "context"), None),
        P(("dp", "context")),
        P(("dp", "context")),
        P(),
        P("context", None, "tensor"),
        P("tensor", "context"),
        P(),
    )
    out_specs = P(("dp", "context"), "tensor")
    sizes = [mesh.shape[name] for name in ("dp", "context", "tensor")]
    body = functools.partial(local, *sizes)
    return jax.shard_map(body, mesh=mesh, in_specs=in_specs, out_specs=out_specs, check_vma=False)
```

```python
import functools

import jax
import jax.numpy as jnp
from jax import lax
from jax.experimental import pallas as pl
from jax.experimental.pallas import tpu as pltpu
from jax.sharding import PartitionSpec as P

HD = 80
WIN = 64
PAIR = 2 * WIN
LANES = 128
HALVES = 2
F32 = jnp.float32
BF16 = jnp.bfloat16
VMEM = pl.BlockSpec(memory_space=pltpu.VMEM)
SMEM = pl.BlockSpec(memory_space=pltpu.SMEM)


def params(mib):
    return pltpu.CompilerParams(vmem_limit_bytes=mib * 1024 * 1024)


def swap(x, axis, size, bit):
    return lax.ppermute(x, axis, [(i, i ^ bit) for i in range(size)])


def cross_keys(size):
    return range(2, size, 2)


def gather_cross(x, size):
    blocks = {0: x}
    bit = size // 2
    while bit > 1:
        for key in list(blocks):
            blocks[key ^ bit] = swap(blocks[key], "context", size, bit)
        bit //= 2
    return blocks


def gather_xor(x, size):
    blocks = gather_cross(x, size)
    for key in list(blocks):
        blocks[key ^ 1] = swap(blocks[key], "context", size, 1)
    return blocks


def together(*values):
    return lax.optimization_barrier(values)


def one_hot(mask):
    return mask.astype(F32).astype(BF16)


def shape(*dims):
    return jax.ShapeDtypeStruct(dims, BF16)


def packs(rows, cols):
    return rows % 32 == 0 and cols == 2 * LANES + LANES // 2


def packed_shape(rows, cols):
    return (rows * 5 // 2, LANES) if packs(rows, cols) else (rows, cols)


def pack(x):
    rows, cols = x.shape
    if not packs(rows, cols):
        return x
    rest = x[:, 2 * LANES :]
    tail = jnp.concatenate([rest[: rows // 2], rest[rows // 2 :]], axis=1)
    return jnp.concatenate([x[:, :LANES], x[:, LANES : 2 * LANES], tail], axis=0)


def unpack(p, rows, cols):
    if not packs(rows, cols):
        return p[:, : 2 * LANES], p[:, 2 * LANES :]
    tail = p[2 * rows :]
    rest = jnp.concatenate([tail[:, : LANES // 2], tail[:, LANES // 2 :]], axis=0)
    return jnp.concatenate([p[:rows], p[rows : 2 * rows]], axis=1), rest


def pack_kernel(index_ref, qkv_ref, first_ref, value_ref, all_ref):
    for j in range(3):
        all_ref[j] = pack(qkv_ref[j])
    first_ref[...] = all_ref[index_ref[2]]
    value_ref[...] = all_ref[2]


def pack_proj_kernel(proj_ref, out_ref):
    out_ref[...] = pack(proj_ref[...])


def norm_kernel(index_ref, patches_ref, gain_ref, hidden_ref, own_ref):
    rows = patches_ref.shape[0]
    x = patches_ref[...]
    xf = x.astype(F32)
    mean_sq = jnp.mean(xf * xf, axis=-1, keepdims=True)
    gain = gain_ref[...].reshape(1, -1)
    hidden_ref[...] = (xf * lax.rsqrt(mean_sq + 1e-06) * gain).astype(BF16)
    step = 256
    pick = step // 4
    row = lax.broadcasted_iota(jnp.int32, (pick, step), 0)
    col = lax.broadcasted_iota(jnp.int32, (pick, step), 1)
    chosen = one_hot(col == 4 * row + index_ref[1])
    for i in range(rows // step):
        own_ref[i * pick : (i + 1) * pick, :] = jnp.dot(
            chosen, x[i * step : (i + 1) * step], preferred_element_type=F32
        ).astype(BF16)


def attend(index_ref, hidden_ref, valid_ref, w_ref, out_refs, q_ref, k_ref, v_ref, mix_ref):
    rows, width = q_ref.shape
    heads = width // HD
    main = 2 * LANES
    rest = width - main
    qkv = jnp.dot(hidden_ref[...], w_ref[...], preferred_element_type=F32)
    for j, ref in enumerate((q_ref, k_ref, v_ref)):
        ref[:, :main] = qkv[:, j * main : (j + 1) * main].astype(BF16)
        at = 3 * main + j * rest
        ref[:, main:] = qkv[:, at : at + rest].astype(BF16)
    lane = lax.broadcasted_iota(jnp.int32, (1, width), 1)
    head_masks = [one_hot((lane >= h * HD) & (lane < (h + 1) * HD)) for h in range(heads)]
    q_win = lax.broadcasted_iota(jnp.int32, (PAIR, PAIR), 0) // WIN
    k_win = lax.broadcasted_iota(jnp.int32, (PAIR, PAIR), 1) // WIN
    same = q_win == k_win
    floor = jnp.where(same, F32(-1e30), F32(-3e38))
    pick = PAIR // 4
    src = lax.broadcasted_iota(jnp.int32, (PAIR, PAIR), 1)
    dst = lax.broadcasted_iota(jnp.int32, (PAIR, PAIR), 0)
    order = one_hot(src == 4 * (dst % pick) + dst // pick)
    for p in range(rows // PAIR):
        at = p * PAIR
        q = q_ref[at : at + PAIR, :]
        k = k_ref[at : at + PAIR, :]
        v = v_ref[at : at + PAIR, :]
        k_all = jnp.concatenate([k * m for m in head_masks], axis=0)
        v_all = jnp.concatenate([v * m for m in head_masks], axis=0)
        scores = lax.dot_general(q, k_all, (((1,), (1,)), ((), ())), preferred_element_type=F32)
        live = valid_ref[p : p + 1, :] > 0
        weights = []
        for h in range(heads):
            s = scores[:, h * PAIR : (h + 1) * PAIR] * F32(HD ** (-0.5))
            s = jnp.where(same & live, s, floor)
            e = jnp.exp(s - jnp.max(s, axis=-1, keepdims=True))
            weights.append((e / jnp.sum(e, axis=-1, keepdims=True)).astype(BF16))
        w_all = jnp.concatenate(weights, axis=1)
        mixed = jnp.dot(w_all, v_all, preferred_element_type=F32).astype(BF16)
        mixed = jnp.dot(order, mixed, preferred_element_type=F32).astype(BF16)
        for t in range(4):
            mix_ref[t, p * pick : (p + 1) * pick, :] = mixed[t * pick : (t + 1) * pick]
    for s, out_ref in enumerate(out_refs):
        out_ref[...] = pack(mix_ref[index_ref[1] ^ s])


def attention_kernel(n_ctx, width, index_ref, hidden_ref, valid_ref, *refs):
    shards = list(refs[: 2 + 3 * (n_ctx - 2)])
    *out_refs, w_ref, q_ref, k_ref, v_ref, mix_ref = refs[len(shards) :]
    depth = w_ref.shape[0] // n_ctx
    me = index_ref[0]
    flip = index_ref[2] > 0
    main = 2 * LANES
    for key in range(n_ctx):
        rows = pl.ds(pl.multiple_of((me ^ key) * depth, depth), depth)
        if key < 2:
            block = shards.pop(0)
            thirds = [block[j] for j in range(3)]
        else:
            first, second, value = [shards.pop(0)[...] for _ in range(3)]
            thirds = [jnp.where(flip, second, first), jnp.where(flip, first, second), value]
        tails = []
        for j, third in enumerate(thirds):
            w_ref[rows, j * main : (j + 1) * main], tail = unpack(third, depth, width)
            tails.append(tail)
        w_ref[rows, 3 * main :] = jnp.concatenate(tails, axis=1)
    attend(index_ref, hidden_ref, valid_ref, w_ref, out_refs, q_ref, k_ref, v_ref, mix_ref)


def project_kernel(n_ctx, width, col, index_ref, *refs):
    *blocks, own_ref, gain_ref = refs[4 : -HALVES - 1]
    *out_refs, part_ref = refs[-HALVES - 1 :]
    rows = own_ref.shape[0]
    mixes = [unpack(m[...], rows, width) for m in refs[:4]]
    flip = index_ref[2] > 0
    mixes[2:] = [
        [jnp.where(flip, b, a) for a, b in zip(mixes[2], mixes[3])],
        [jnp.where(flip, a, b) for a, b in zip(mixes[2], mixes[3])],
    ]
    me = index_ref[0]
    main = 2 * LANES
    mixed = jnp.concatenate([m for m, _ in mixes] + [r for _, r in mixes], axis=1)
    mains = []
    rests = []
    for key in range(n_ctx):
        pieces = []
        for ref in [blocks.pop(0) for _ in range((4, 1)[key] if key < 2 else 2)]:
            pieces += [ref[...]] if len(ref.shape) == 2 else [ref[i] for i in range(ref.shape[0])]
        halves = [unpack(p, width, col) for p in pieces]
        both = []
        for half in ([h[0] for h in halves], [h[1] for h in halves]):
            both.append(jnp.concatenate([h[:main] for h in half] + [h[main:] for h in half], axis=0))
        mains.append(jnp.dot(mixed, both[0], preferred_element_type=F32))
        rests.append(both[1])
    if rests[0].shape[1]:
        rest = jnp.dot(mixed, jnp.concatenate(rests, axis=1), preferred_element_type=F32)
        count = rests[0].shape[1]
        mains = [
            jnp.concatenate([m, rest[:, key * count : (key + 1) * count]], axis=1)
            for key, m in enumerate(mains)
        ]
    for key in range(n_ctx):
        part_ref[me ^ key] = mains[key]
    total = jnp.concatenate([part_ref[i] for i in range(n_ctx)], axis=1)
    total = total + own_ref[...].astype(F32)
    mean_sq = jnp.mean(total * total, axis=-1, keepdims=True)
    normed = (total * lax.rsqrt(mean_sq + 1e-06) * gain_ref[...].reshape(1, -1)).astype(BF16)
    count = rows // HALVES
    for i, out_ref in enumerate(out_refs):
        out_ref[...] = normed[i * count : (i + 1) * count]


def place_kernel(n_ctx, index_ref, *refs):
    place_refs = refs[:n_ctx]
    row_refs = refs[n_ctx:-1]
    out_ref = refs[-1]
    spots = out_ref.shape[0]
    chosen = []
    for place_ref in place_refs:
        target = place_ref[...] - index_ref[0] * spots
        grid = lax.broadcasted_iota(jnp.int32, (spots, target.shape[1]), 0)
        chosen.append(one_hot(grid == target))
    out_ref[...] = jnp.dot(
        jnp.concatenate(chosen, axis=1),
        jnp.concatenate([ref[...] for ref in row_refs], axis=0),
        preferred_element_type=F32,
    ).astype(BF16)


def local(n_dp, n_ctx, n_ten, patches, valid, place, gain_attn, w_qkv, w_proj, gain_merge):
    rows, feat = patches.shape
    depth, _, width = w_qkv.shape
    col = w_proj.shape[1]
    groups = rows // 4
    ten = lax.axis_index("tensor")
    half = lax.axis_index("dp") % 2
    index = jnp.stack([lax.axis_index("context"), ten, half]).astype(jnp.int32)
    cross = list(cross_keys(n_ctx))

    def over_dp(x):
        return swap(x, "dp", n_dp, 1)

    def over_core(x):
        return swap(x, "context", n_ctx, 1)

    third = packed_shape(depth, width)
    piece = packed_shape(width, col)
    first, value, own = pl.pallas_call(
        pack_kernel,
        out_shape=(shape(*third), shape(*third), shape(3, *third)),
        in_specs=[SMEM, VMEM],
        out_specs=(VMEM,) * 3,
        compiler_params=params(8),
        name="pack",
    )(index, jnp.transpose(w_qkv, (1, 0, 2)))
    w_proj = pl.pallas_call(
        pack_proj_kernel,
        out_shape=shape(*piece),
        in_specs=[VMEM],
        out_specs=VMEM,
        compiler_params=params(8),
        name="pack_proj",
    )(w_proj)
    first = gather_cross(first, n_ctx)
    value = gather_cross(value, n_ctx)
    twin = over_core(own)
    far = lax.ppermute(
        w_proj,
        ("dp", "tensor"),
        [
            (d * n_ten + t, d * n_ten + (t ^ (2 + d % 2)))
            for d in range(n_dp)
            for t in range(n_ten)
        ],
    )
    by_one = swap(w_proj, "tensor", n_ten, 1)
    first, twin, patches = together(first, twin, patches)

    second = {k: over_dp(first[k]) for k in cross}
    first_twin = {k: over_core(first[k]) for k in cross}
    hidden, own_patches = pl.pallas_call(
        norm_kernel,
        out_shape=(shape(rows, feat), shape(groups, feat)),
        in_specs=[SMEM, VMEM, VMEM],
        out_specs=(VMEM, VMEM),
        compiler_params=params(16),
        name="norm",
    )(index, patches, gain_attn)
    by_one, hidden = together(by_one, hidden)
    low = gather_cross(jnp.stack([w_proj, by_one]), n_ctx)
    second, value, first_twin, hidden = together(second, value, first_twin, hidden)

    second_twin = {k: over_core(second[k]) for k in cross}
    value_twin = {k: over_core(value[k]) for k in cross}
    far, *_ = together(far, *second.values())
    far2 = over_dp(far)

    shard_list = [own, twin]
    for k in cross:
        shard_list += [first[k], second[k], value[k], first_twin[k], second_twin[k], value_twin[k]]

    mix_shapes = (shape(*packed_shape(groups, width)),) * n_ten
    mixed = pl.pallas_call(
        functools.partial(attention_kernel, n_ctx, width),
        out_shape=mix_shapes,
        in_specs=[SMEM] + [VMEM] * (2 + len(shard_list)),
        out_specs=(VMEM,) * n_ten,
        scratch_shapes=[pltpu.VMEM((feat, 3 * width), BF16)]
        + [pltpu.VMEM((rows, width), BF16)] * 3
        + [pltpu.VMEM((4, groups, width), BF16)],
        compiler_params=params(20),
        name="attention",
    )(index, hidden, valid.reshape(rows // PAIR, PAIR), *shard_list)

    mixed, far, far2, low = together(mixed, far, far2, low)
    received = {s: swap(mixed[s], "tensor", n_ten, s) for s in (2, 3, 1)}
    mixed = [mixed[0]] + [received[s] for s in range(1, n_ten)]
    high = gather_cross(jnp.stack([far, far2]), n_ctx)
    blocks = [w_proj, by_one, far, far2, over_core(jnp.stack([w_proj, by_one, far, far2]))]
    low_twin = {k: over_core(low[k]) for k in cross}
    mixed, high, place = together(mixed, high, place)
    places = gather_cross(place.reshape(1, groups), n_ctx)
    for k in cross:
        blocks += [low[k], high[k], low_twin[k], over_core(high[k])]
    done = pl.pallas_call(
        functools.partial(project_kernel, n_ctx, width, col),
        out_shape=(shape(groups // HALVES, feat),) * HALVES,
        in_specs=[SMEM] + [VMEM] * (n_ten + len(blocks) + 2),
        out_specs=(VMEM,) * HALVES,
        scratch_shapes=[pltpu.VMEM((n_ctx, groups, col), F32)],
        compiler_params=params(24),
        name="project",
    )(index, *mixed, *blocks, own_patches, gain_merge)

    done, place_group = together(done, jnp.stack([places[k] for k in (0, *cross)]))
    gathered = []
    for r in range(HALVES):
        crossed = gather_cross(done[r], n_ctx)
        if r == 0:
            place_twin = over_core(place_group)
        else:
            for k in cross:
                crossed[k], gathered[r - 1][k ^ 1], place_twin = together(
                    crossed[k], gathered[r - 1][k ^ 1], place_twin
                )
        for k in list(crossed):
            crossed[k ^ 1] = over_core(crossed[k])
        gathered.append(crossed)
    place_list = []
    for i, k in enumerate((0, *cross)):
        place_list += [places[k], place_twin[i]]
    return pl.pallas_call(
        functools.partial(place_kernel, n_ctx),
        out_shape=shape(groups, feat),
        in_specs=[SMEM] + [VMEM] * (n_ctx + n_ctx * HALVES),
        out_specs=VMEM,
        compiler_params=params(28),
        name="placement",
    )(index, *place_list, *[gathered[r][k] for k in range(n_ctx) for r in range(HALVES)])


def solution(mesh):
    in_specs = (
        P(("dp", "context"), None),
        P(("dp", "context")),
        P(("dp", "context")),
        P(),
        P("context", None, "tensor"),
        P("tensor", "context"),
        P(),
    )
    out_specs = P(("dp", "context"), "tensor")
    sizes = [mesh.shape[name] for name in ("dp", "context", "tensor")]
    body = functools.partial(local, *sizes)
    return jax.shard_map(body, mesh=mesh, in_specs=in_specs, out_specs=out_specs, check_vma=False)
```

```python
import functools

import jax
import jax.numpy as jnp
from jax import lax
from jax.experimental import pallas as pl
from jax.experimental.pallas import tpu as pltpu
from jax.sharding import PartitionSpec as P

HD = 80
WIN = 64
PAIR = 2 * WIN
LANES = 128
HALVES = 2
F32 = jnp.float32
BF16 = jnp.bfloat16
VMEM = pl.BlockSpec(memory_space=pltpu.VMEM)
SMEM = pl.BlockSpec(memory_space=pltpu.SMEM)


def params(mib):
    return pltpu.CompilerParams(vmem_limit_bytes=mib * 1024 * 1024)


def cost(us):
    return pl.CostEstimate(flops=0, bytes_accessed=int(us * 3.3e6), transcendentals=0)


def swap(x, axis, size, bit):
    return lax.ppermute(x, axis, [(i, i ^ bit) for i in range(size)])


def cross_keys(size):
    return range(2, size, 2)


def gather_cross(x, size):
    blocks = {0: x}
    bit = size // 2
    while bit > 1:
        for key in list(blocks):
            blocks[key ^ bit] = swap(blocks[key], "context", size, bit)
        bit //= 2
    return blocks


def gather_xor(x, size):
    blocks = gather_cross(x, size)
    for key in list(blocks):
        blocks[key ^ 1] = swap(blocks[key], "context", size, 1)
    return blocks


def together(*values):
    return lax.optimization_barrier(values)


def one_hot(mask):
    return mask.astype(F32).astype(BF16)


def shape(*dims):
    return jax.ShapeDtypeStruct(dims, BF16)


def packs(rows, cols):
    return rows % 32 == 0 and cols == 2 * LANES + LANES // 2


def packed_shape(rows, cols):
    return (rows * 5 // 2, LANES) if packs(rows, cols) else (rows, cols)


def pack(x):
    rows, cols = x.shape
    if not packs(rows, cols):
        return x
    rest = x[:, 2 * LANES :]
    tail = jnp.concatenate([rest[: rows // 2], rest[rows // 2 :]], axis=1)
    return jnp.concatenate([x[:, :LANES], x[:, LANES : 2 * LANES], tail], axis=0)


def unpack(p, rows, cols):
    if not packs(rows, cols):
        return p[:, : 2 * LANES], p[:, 2 * LANES :]
    tail = p[2 * rows :]
    rest = jnp.concatenate([tail[:, : LANES // 2], tail[:, LANES // 2 :]], axis=0)
    return jnp.concatenate([p[:rows], p[rows : 2 * rows]], axis=1), rest


def pack_kernel(index_ref, qkv_ref, first_ref, value_ref, all_ref):
    for j in range(3):
        all_ref[j] = pack(qkv_ref[j])
    first_ref[...] = all_ref[index_ref[2]]
    value_ref[...] = all_ref[2]


def pack_proj_kernel(proj_ref, out_ref):
    out_ref[...] = pack(proj_ref[...])


def norm_kernel(index_ref, patches_ref, gain_ref, hidden_ref, own_ref):
    rows = patches_ref.shape[0]
    x = patches_ref[...]
    xf = x.astype(F32)
    mean_sq = jnp.mean(xf * xf, axis=-1, keepdims=True)
    gain = gain_ref[...].reshape(1, -1)
    hidden_ref[...] = (xf * lax.rsqrt(mean_sq + 1e-06) * gain).astype(BF16)
    step = 256
    pick = step // 4
    row = lax.broadcasted_iota(jnp.int32, (pick, step), 0)
    col = lax.broadcasted_iota(jnp.int32, (pick, step), 1)
    chosen = one_hot(col == 4 * row + index_ref[1])
    for i in range(rows // step):
        own_ref[i * pick : (i + 1) * pick, :] = jnp.dot(
            chosen, x[i * step : (i + 1) * step], preferred_element_type=F32
        ).astype(BF16)


def attend(row0, index_ref, hidden_ref, valid_ref, w_ref, out_refs, q_ref, k_ref, v_ref, mix_ref):
    rows, width = q_ref.shape
    heads = width // HD
    main = 2 * LANES
    rest = width - main
    qkv = jnp.dot(hidden_ref[row0 : row0 + rows, :], w_ref[...], preferred_element_type=F32)
    for j, ref in enumerate((q_ref, k_ref, v_ref)):
        ref[:, :main] = qkv[:, j * main : (j + 1) * main].astype(BF16)
        at = 3 * main + j * rest
        ref[:, main:] = qkv[:, at : at + rest].astype(BF16)
    lane = lax.broadcasted_iota(jnp.int32, (1, width), 1)
    head_masks = [one_hot((lane >= h * HD) & (lane < (h + 1) * HD)) for h in range(heads)]
    q_win = lax.broadcasted_iota(jnp.int32, (PAIR, PAIR), 0) // WIN
    k_win = lax.broadcasted_iota(jnp.int32, (PAIR, PAIR), 1) // WIN
    same = q_win == k_win
    floor = jnp.where(same, F32(-1e30), F32(-3e38))
    pick = PAIR // 4
    src = lax.broadcasted_iota(jnp.int32, (PAIR, PAIR), 1)
    dst = lax.broadcasted_iota(jnp.int32, (PAIR, PAIR), 0)
    order = one_hot(src == 4 * (dst % pick) + dst // pick)
    for p in range(rows // PAIR):
        at = p * PAIR
        q = q_ref[at : at + PAIR, :]
        k = k_ref[at : at + PAIR, :]
        v = v_ref[at : at + PAIR, :]
        k_all = jnp.concatenate([k * m for m in head_masks], axis=0)
        v_all = jnp.concatenate([v * m for m in head_masks], axis=0)
        scores = lax.dot_general(q, k_all, (((1,), (1,)), ((), ())), preferred_element_type=F32)
        live = valid_ref[row0 // PAIR + p : row0 // PAIR + p + 1, :] > 0
        weights = []
        for h in range(heads):
            s = scores[:, h * PAIR : (h + 1) * PAIR] * F32(HD ** (-0.5))
            s = jnp.where(same & live, s, floor)
            e = jnp.exp(s - jnp.max(s, axis=-1, keepdims=True))
            weights.append((e / jnp.sum(e, axis=-1, keepdims=True)).astype(BF16))
        w_all = jnp.concatenate(weights, axis=1)
        mixed = jnp.dot(w_all, v_all, preferred_element_type=F32).astype(BF16)
        mixed = jnp.dot(order, mixed, preferred_element_type=F32).astype(BF16)
        for t in range(4):
            mix_ref[t, p * pick : (p + 1) * pick, :] = mixed[t * pick : (t + 1) * pick]
    for s, out_ref in enumerate(out_refs):
        out_ref[...] = pack(mix_ref[index_ref[1] ^ s])


def first_attention_kernel(n_ctx, width, index_ref, hidden_ref, valid_ref, *refs):
    shards = list(refs[: 2 + 3 * (n_ctx - 2)])
    *out_refs, w_ref, q_ref, k_ref, v_ref, mix_ref = refs[len(shards) :]
    depth = w_ref.shape[0] // n_ctx
    me = index_ref[0]
    flip = index_ref[2] > 0
    main = 2 * LANES
    for key in range(n_ctx):
        rows = pl.ds(pl.multiple_of((me ^ key) * depth, depth), depth)
        if key < 2:
            block = shards.pop(0)
            thirds = [block[j] for j in range(3)]
        else:
            first, second, value = [shards.pop(0)[...] for _ in range(3)]
            thirds = [jnp.where(flip, second, first), jnp.where(flip, first, second), value]
        tails = []
        for j, third in enumerate(thirds):
            w_ref[rows, j * main : (j + 1) * main], tail = unpack(third, depth, width)
            tails.append(tail)
        w_ref[rows, 3 * main :] = jnp.concatenate(tails, axis=1)
    attend(0, index_ref, hidden_ref, valid_ref, w_ref, out_refs, q_ref, k_ref, v_ref, mix_ref)


def next_attention_kernel(row0, index_ref, hidden_ref, valid_ref, w_ref, before_ref, *refs):
    *out_refs, q_ref, k_ref, v_ref, mix_ref = refs
    out_refs[1][0] = before_ref[...]
    out_refs[1] = out_refs[1].at[1]
    attend(row0, index_ref, hidden_ref, valid_ref, w_ref, out_refs, q_ref, k_ref, v_ref, mix_ref)


def project_kernel(n_ctx, width, col, index_ref, *refs):
    *blocks, own_ref, gain_ref = refs[7 : -HALVES - 1]
    *out_refs, part_ref = refs[-HALVES - 1 :]
    rows = own_ref.shape[0]
    halves = [refs[0][...], refs[1][...], refs[2][0], refs[2][1]] + [ref[...] for ref in refs[3:7]]
    halves = [unpack(half, rows // 2, width) for half in halves]
    mixes = [
        [jnp.concatenate([a, b], axis=0) for a, b in zip(halves[2 * s], halves[2 * s + 1])]
        for s in range(4)
    ]
    flip = index_ref[2] > 0
    mixes[2:] = [
        [jnp.where(flip, b, a) for a, b in zip(mixes[2], mixes[3])],
        [jnp.where(flip, a, b) for a, b in zip(mixes[2], mixes[3])],
    ]
    me = index_ref[0]
    main = 2 * LANES
    mixed = jnp.concatenate([m for m, _ in mixes] + [r for _, r in mixes], axis=1)
    mains = []
    rests = []
    for key in range(n_ctx):
        pieces = []
        for ref in [blocks.pop(0) for _ in range((4, 1)[key] if key < 2 else 2)]:
            pieces += [ref[...]] if len(ref.shape) == 2 else [ref[i] for i in range(ref.shape[0])]
        halves = [unpack(p, width, col) for p in pieces]
        both = []
        for half in ([h[0] for h in halves], [h[1] for h in halves]):
            both.append(jnp.concatenate([h[:main] for h in half] + [h[main:] for h in half], axis=0))
        mains.append(jnp.dot(mixed, both[0], preferred_element_type=F32))
        rests.append(both[1])
    if rests[0].shape[1]:
        rest = jnp.dot(mixed, jnp.concatenate(rests, axis=1), preferred_element_type=F32)
        count = rests[0].shape[1]
        mains = [
            jnp.concatenate([m, rest[:, key * count : (key + 1) * count]], axis=1)
            for key, m in enumerate(mains)
        ]
    for key in range(n_ctx):
        part_ref[me ^ key] = mains[key]
    total = jnp.concatenate([part_ref[i] for i in range(n_ctx)], axis=1)
    total = total + own_ref[...].astype(F32)
    mean_sq = jnp.mean(total * total, axis=-1, keepdims=True)
    normed = (total * lax.rsqrt(mean_sq + 1e-06) * gain_ref[...].reshape(1, -1)).astype(BF16)
    count = rows // HALVES
    for i, out_ref in enumerate(out_refs):
        out_ref[...] = normed[i * count : (i + 1) * count]


def place_kernel(n_ctx, index_ref, *refs):
    place_refs = refs[:n_ctx]
    row_refs = refs[n_ctx:-1]
    out_ref = refs[-1]
    spots = out_ref.shape[0]
    chosen = []
    for place_ref in place_refs:
        target = place_ref[...] - index_ref[0] * spots
        grid = lax.broadcasted_iota(jnp.int32, (spots, target.shape[1]), 0)
        chosen.append(one_hot(grid == target))
    out_ref[...] = jnp.dot(
        jnp.concatenate(chosen, axis=1),
        jnp.concatenate([ref[...] for ref in row_refs], axis=0),
        preferred_element_type=F32,
    ).astype(BF16)


def local(n_dp, n_ctx, n_ten, patches, valid, place, gain_attn, w_qkv, w_proj, gain_merge):
    rows, feat = patches.shape
    depth, _, width = w_qkv.shape
    col = w_proj.shape[1]
    groups = rows // 4
    ten = lax.axis_index("tensor")
    half = lax.axis_index("dp") % 2
    index = jnp.stack([lax.axis_index("context"), ten, half]).astype(jnp.int32)
    cross = list(cross_keys(n_ctx))

    def over_dp(x):
        return swap(x, "dp", n_dp, 1)

    def over_core(x):
        return swap(x, "context", n_ctx, 1)

    third = packed_shape(depth, width)
    piece = packed_shape(width, col)
    first, value, own = pl.pallas_call(
        pack_kernel,
        out_shape=(shape(*third), shape(*third), shape(3, *third)),
        in_specs=[SMEM, VMEM],
        out_specs=(VMEM,) * 3,
        compiler_params=params(8),
        name="pack",
    )(index, jnp.transpose(w_qkv, (1, 0, 2)))
    w_proj = pl.pallas_call(
        pack_proj_kernel,
        out_shape=shape(*piece),
        in_specs=[VMEM],
        out_specs=VMEM,
        compiler_params=params(8),
        name="pack_proj",
    )(w_proj)
    first = gather_cross(first, n_ctx)
    value = gather_cross(value, n_ctx)
    twin = over_core(own)
    far = lax.ppermute(
        w_proj,
        ("dp", "tensor"),
        [
            (d * n_ten + t, d * n_ten + (t ^ (2 + d % 2)))
            for d in range(n_dp)
            for t in range(n_ten)
        ],
    )
    by_one = swap(w_proj, "tensor", n_ten, 1)
    first, twin, patches = together(first, twin, patches)

    second = {k: over_dp(first[k]) for k in cross}
    first_twin = {k: over_core(first[k]) for k in cross}
    hidden, own_patches = pl.pallas_call(
        norm_kernel,
        out_shape=(shape(rows, feat), shape(groups, feat)),
        in_specs=[SMEM, VMEM, VMEM],
        out_specs=(VMEM, VMEM),
        compiler_params=params(16),
        name="norm",
    )(index, patches, gain_attn)
    by_one, hidden = together(by_one, hidden)
    low = gather_cross(jnp.stack([w_proj, by_one]), n_ctx)
    second, value, first_twin, hidden = together(second, value, first_twin, hidden)

    second_twin = {k: over_core(second[k]) for k in cross}
    value_twin = {k: over_core(value[k]) for k in cross}
    far, *_ = together(far, *second.values())
    far2 = over_dp(far)

    shard_list = [own, twin]
    for k in cross:
        shard_list += [first[k], second[k], value[k], first_twin[k], second_twin[k], value_twin[k]]

    valid_pairs = valid.reshape(rows // PAIR, PAIR)
    part = rows // HALVES
    mix_shape = shape(*packed_shape(part // 4, width))
    scratch = [pltpu.VMEM((part, width), BF16)] * 3 + [pltpu.VMEM((4, part // 4, width), BF16)]
    *mixed, w_full = pl.pallas_call(
        functools.partial(first_attention_kernel, n_ctx, width),
        out_shape=(mix_shape,) * n_ten + (shape(feat, 3 * width),),
        in_specs=[SMEM] + [VMEM] * (2 + len(shard_list)),
        out_specs=(VMEM,) * (n_ten + 1),
        scratch_shapes=scratch,
        compiler_params=params(16),
        name="attention0",
    )(index, hidden, valid_pairs, *shard_list)

    mixed, far, far2, low = together(mixed, far, far2, low)
    early = [swap(mixed[s], "tensor", n_ten, s) for s in (2, 3)]
    later = pl.pallas_call(
        functools.partial(next_attention_kernel, part),
        out_shape=(mix_shape, shape(2, *mix_shape.shape), mix_shape, mix_shape),
        in_specs=[SMEM] + [VMEM] * 4,
        out_specs=(VMEM,) * n_ten,
        scratch_shapes=scratch,
        compiler_params=params(16),
        cost_estimate=cost(1000),
        name="attention1",
    )(index, hidden, valid_pairs, w_full, mixed[1])
    high = gather_cross(jnp.stack([far, far2]), n_ctx)
    own_twin = over_core(jnp.stack([w_proj, by_one, far, far2]))
    later, early, own_twin = together(later, early, own_twin)
    late = [swap(later[s], "tensor", n_ten, s) for s in (2, 3)]
    mixed = [mixed[0], later[0], swap(later[1], "tensor", n_ten, 1)]
    mixed += [early[0], late[0], early[1], late[1]]
    blocks = [w_proj, by_one, far, far2, own_twin]
    low_twin = {k: over_core(low[k]) for k in cross}
    mixed, high, place = together(mixed, high, place)
    places = gather_cross(place.reshape(1, groups), n_ctx)
    for k in cross:
        blocks += [low[k], high[k], low_twin[k], over_core(high[k])]
    done = pl.pallas_call(
        functools.partial(project_kernel, n_ctx, width, col),
        out_shape=(shape(groups // HALVES, feat),) * HALVES,
        in_specs=[SMEM] + [VMEM] * (len(mixed) + len(blocks) + 2),
        out_specs=(VMEM,) * HALVES,
        scratch_shapes=[pltpu.VMEM((n_ctx, groups, col), F32)],
        compiler_params=params(24),
        name="project",
    )(index, *mixed, *blocks, own_patches, gain_merge)

    done, place_group = together(done, jnp.stack([places[k] for k in (0, *cross)]))
    gathered = []
    for r in range(HALVES):
        crossed = gather_cross(done[r], n_ctx)
        if r == 0:
            place_twin = over_core(place_group)
        else:
            for k in cross:
                crossed[k], gathered[r - 1][k ^ 1], place_twin = together(
                    crossed[k], gathered[r - 1][k ^ 1], place_twin
                )
        for k in list(crossed):
            crossed[k ^ 1] = over_core(crossed[k])
        gathered.append(crossed)
    place_list = []
    for i, k in enumerate((0, *cross)):
        place_list += [places[k], place_twin[i]]
    return pl.pallas_call(
        functools.partial(place_kernel, n_ctx),
        out_shape=shape(groups, feat),
        in_specs=[SMEM] + [VMEM] * (n_ctx + n_ctx * HALVES),
        out_specs=VMEM,
        compiler_params=params(28),
        name="placement",
    )(index, *place_list, *[gathered[r][k] for k in range(n_ctx) for r in range(HALVES)])


def solution(mesh):
    in_specs = (
        P(("dp", "context"), None),
        P(("dp", "context")),
        P(("dp", "context")),
        P(),
        P("context", None, "tensor"),
        P("tensor", "context"),
        P(),
    )
    out_specs = P(("dp", "context"), "tensor")
    sizes = [mesh.shape[name] for name in ("dp", "context", "tensor")]
    body = functools.partial(local, *sizes)
    return jax.shard_map(body, mesh=mesh, in_specs=in_specs, out_specs=out_specs, check_vma=False)
```

```python
import functools
import math

import jax
import jax.numpy as jnp
from jax import lax
from jax.experimental import pallas as pl
from jax.experimental.pallas import tpu as pltpu
from jax.sharding import PartitionSpec as P

HD = 80
WIN = 64
PAIR = 2 * WIN
LANES = 128
F32 = jnp.float32
BF16 = jnp.bfloat16
VMEM = pl.BlockSpec(memory_space=pltpu.VMEM)
SMEM = pl.BlockSpec(memory_space=pltpu.SMEM)


def params(mib):
    return pltpu.CompilerParams(vmem_limit_bytes=mib * 1024 * 1024)


def swap(x, axis, size, bit):
    return lax.ppermute(x, axis, [(i, i ^ bit) for i in range(size)])


def cross_keys(size):
    return range(2, size, 2)


def gather_cross(x, size):
    blocks = {0: x}
    bit = size // 2
    while bit > 1:
        for key in list(blocks):
            blocks[key ^ bit] = swap(blocks[key], "context", size, bit)
        bit //= 2
    return blocks


def gather_xor(x, size):
    blocks = gather_cross(x, size)
    for key in list(blocks):
        blocks[key ^ 1] = swap(blocks[key], "context", size, 1)
    return blocks


def together(*values):
    return lax.optimization_barrier(values)


def one_hot(mask):
    return mask.astype(F32).astype(BF16)


def shape(*dims):
    return jax.ShapeDtypeStruct(dims, BF16)


def packs(rows, cols):
    return rows % 32 == 0 and cols == 2 * LANES + LANES // 2


def packed_shape(rows, cols):
    return (rows * 5 // 2, LANES) if packs(rows, cols) else (rows, cols)


def pack(x):
    rows, cols = x.shape
    if not packs(rows, cols):
        return x
    rest = x[:, 2 * LANES :]
    tail = jnp.concatenate([rest[: rows // 2], rest[rows // 2 :]], axis=1)
    return jnp.concatenate([x[:, :LANES], x[:, LANES : 2 * LANES], tail], axis=0)


def unpack(p, rows, cols):
    if not packs(rows, cols):
        return p[:, : 2 * LANES], p[:, 2 * LANES :]
    tail = p[2 * rows :]
    rest = jnp.concatenate([tail[:, : LANES // 2], tail[:, LANES // 2 :]], axis=0)
    return jnp.concatenate([p[:rows], p[rows : 2 * rows]], axis=1), rest


def pack_kernel(index_ref, qkv_ref, first_ref, value_ref, all_ref):
    for j in range(3):
        all_ref[j] = pack(qkv_ref[j])
    first_ref[...] = all_ref[index_ref[2]]
    value_ref[...] = all_ref[2]


def pack_proj_kernel(proj_ref, out_ref):
    out_ref[...] = pack(proj_ref[...])


def norm_kernel(index_ref, patches_ref, gain_ref, hidden_ref, own_ref):
    rows = patches_ref.shape[0]
    x = patches_ref[...]
    xf = x.astype(F32)
    mean_sq = jnp.mean(xf * xf, axis=-1, keepdims=True)
    gain = gain_ref[...].reshape(1, -1)
    hidden_ref[...] = (xf * lax.rsqrt(mean_sq + 1e-06) * gain).astype(BF16)
    step = 256
    pick = step // 4
    row = lax.broadcasted_iota(jnp.int32, (pick, step), 0)
    col = lax.broadcasted_iota(jnp.int32, (pick, step), 1)
    chosen = one_hot(col == 4 * row + index_ref[1])
    for i in range(rows // step):
        own_ref[i * pick : (i + 1) * pick, :] = jnp.dot(
            chosen, x[i * step : (i + 1) * step], preferred_element_type=F32
        ).astype(BF16)


def attend(index_ref, hidden_ref, valid_ref, w_ref, out_refs, q_ref, k_ref, v_ref, mix_ref):
    rows, width = q_ref.shape
    heads = width // HD
    main = 2 * LANES
    rest = width - main
    qkv = jnp.dot(hidden_ref[...], w_ref[...], preferred_element_type=F32)
    for j, ref in enumerate((q_ref, k_ref, v_ref)):
        ref[:, :main] = qkv[:, j * main : (j + 1) * main].astype(BF16)
        at = 3 * main + j * rest
        ref[:, main:] = qkv[:, at : at + rest].astype(BF16)
    q_win = lax.broadcasted_iota(jnp.int32, (PAIR, PAIR), 1) // WIN
    k_win = lax.broadcasted_iota(jnp.int32, (PAIR, PAIR), 0) // WIN
    same = q_win == k_win
    floor = jnp.where(same, F32(-1e30), F32(-3e38))
    pick = PAIR // 4
    src = lax.broadcasted_iota(jnp.int32, (PAIR, PAIR), 1)
    dst = lax.broadcasted_iota(jnp.int32, (PAIR, PAIR), 0)
    order = one_hot(src == 4 * (dst % pick) + dst // pick)
    zero = jnp.zeros((HD, PAIR), BF16)
    factor = F32(HD ** (-0.5) * math.log2(math.e))
    for p in range(rows // PAIR):
        at = p * PAIR
        q_turned = q_ref[at : at + PAIR, :].T
        v_turned = v_ref[at : at + PAIR, :].T
        q_all = jnp.concatenate(
            [
                jnp.concatenate(
                    [q_turned[h * HD : (h + 1) * HD] if i == h else zero for i in range(heads)], axis=1
                )
                for h in range(heads)
            ],
            axis=0,
        )
        scores = jnp.dot(k_ref[at : at + PAIR, :], q_all, preferred_element_type=F32)
        live = jnp.broadcast_to(valid_ref[p : p + 1, :].astype(F32), (PAIR, PAIR)).T > 0
        bias = jnp.where(same & live, F32(0), floor)
        mixed = []
        for h in range(heads):
            s = scores[:, h * PAIR : (h + 1) * PAIR] + bias
            e = jnp.exp2((s - jnp.max(s, axis=0, keepdims=True)) * factor)
            weights = (e * (1.0 / jnp.sum(e, axis=0, keepdims=True))).astype(BF16)
            mixed.append(
                jnp.dot(v_turned[h * HD : (h + 1) * HD], weights, preferred_element_type=F32)
            )
        mixed = jnp.concatenate(mixed, axis=0).astype(BF16)
        mixed = lax.dot_general(
            order, mixed, (((1,), (1,)), ((), ())), preferred_element_type=F32
        ).astype(BF16)
        for t in range(4):
            mix_ref[t, p * pick : (p + 1) * pick, :] = mixed[t * pick : (t + 1) * pick]
    for s, out_ref in enumerate(out_refs):
        out_ref[...] = pack(mix_ref[index_ref[1] ^ s])


def attention_kernel(n_ctx, width, index_ref, hidden_ref, valid_ref, *refs):
    shards = list(refs[: 2 + 3 * (n_ctx - 2)])
    *out_refs, w_ref, q_ref, k_ref, v_ref, mix_ref = refs[len(shards) :]
    depth = w_ref.shape[0] // n_ctx
    me = index_ref[0]
    flip = index_ref[2] > 0
    main = 2 * LANES
    for key in range(n_ctx):
        rows = pl.ds(pl.multiple_of((me ^ key) * depth, depth), depth)
        if key < 2:
            block = shards.pop(0)
            thirds = [block[j] for j in range(3)]
        else:
            first, second, value = [shards.pop(0)[...] for _ in range(3)]
            thirds = [jnp.where(flip, second, first), jnp.where(flip, first, second), value]
        tails = []
        for j, third in enumerate(thirds):
            w_ref[rows, j * main : (j + 1) * main], tail = unpack(third, depth, width)
            tails.append(tail)
        w_ref[rows, 3 * main :] = jnp.concatenate(tails, axis=1)
    attend(index_ref, hidden_ref, valid_ref, w_ref, out_refs, q_ref, k_ref, v_ref, mix_ref)


def project_kernel(n_ctx, width, col, index_ref, *refs):
    *blocks, own_ref, gain_ref, out_ref, part_ref = refs[4:]
    rows = own_ref.shape[0]
    mixes = [unpack(m[...], rows, width) for m in refs[:4]]
    flip = index_ref[2] > 0
    mixes[2:] = [
        [jnp.where(flip, b, a) for a, b in zip(mixes[2], mixes[3])],
        [jnp.where(flip, a, b) for a, b in zip(mixes[2], mixes[3])],
    ]
    me = index_ref[0]
    main = 2 * LANES
    mixed = jnp.concatenate([m for m, _ in mixes] + [r for _, r in mixes], axis=1)
    mains = []
    rests = []
    for key in range(n_ctx):
        pieces = []
        for ref in [blocks.pop(0) for _ in range((4, 1)[key] if key < 2 else 2)]:
            pieces += [ref[...]] if len(ref.shape) == 2 else [ref[i] for i in range(ref.shape[0])]
        halves = [unpack(p, width, col) for p in pieces]
        both = []
        for half in ([h[0] for h in halves], [h[1] for h in halves]):
            both.append(jnp.concatenate([h[:main] for h in half] + [h[main:] for h in half], axis=0))
        mains.append(jnp.dot(mixed, both[0], preferred_element_type=F32))
        rests.append(both[1])
    if rests[0].shape[1]:
        rest = jnp.dot(mixed, jnp.concatenate(rests, axis=1), preferred_element_type=F32)
        count = rests[0].shape[1]
        mains = [
            jnp.concatenate([m, rest[:, key * count : (key + 1) * count]], axis=1)
            for key, m in enumerate(mains)
        ]
    for key in range(n_ctx):
        part_ref[me ^ key] = mains[key]
    total = jnp.concatenate([part_ref[i] for i in range(n_ctx)], axis=1)
    total = total + own_ref[...].astype(F32)
    mean_sq = jnp.mean(total * total, axis=-1, keepdims=True)
    gain = gain_ref[...].reshape(1, -1)
    out_ref[...] = (total * lax.rsqrt(mean_sq + 1e-06) * gain).astype(BF16)


def place_kernel(count, index_ref, *refs):
    place_refs = refs[:count]
    row_refs = refs[count : 2 * count]
    before = refs[2 * count : -1]
    out_ref = refs[-1]
    spots = out_ref.shape[0]
    chosen = []
    for place_ref in place_refs:
        target = place_ref[...] - index_ref[0] * spots
        grid = lax.broadcasted_iota(jnp.int32, (spots, target.shape[1]), 0)
        chosen.append(one_hot(grid == target))
    total = jnp.dot(
        jnp.concatenate(chosen, axis=1),
        jnp.concatenate([ref[...] for ref in row_refs], axis=0),
        preferred_element_type=F32,
    )
    for ref in before:
        total = total + ref[...]
    out_ref[...] = total.astype(out_ref.dtype)


def local(n_dp, n_ctx, n_ten, patches, valid, place, gain_attn, w_qkv, w_proj, gain_merge):
    rows, feat = patches.shape
    depth, _, width = w_qkv.shape
    col = w_proj.shape[1]
    groups = rows // 4
    ten = lax.axis_index("tensor")
    half = lax.axis_index("dp") % 2
    index = jnp.stack([lax.axis_index("context"), ten, half]).astype(jnp.int32)
    cross = list(cross_keys(n_ctx))

    def over_dp(x):
        return swap(x, "dp", n_dp, 1)

    def over_core(x):
        return swap(x, "context", n_ctx, 1)

    third = packed_shape(depth, width)
    piece = packed_shape(width, col)
    first, value, own = pl.pallas_call(
        pack_kernel,
        out_shape=(shape(*third), shape(*third), shape(3, *third)),
        in_specs=[SMEM, VMEM],
        out_specs=(VMEM,) * 3,
        compiler_params=params(8),
        name="pack",
    )(index, jnp.transpose(w_qkv, (1, 0, 2)))
    w_proj = pl.pallas_call(
        pack_proj_kernel,
        out_shape=shape(*piece),
        in_specs=[VMEM],
        out_specs=VMEM,
        compiler_params=params(8),
        name="pack_proj",
    )(w_proj)
    first = gather_cross(first, n_ctx)
    value = gather_cross(value, n_ctx)
    twin = over_core(own)
    far = lax.ppermute(
        w_proj,
        ("dp", "tensor"),
        [
            (d * n_ten + t, d * n_ten + (t ^ (2 + d % 2)))
            for d in range(n_dp)
            for t in range(n_ten)
        ],
    )
    by_one = swap(w_proj, "tensor", n_ten, 1)
    first, twin, patches = together(first, twin, patches)

    second = {k: over_dp(first[k]) for k in cross}
    first_twin = {k: over_core(first[k]) for k in cross}
    hidden, own_patches = pl.pallas_call(
        norm_kernel,
        out_shape=(shape(rows, feat), shape(groups, feat)),
        in_specs=[SMEM, VMEM, VMEM],
        out_specs=(VMEM, VMEM),
        compiler_params=params(16),
        name="norm",
    )(index, patches, gain_attn)
    by_one, hidden = together(by_one, hidden)
    low = gather_cross(jnp.stack([w_proj, by_one]), n_ctx)
    second, value, first_twin, hidden = together(second, value, first_twin, hidden)

    second_twin = {k: over_core(second[k]) for k in cross}
    value_twin = {k: over_core(value[k]) for k in cross}
    far, *_ = together(far, *second.values())
    far2 = over_dp(far)

    shard_list = [own, twin]
    for k in cross:
        shard_list += [first[k], second[k], value[k], first_twin[k], second_twin[k], value_twin[k]]

    mix_shapes = (shape(*packed_shape(groups, width)),) * n_ten
    mixed = pl.pallas_call(
        functools.partial(attention_kernel, n_ctx, width),
        out_shape=mix_shapes,
        in_specs=[SMEM] + [VMEM] * (2 + len(shard_list)),
        out_specs=(VMEM,) * n_ten,
        scratch_shapes=[pltpu.VMEM((feat, 3 * width), BF16)]
        + [pltpu.VMEM((rows, width), BF16)] * 3
        + [pltpu.VMEM((4, groups, width), BF16)],
        compiler_params=params(20),
        name="attention",
    )(index, hidden, valid.reshape(rows // PAIR, PAIR), *shard_list)

    mixed, far, far2, low = together(mixed, far, far2, low)
    received = {s: swap(mixed[s], "tensor", n_ten, s) for s in (2, 3, 1)}
    mixed = [mixed[0]] + [received[s] for s in range(1, n_ten)]
    high = gather_cross(jnp.stack([far, far2]), n_ctx)
    blocks = [w_proj, by_one, far, far2, over_core(jnp.stack([w_proj, by_one, far, far2]))]
    low_twin = {k: over_core(low[k]) for k in cross}
    mixed, high = together(mixed, high)
    for k in cross:
        blocks += [low[k], high[k], low_twin[k], over_core(high[k])]
    done = pl.pallas_call(
        functools.partial(project_kernel, n_ctx, width, col),
        out_shape=shape(groups, feat),
        in_specs=[SMEM] + [VMEM] * (n_ten + len(blocks) + 2),
        out_specs=VMEM,
        scratch_shapes=[pltpu.VMEM((n_ctx, groups, col), F32)],
        compiler_params=params(24),
        name="project",
    )(index, *mixed, *blocks, own_patches, gain_merge)

    crossed = gather_cross(done, n_ctx)
    near_rows = over_core(done)
    places = gather_cross(place.reshape(1, groups), n_ctx)
    place_twin = over_core(jnp.stack([places[k] for k in (0, *cross)]))

    def put(ids, rows_in, before, dtype, name):
        return pl.pallas_call(
            functools.partial(place_kernel, len(ids)),
            out_shape=jax.ShapeDtypeStruct((groups, feat), dtype),
            in_specs=[SMEM] + [VMEM] * (2 * len(ids) + len(before)),
            out_specs=VMEM,
            compiler_params=params(24),
            name=name,
        )(index, *ids, *rows_in, *before)

    total = put([places[0], place_twin[0]], [done, near_rows], [], F32, "placement0")
    for k in cross:
        crossed[k], total = together(crossed[k], total)
        crossed[k ^ 1] = over_core(crossed[k])
    ids = []
    for i, k in enumerate(cross):
        ids += [places[k], place_twin[1 + i]]
    return put(ids, [crossed[k] for k in range(2, n_ctx)], [total], BF16, "placement1")


def solution(mesh):
    in_specs = (
        P(("dp", "context"), None),
        P(("dp", "context")),
        P(("dp", "context")),
        P(),
        P("context", None, "tensor"),
        P("tensor", "context"),
        P(),
    )
    out_specs = P(("dp", "context"), "tensor")
    sizes = [mesh.shape[name] for name in ("dp", "context", "tensor")]
    body = functools.partial(local, *sizes)
    return jax.shard_map(body, mesh=mesh, in_specs=in_specs, out_specs=out_specs, check_vma=False)
```

```python
import functools
import math

import jax
import jax.numpy as jnp
from jax import lax
from jax.experimental import pallas as pl
from jax.experimental.pallas import tpu as pltpu
from jax.sharding import PartitionSpec as P

HD = 80
WIN = 64
PAIR = 2 * WIN
LANES = 128
F32 = jnp.float32
BF16 = jnp.bfloat16
VMEM = pl.BlockSpec(memory_space=pltpu.VMEM)
SMEM = pl.BlockSpec(memory_space=pltpu.SMEM)


def params(mib):
    return pltpu.CompilerParams(vmem_limit_bytes=mib * 1024 * 1024)


def swap(x, axis, size, bit):
    return lax.ppermute(x, axis, [(i, i ^ bit) for i in range(size)])


def cross_keys(size):
    return range(2, size, 2)


def gather_cross(x, size):
    blocks = {0: x}
    bit = size // 2
    while bit > 1:
        for key in list(blocks):
            blocks[key ^ bit] = swap(blocks[key], "context", size, bit)
        bit //= 2
    return blocks


def gather_xor(x, size):
    blocks = gather_cross(x, size)
    for key in list(blocks):
        blocks[key ^ 1] = swap(blocks[key], "context", size, 1)
    return blocks


def together(*values):
    return lax.optimization_barrier(values)


def one_hot(mask):
    return mask.astype(F32).astype(BF16)


def shape(*dims):
    return jax.ShapeDtypeStruct(dims, BF16)


def packs(rows, cols):
    return rows % 32 == 0 and cols == 2 * LANES + LANES // 2


def packed_shape(rows, cols):
    return (rows * 5 // 2, LANES) if packs(rows, cols) else (rows, cols)


def pack(x):
    rows, cols = x.shape
    if not packs(rows, cols):
        return x
    rest = x[:, 2 * LANES :]
    tail = jnp.concatenate([rest[: rows // 2], rest[rows // 2 :]], axis=1)
    return jnp.concatenate([x[:, :LANES], x[:, LANES : 2 * LANES], tail], axis=0)


def unpack(p, rows, cols):
    if not packs(rows, cols):
        return p[:rows, : 2 * LANES], p[:rows, 2 * LANES :]
    tail = p[2 * rows : 5 * rows // 2]
    rest = jnp.concatenate([tail[:, : LANES // 2], tail[:, LANES // 2 :]], axis=0)
    return jnp.concatenate([p[:rows], p[rows : 2 * rows]], axis=1), rest


NOTE = 16


def write_note(place, lanes):
    count = place.shape[1]
    filled = []
    for digit in (place >> 6, place & 63):
        for at in range(0, count, lanes):
            part = digit[:, at : at + lanes].astype(F32)
            spare = lanes - part.shape[1]
            filled.append(jnp.concatenate([part, jnp.zeros((1, spare), F32)], axis=1) if spare else part)
    filled.append(jnp.zeros((NOTE - len(filled), lanes), F32))
    return jnp.concatenate(filled, axis=0).astype(BF16)


def read_note(ref, count):
    note = ref[ref.shape[0] - NOTE :, :].astype(F32)
    lanes = note.shape[1]
    lines = -(-count // lanes)
    digits = []
    for d in range(2):
        parts = [
            note[d * lines + i : d * lines + i + 1, : min(lanes, count - i * lanes)]
            for i in range(lines)
        ]
        digits.append(parts[0] if lines == 1 else jnp.concatenate(parts, axis=1))
    return digits[0] * 64 + digits[1]


def pack_kernel(index_ref, qkv_ref, place_ref, first_ref, value_ref, all_ref):
    note = write_note(place_ref[...], all_ref.shape[2])
    count = all_ref.shape[1] - NOTE
    for j in range(3):
        all_ref[j, :count, :] = pack(qkv_ref[j])
        all_ref[j, count:, :] = note
    first_ref[...] = all_ref[index_ref[2]]
    value_ref[...] = all_ref[2]


def pack_proj_kernel(proj_ref, out_ref):
    out_ref[...] = pack(proj_ref[...])


def norm_kernel(index_ref, patches_ref, gain_ref, hidden_ref, own_ref):
    rows = patches_ref.shape[0]
    x = patches_ref[...]
    xf = x.astype(F32)
    mean_sq = jnp.mean(xf * xf, axis=-1, keepdims=True)
    gain = gain_ref[...].reshape(1, -1)
    hidden_ref[...] = (xf * lax.rsqrt(mean_sq + 1e-06) * gain).astype(BF16)
    step = 256
    pick = step // 4
    row = lax.broadcasted_iota(jnp.int32, (pick, step), 0)
    col = lax.broadcasted_iota(jnp.int32, (pick, step), 1)
    chosen = one_hot(col == 4 * row + index_ref[1])
    for i in range(rows // step):
        own_ref[i * pick : (i + 1) * pick, :] = jnp.dot(
            chosen, x[i * step : (i + 1) * step], preferred_element_type=F32
        ).astype(BF16)


def attend(index_ref, hidden_ref, valid_ref, w_ref, out_refs, q_ref, k_ref, v_ref, mix_ref):
    rows, width = q_ref.shape
    heads = width // HD
    main = 2 * LANES
    rest = width - main
    qkv = jnp.dot(hidden_ref[...], w_ref[...], preferred_element_type=F32)
    for j, ref in enumerate((q_ref, k_ref, v_ref)):
        ref[:, :main] = qkv[:, j * main : (j + 1) * main].astype(BF16)
        at = 3 * main + j * rest
        ref[:, main:] = qkv[:, at : at + rest].astype(BF16)
    q_win = lax.broadcasted_iota(jnp.int32, (PAIR, PAIR), 1) // WIN
    k_win = lax.broadcasted_iota(jnp.int32, (PAIR, PAIR), 0) // WIN
    same = q_win == k_win
    floor = jnp.where(same, F32(-1e30), F32(-3e38))
    pick = PAIR // 4
    src = lax.broadcasted_iota(jnp.int32, (PAIR, PAIR), 1)
    dst = lax.broadcasted_iota(jnp.int32, (PAIR, PAIR), 0)
    order = one_hot(src == 4 * (dst % pick) + dst // pick)
    zero = jnp.zeros((HD, PAIR), BF16)
    factor = F32(HD ** (-0.5) * math.log2(math.e))
    for p in range(rows // PAIR):
        at = p * PAIR
        q_turned = q_ref[at : at + PAIR, :].T
        v_turned = v_ref[at : at + PAIR, :].T
        q_all = jnp.concatenate(
            [
                jnp.concatenate(
                    [q_turned[h * HD : (h + 1) * HD] if i == h else zero for i in range(heads)], axis=1
                )
                for h in range(heads)
            ],
            axis=0,
        )
        scores = jnp.dot(k_ref[at : at + PAIR, :], q_all, preferred_element_type=F32)
        live = jnp.broadcast_to(valid_ref[p : p + 1, :].astype(F32), (PAIR, PAIR)).T > 0
        bias = jnp.where(same & live, F32(0), floor)
        mixed = []
        for h in range(heads):
            s = scores[:, h * PAIR : (h + 1) * PAIR] + bias
            e = jnp.exp2((s - jnp.max(s, axis=0, keepdims=True)) * factor)
            weights = (e * (1.0 / jnp.sum(e, axis=0, keepdims=True))).astype(BF16)
            mixed.append(
                jnp.dot(v_turned[h * HD : (h + 1) * HD], weights, preferred_element_type=F32)
            )
        mixed = jnp.concatenate(mixed, axis=0).astype(BF16)
        mixed = lax.dot_general(
            order, mixed, (((1,), (1,)), ((), ())), preferred_element_type=F32
        ).astype(BF16)
        for t in range(4):
            mix_ref[t, p * pick : (p + 1) * pick, :] = mixed[t * pick : (t + 1) * pick]
    for s, out_ref in enumerate(out_refs):
        out_ref[...] = pack(mix_ref[index_ref[1] ^ s])


def attention_kernel(n_ctx, width, index_ref, hidden_ref, valid_ref, *refs):
    shards = list(refs[: 2 + 3 * (n_ctx - 2)])
    *out_refs, w_ref, q_ref, k_ref, v_ref, mix_ref = refs[len(shards) :]
    depth = w_ref.shape[0] // n_ctx
    me = index_ref[0]
    flip = index_ref[2] > 0
    main = 2 * LANES
    for key in range(n_ctx):
        rows = pl.ds(pl.multiple_of((me ^ key) * depth, depth), depth)
        if key < 2:
            block = shards.pop(0)
            thirds = [block[j] for j in range(3)]
        else:
            first, second, value = [shards.pop(0)[...] for _ in range(3)]
            thirds = [jnp.where(flip, second, first), jnp.where(flip, first, second), value]
        tails = []
        for j, third in enumerate(thirds):
            w_ref[rows, j * main : (j + 1) * main], tail = unpack(third, depth, width)
            tails.append(tail)
        w_ref[rows, 3 * main :] = jnp.concatenate(tails, axis=1)
    attend(index_ref, hidden_ref, valid_ref, w_ref, out_refs, q_ref, k_ref, v_ref, mix_ref)


def project_kernel(n_ctx, width, col, index_ref, *refs):
    *blocks, own_ref, gain_ref, low_ref, high_ref, part_ref = refs[4:]
    rows = own_ref.shape[0]
    mixes = [unpack(m[...], rows, width) for m in refs[:4]]
    flip = index_ref[2] > 0
    mixes[2:] = [
        [jnp.where(flip, b, a) for a, b in zip(mixes[2], mixes[3])],
        [jnp.where(flip, a, b) for a, b in zip(mixes[2], mixes[3])],
    ]
    me = index_ref[0]
    main = 2 * LANES
    mixed = jnp.concatenate([m for m, _ in mixes] + [r for _, r in mixes], axis=1)
    mains = []
    rests = []
    for key in range(n_ctx):
        pieces = []
        for ref in [blocks.pop(0) for _ in range((4, 1)[key] if key < 2 else 2)]:
            pieces += [ref[...]] if len(ref.shape) == 2 else [ref[i] for i in range(ref.shape[0])]
        halves = [unpack(p, width, col) for p in pieces]
        both = []
        for half in ([h[0] for h in halves], [h[1] for h in halves]):
            both.append(jnp.concatenate([h[:main] for h in half] + [h[main:] for h in half], axis=0))
        mains.append(jnp.dot(mixed, both[0], preferred_element_type=F32))
        rests.append(both[1])
    if rests[0].shape[1]:
        rest = jnp.dot(mixed, jnp.concatenate(rests, axis=1), preferred_element_type=F32)
        count = rests[0].shape[1]
        mains = [
            jnp.concatenate([m, rest[:, key * count : (key + 1) * count]], axis=1)
            for key, m in enumerate(mains)
        ]
    for key in range(n_ctx):
        part_ref[me ^ key] = mains[key]
    total = jnp.concatenate([part_ref[i] for i in range(n_ctx)], axis=1)
    total = total + own_ref[...].astype(F32)
    mean_sq = jnp.mean(total * total, axis=-1, keepdims=True)
    gain = gain_ref[...].reshape(1, -1)
    normed = (total * lax.rsqrt(mean_sq + 1e-06) * gain).astype(BF16)
    half = low_ref.shape[0]
    low_ref[...] = normed[:half]
    high_ref[...] = normed[half:]


def place_kernel(count, index_ref, *refs):
    place_refs = refs[:count]
    row_refs = refs[count : 3 * count]
    before = refs[3 * count : -1]
    out_ref = refs[-1]
    spots = out_ref.shape[0]
    chosen = []
    base = (index_ref[0] * spots).astype(F32)
    for place_ref in place_refs:
        note_ref = place_ref.at[0] if len(place_ref.shape) == 3 else place_ref
        target = read_note(note_ref, spots) - base
        grid = lax.broadcasted_iota(jnp.int32, (spots, spots), 0).astype(F32)
        chosen.append(one_hot(grid == target))
    total = jnp.dot(
        jnp.concatenate(chosen, axis=1),
        jnp.concatenate([ref[...] for ref in row_refs], axis=0),
        preferred_element_type=F32,
    )
    for ref in before:
        total = total + ref[...].astype(F32)
    out_ref[...] = total.astype(out_ref.dtype)


def local(n_dp, n_ctx, n_ten, patches, valid, place, gain_attn, w_qkv, w_proj, gain_merge):
    rows, feat = patches.shape
    depth, _, width = w_qkv.shape
    col = w_proj.shape[1]
    groups = rows // 4
    ten = lax.axis_index("tensor")
    half = lax.axis_index("dp") % 2
    index = jnp.stack([lax.axis_index("context"), ten, half]).astype(jnp.int32)
    cross = list(cross_keys(n_ctx))

    def over_dp(x):
        return swap(x, "dp", n_dp, 1)

    def over_core(x):
        return swap(x, "context", n_ctx, 1)

    third = packed_shape(depth, width)
    third = (third[0] + NOTE, third[1])
    piece = packed_shape(width, col)
    first, value, own = pl.pallas_call(
        pack_kernel,
        out_shape=(shape(*third), shape(*third), shape(3, *third)),
        in_specs=[SMEM, VMEM, VMEM],
        out_specs=(VMEM,) * 3,
        compiler_params=params(8),
        name="pack",
    )(index, jnp.transpose(w_qkv, (1, 0, 2)), place.reshape(1, groups))
    w_proj = pl.pallas_call(
        pack_proj_kernel,
        out_shape=shape(*piece),
        in_specs=[VMEM],
        out_specs=VMEM,
        compiler_params=params(8),
        name="pack_proj",
    )(w_proj)
    first = gather_cross(first, n_ctx)
    value = gather_cross(value, n_ctx)
    twin = over_core(own)
    far = lax.ppermute(
        w_proj,
        ("dp", "tensor"),
        [
            (d * n_ten + t, d * n_ten + (t ^ (2 + d % 2)))
            for d in range(n_dp)
            for t in range(n_ten)
        ],
    )
    by_one = swap(w_proj, "tensor", n_ten, 1)
    first, twin, patches = together(first, twin, patches)

    second = {k: over_dp(first[k]) for k in cross}
    first_twin = {k: over_core(first[k]) for k in cross}
    hidden, own_patches = pl.pallas_call(
        norm_kernel,
        out_shape=(shape(rows, feat), shape(groups, feat)),
        in_specs=[SMEM, VMEM, VMEM],
        out_specs=(VMEM, VMEM),
        compiler_params=params(16),
        name="norm",
    )(index, patches, gain_attn)
    by_one, hidden = together(by_one, hidden)
    low = gather_cross(jnp.stack([w_proj, by_one]), n_ctx)
    second, value, first_twin, hidden = together(second, value, first_twin, hidden)

    second_twin = {k: over_core(second[k]) for k in cross}
    value_twin = {k: over_core(value[k]) for k in cross}
    far, *_ = together(far, *second.values())
    far2 = over_dp(far)

    shard_list = [own, twin]
    for k in cross:
        shard_list += [first[k], second[k], value[k], first_twin[k], second_twin[k], value_twin[k]]

    mix_shapes = (shape(*packed_shape(groups, width)),) * n_ten
    mixed = pl.pallas_call(
        functools.partial(attention_kernel, n_ctx, width),
        out_shape=mix_shapes,
        in_specs=[SMEM] + [VMEM] * (2 + len(shard_list)),
        out_specs=(VMEM,) * n_ten,
        scratch_shapes=[pltpu.VMEM((feat, 3 * width), BF16)]
        + [pltpu.VMEM((rows, width), BF16)] * 3
        + [pltpu.VMEM((4, groups, width), BF16)],
        compiler_params=params(20),
        name="attention",
    )(index, hidden, valid.reshape(rows // PAIR, PAIR), *shard_list)

    mixed, far, far2, low = together(list(mixed), far, far2, low)
    received = [mixed[0]] + [swap(mixed[s], "tensor", n_ten, s) for s in range(1, n_ten)]
    high = gather_cross(jnp.stack([far, far2]), n_ctx)
    blocks = [w_proj, by_one, far, far2, over_core(jnp.stack([w_proj, by_one, far, far2]))]
    low_twin = {k: over_core(low[k]) for k in cross}
    received, high = together(received, high)
    for k in cross:
        blocks += [low[k], high[k], low_twin[k], over_core(high[k])]
    done = pl.pallas_call(
        functools.partial(project_kernel, n_ctx, width, col),
        out_shape=(shape(groups // 2, feat),) * 2,
        in_specs=[SMEM] + [VMEM] * (n_ten + len(blocks) + 2),
        out_specs=(VMEM,) * 2,
        scratch_shapes=[pltpu.VMEM((n_ctx, groups, col), F32)],
        compiler_params=params(24),
        name="project",
    )(index, *received, *blocks, own_patches, gain_merge)

    crossed = [gather_cross(x, n_ctx) for x in done]
    near_rows = [over_core(x) for x in done]

    def put(ids, rows_in, before, name):
        return pl.pallas_call(
            functools.partial(place_kernel, len(ids)),
            out_shape=shape(groups, feat),
            in_specs=[SMEM] + [VMEM] * (3 * len(ids) + len(before)),
            out_specs=VMEM,
            compiler_params=params(24),
            name=name,
        )(index, *ids, *rows_in, *before)

    total = put([own, twin], [*done, *near_rows], [], "placement0")
    last = []
    for k in cross:
        crossed[0][k], crossed[1][k], total = together(crossed[0][k], crossed[1][k], total)
        twins = [over_core(x[k]) for x in crossed]
        last += [crossed[0][k], crossed[1][k], *twins]
    ids = []
    for k in cross:
        ids += [first[k], first_twin[k]]
    return put(ids, last, [total], "placement1")


def solution(mesh):
    in_specs = (
        P(("dp", "context"), None),
        P(("dp", "context")),
        P(("dp", "context")),
        P(),
        P("context", None, "tensor"),
        P("tensor", "context"),
        P(),
    )
    out_specs = P(("dp", "context"), "tensor")
    sizes = [mesh.shape[name] for name in ("dp", "context", "tensor")]
    body = functools.partial(local, *sizes)
    return jax.shard_map(body, mesh=mesh, in_specs=in_specs, out_specs=out_specs, check_vma=False)
```

```python
import functools
import math

import jax
import jax.numpy as jnp
from jax import lax
from jax.experimental import pallas as pl
from jax.experimental.pallas import tpu as pltpu
from jax.sharding import PartitionSpec as P

HD = 80
WIN = 64
PAIR = 2 * WIN
LANES = 128
F32 = jnp.float32
BF16 = jnp.bfloat16
VMEM = pl.BlockSpec(memory_space=pltpu.VMEM)
SMEM = pl.BlockSpec(memory_space=pltpu.SMEM)


def params(mib):
    return pltpu.CompilerParams(vmem_limit_bytes=mib * 1024 * 1024)


def swap(x, axis, size, bit):
    return lax.ppermute(x, axis, [(i, i ^ bit) for i in range(size)])


def cross_keys(size):
    return range(2, size, 2)


def gather_cross(x, size):
    blocks = {0: x}
    bit = size // 2
    while bit > 1:
        for key in list(blocks):
            blocks[key ^ bit] = swap(blocks[key], "context", size, bit)
        bit //= 2
    return blocks


def gather_xor(x, size):
    blocks = gather_cross(x, size)
    for key in list(blocks):
        blocks[key ^ 1] = swap(blocks[key], "context", size, 1)
    return blocks


def together(*values):
    return lax.optimization_barrier(values)


def one_hot(mask):
    return mask.astype(F32).astype(BF16)


def shape(*dims):
    return jax.ShapeDtypeStruct(dims, BF16)


def packs(rows, cols):
    return rows % 32 == 0 and cols == 2 * LANES + LANES // 2


def packed_shape(rows, cols):
    return (rows * 5 // 2, LANES) if packs(rows, cols) else (rows, cols)


def pack(x):
    rows, cols = x.shape
    if not packs(rows, cols):
        return x
    rest = x[:, 2 * LANES :]
    tail = jnp.concatenate([rest[: rows // 2], rest[rows // 2 :]], axis=1)
    return jnp.concatenate([x[:, :LANES], x[:, LANES : 2 * LANES], tail], axis=0)


def unpack(p, rows, cols):
    if not packs(rows, cols):
        return p[:rows, : 2 * LANES], p[:rows, 2 * LANES :]
    tail = p[2 * rows : 5 * rows // 2]
    rest = jnp.concatenate([tail[:, : LANES // 2], tail[:, LANES // 2 :]], axis=0)
    return jnp.concatenate([p[:rows], p[rows : 2 * rows]], axis=1), rest


NOTE = 16
SPARE = 32


def write_note(place, lanes):
    count = place.shape[1]
    filled = []
    for digit in (place >> 6, place & 63):
        for at in range(0, count, lanes):
            part = digit[:, at : at + lanes].astype(F32)
            spare = lanes - part.shape[1]
            filled.append(jnp.concatenate([part, jnp.zeros((1, spare), F32)], axis=1) if spare else part)
    filled.append(jnp.zeros((NOTE - len(filled), lanes), F32))
    return jnp.concatenate(filled, axis=0).astype(BF16)


def read_note(ref, count):
    note = ref[ref.shape[0] - NOTE :, :].astype(F32)
    lanes = note.shape[1]
    lines = -(-count // lanes)
    digits = []
    for d in range(2):
        parts = [
            note[d * lines + i : d * lines + i + 1, : min(lanes, count - i * lanes)]
            for i in range(lines)
        ]
        digits.append(parts[0] if lines == 1 else jnp.concatenate(parts, axis=1))
    return digits[0] * 64 + digits[1]


def pack_kernel(index_ref, qkv_ref, first_ref, value_ref, all_ref):
    count = all_ref.shape[1] - SPARE
    for j in range(3):
        all_ref[j, :count, :] = pack(qkv_ref[j])
        all_ref[j, count:, :] = jnp.zeros((SPARE, all_ref.shape[2]), BF16)
    first_ref[...] = all_ref[index_ref[2]]
    value_ref[...] = all_ref[2]


def pack_proj_kernel(proj_ref, place_ref, out_ref):
    count = out_ref.shape[0] - NOTE
    out_ref[:count, :] = pack(proj_ref[...])
    out_ref[count:, :] = write_note(place_ref[...], out_ref.shape[1])


def norm_kernel(index_ref, patches_ref, gain_ref, hidden_ref, own_ref):
    rows = patches_ref.shape[0]
    x = patches_ref[...]
    xf = x.astype(F32)
    mean_sq = jnp.mean(xf * xf, axis=-1, keepdims=True)
    gain = gain_ref[...].reshape(1, -1)
    hidden_ref[...] = (xf * lax.rsqrt(mean_sq + 1e-06) * gain).astype(BF16)
    step = 256
    pick = step // 4
    row = lax.broadcasted_iota(jnp.int32, (pick, step), 0)
    col = lax.broadcasted_iota(jnp.int32, (pick, step), 1)
    chosen = one_hot(col == 4 * row + index_ref[1])
    for i in range(rows // step):
        own_ref[i * pick : (i + 1) * pick, :] = jnp.dot(
            chosen, x[i * step : (i + 1) * step], preferred_element_type=F32
        ).astype(BF16)


def attend(index_ref, hidden_ref, valid_ref, w_ref, out_refs, q_ref, k_ref, v_ref, mix_ref):
    rows, width = q_ref.shape
    heads = width // HD
    main = 2 * LANES
    rest = width - main
    qkv = jnp.dot(hidden_ref[...], w_ref[...], preferred_element_type=F32)
    for j, ref in enumerate((q_ref, k_ref, v_ref)):
        ref[:, :main] = qkv[:, j * main : (j + 1) * main].astype(BF16)
        at = 3 * main + j * rest
        ref[:, main:] = qkv[:, at : at + rest].astype(BF16)
    q_win = lax.broadcasted_iota(jnp.int32, (PAIR, PAIR), 1) // WIN
    k_win = lax.broadcasted_iota(jnp.int32, (PAIR, PAIR), 0) // WIN
    same = q_win == k_win
    floor = jnp.where(same, F32(-1e30), F32(-3e38))
    pick = PAIR // 4
    src = lax.broadcasted_iota(jnp.int32, (PAIR, PAIR), 1)
    dst = lax.broadcasted_iota(jnp.int32, (PAIR, PAIR), 0)
    order = one_hot(src == 4 * (dst % pick) + dst // pick)
    zero = jnp.zeros((HD, PAIR), BF16)
    factor = F32(HD ** (-0.5) * math.log2(math.e))
    for p in range(rows // PAIR):
        at = p * PAIR
        q_turned = q_ref[at : at + PAIR, :].T
        v_turned = v_ref[at : at + PAIR, :].T
        q_all = jnp.concatenate(
            [
                jnp.concatenate(
                    [q_turned[h * HD : (h + 1) * HD] if i == h else zero for i in range(heads)], axis=1
                )
                for h in range(heads)
            ],
            axis=0,
        )
        scores = jnp.dot(k_ref[at : at + PAIR, :], q_all, preferred_element_type=F32)
        live = jnp.broadcast_to(valid_ref[p : p + 1, :].astype(F32), (PAIR, PAIR)).T > 0
        bias = jnp.where(same & live, F32(0), floor)
        mixed = []
        for h in range(heads):
            s = scores[:, h * PAIR : (h + 1) * PAIR] + bias
            e = jnp.exp2((s - jnp.max(s, axis=0, keepdims=True)) * factor)
            weights = (e * (1.0 / jnp.sum(e, axis=0, keepdims=True))).astype(BF16)
            mixed.append(
                jnp.dot(v_turned[h * HD : (h + 1) * HD], weights, preferred_element_type=F32)
            )
        mixed = jnp.concatenate(mixed, axis=0).astype(BF16)
        mixed = lax.dot_general(
            order, mixed, (((1,), (1,)), ((), ())), preferred_element_type=F32
        ).astype(BF16)
        for t in range(4):
            mix_ref[t, p * pick : (p + 1) * pick, :] = mixed[t * pick : (t + 1) * pick]
    for s, out_ref in enumerate(out_refs):
        out_ref[...] = pack(mix_ref[index_ref[1] ^ s])


def attention_kernel(n_ctx, width, index_ref, hidden_ref, valid_ref, *refs):
    shards = list(refs[: 2 + 3 * (n_ctx - 2)])
    *out_refs, w_ref, q_ref, k_ref, v_ref, mix_ref = refs[len(shards) :]
    depth = w_ref.shape[0] // n_ctx
    me = index_ref[0]
    flip = index_ref[2] > 0
    main = 2 * LANES
    for key in range(n_ctx):
        rows = pl.ds(pl.multiple_of((me ^ key) * depth, depth), depth)
        if key < 2:
            block = shards.pop(0)
            thirds = [block[j] for j in range(3)]
        else:
            first, second, value = [shards.pop(0)[...] for _ in range(3)]
            thirds = [jnp.where(flip, second, first), jnp.where(flip, first, second), value]
        tails = []
        for j, third in enumerate(thirds):
            w_ref[rows, j * main : (j + 1) * main], tail = unpack(third, depth, width)
            tails.append(tail)
        w_ref[rows, 3 * main :] = jnp.concatenate(tails, axis=1)
    attend(index_ref, hidden_ref, valid_ref, w_ref, out_refs, q_ref, k_ref, v_ref, mix_ref)


def project_kernel(n_ctx, width, col, index_ref, *refs):
    *blocks, own_ref, gain_ref, low_ref, high_ref, part_ref = refs[4:]
    rows = own_ref.shape[0]
    mixes = [unpack(m[...], rows, width) for m in refs[:4]]
    flip = index_ref[2] > 0
    mixes[2:] = [
        [jnp.where(flip, b, a) for a, b in zip(mixes[2], mixes[3])],
        [jnp.where(flip, a, b) for a, b in zip(mixes[2], mixes[3])],
    ]
    me = index_ref[0]
    main = 2 * LANES
    mixed = jnp.concatenate([m for m, _ in mixes] + [r for _, r in mixes], axis=1)
    mains = []
    rests = []
    for key in range(n_ctx):
        pieces = []
        for ref in [blocks.pop(0) for _ in range((4, 1)[key] if key < 2 else 2)]:
            pieces += [ref[...]] if len(ref.shape) == 2 else [ref[i] for i in range(ref.shape[0])]
        halves = [unpack(p, width, col) for p in pieces]
        both = []
        for half in ([h[0] for h in halves], [h[1] for h in halves]):
            both.append(jnp.concatenate([h[:main] for h in half] + [h[main:] for h in half], axis=0))
        mains.append(jnp.dot(mixed, both[0], preferred_element_type=F32))
        rests.append(both[1])
    if rests[0].shape[1]:
        rest = jnp.dot(mixed, jnp.concatenate(rests, axis=1), preferred_element_type=F32)
        count = rests[0].shape[1]
        mains = [
            jnp.concatenate([m, rest[:, key * count : (key + 1) * count]], axis=1)
            for key, m in enumerate(mains)
        ]
    for key in range(n_ctx):
        part_ref[me ^ key] = mains[key]
    total = jnp.concatenate([part_ref[i] for i in range(n_ctx)], axis=1)
    total = total + own_ref[...].astype(F32)
    mean_sq = jnp.mean(total * total, axis=-1, keepdims=True)
    gain = gain_ref[...].reshape(1, -1)
    normed = (total * lax.rsqrt(mean_sq + 1e-06) * gain).astype(BF16)
    half = low_ref.shape[0]
    low_ref[...] = normed[:half]
    high_ref[...] = normed[half:]


def place_kernel(count, index_ref, *refs):
    place_refs = refs[:count]
    row_refs = refs[count:-1]
    out_ref = refs[-1]
    spots = out_ref.shape[0]
    chosen = []
    base = (index_ref[0] * spots).astype(F32)
    for place_ref in place_refs:
        note_ref = place_ref.at[0] if len(place_ref.shape) == 3 else place_ref
        target = read_note(note_ref, spots) - base
        grid = lax.broadcasted_iota(jnp.int32, (spots, spots), 0).astype(F32)
        chosen.append(one_hot(grid == target))
    out_ref[...] = jnp.dot(
        jnp.concatenate(chosen, axis=1),
        jnp.concatenate([ref[...] for ref in row_refs], axis=0),
        preferred_element_type=F32,
    ).astype(BF16)


def local(n_dp, n_ctx, n_ten, patches, valid, place, gain_attn, w_qkv, w_proj, gain_merge):
    rows, feat = patches.shape
    depth, _, width = w_qkv.shape
    col = w_proj.shape[1]
    groups = rows // 4
    ten = lax.axis_index("tensor")
    half = lax.axis_index("dp") % 2
    index = jnp.stack([lax.axis_index("context"), ten, half]).astype(jnp.int32)
    cross = list(cross_keys(n_ctx))

    def over_dp(x):
        return swap(x, "dp", n_dp, 1)

    def over_core(x):
        return swap(x, "context", n_ctx, 1)

    third = packed_shape(depth, width)
    third = (third[0] + SPARE, third[1])
    piece = packed_shape(width, col)
    first, value, own = pl.pallas_call(
        pack_kernel,
        out_shape=(shape(*third), shape(*third), shape(3, *third)),
        in_specs=[SMEM, VMEM],
        out_specs=(VMEM,) * 3,
        compiler_params=params(8),
        name="pack",
    )(index, jnp.transpose(w_qkv, (1, 0, 2)))
    w_proj = pl.pallas_call(
        pack_proj_kernel,
        out_shape=shape(piece[0] + NOTE, piece[1]),
        in_specs=[VMEM, VMEM],
        out_specs=VMEM,
        compiler_params=params(8),
        name="pack_proj",
    )(w_proj, place.reshape(1, groups))
    first = gather_cross(first, n_ctx)
    value = gather_cross(value, n_ctx)
    twin = over_core(own)
    far = lax.ppermute(
        w_proj,
        ("dp", "tensor"),
        [
            (d * n_ten + t, d * n_ten + (t ^ (2 + d % 2)))
            for d in range(n_dp)
            for t in range(n_ten)
        ],
    )
    by_one = swap(w_proj, "tensor", n_ten, 1)
    first, twin, patches = together(first, twin, patches)

    second = {k: over_dp(first[k]) for k in cross}
    first_twin = {k: over_core(first[k]) for k in cross}
    hidden, own_patches = pl.pallas_call(
        norm_kernel,
        out_shape=(shape(rows, feat), shape(groups, feat)),
        in_specs=[SMEM, VMEM, VMEM],
        out_specs=(VMEM, VMEM),
        compiler_params=params(16),
        name="norm",
    )(index, patches, gain_attn)
    by_one, hidden = together(by_one, hidden)
    low = gather_cross(jnp.stack([w_proj, by_one]), n_ctx)
    second, value, first_twin, hidden = together(second, value, first_twin, hidden)

    second_twin = {k: over_core(second[k]) for k in cross}
    value_twin = {k: over_core(value[k]) for k in cross}
    far, *_ = together(far, *second.values())
    far2 = over_dp(far)

    shard_list = [own, twin]
    for k in cross:
        shard_list += [first[k], second[k], value[k], first_twin[k], second_twin[k], value_twin[k]]

    mix_shapes = (shape(*packed_shape(groups, width)),) * n_ten
    mixed = pl.pallas_call(
        functools.partial(attention_kernel, n_ctx, width),
        out_shape=mix_shapes,
        in_specs=[SMEM] + [VMEM] * (2 + len(shard_list)),
        out_specs=(VMEM,) * n_ten,
        scratch_shapes=[pltpu.VMEM((feat, 3 * width), BF16)]
        + [pltpu.VMEM((rows, width), BF16)] * 3
        + [pltpu.VMEM((4, groups, width), BF16)],
        compiler_params=params(20),
        name="attention",
    )(index, hidden, valid.reshape(rows // PAIR, PAIR), *shard_list)

    mixed, far, far2, low = together(list(mixed), far, far2, low)
    received = [mixed[0]] + [swap(mixed[s], "tensor", n_ten, s) for s in range(1, n_ten)]
    high = gather_cross(jnp.stack([far, far2]), n_ctx)
    blocks = [w_proj, by_one, far, far2, over_core(jnp.stack([w_proj, by_one, far, far2]))]
    low_twin = {k: over_core(low[k]) for k in cross}
    received, high = together(received, high)
    for k in cross:
        blocks += [low[k], high[k], low_twin[k], over_core(high[k])]
    done = pl.pallas_call(
        functools.partial(project_kernel, n_ctx, width, col),
        out_shape=(shape(groups // 2, feat),) * 2,
        in_specs=[SMEM] + [VMEM] * (n_ten + len(blocks) + 2),
        out_specs=(VMEM,) * 2,
        scratch_shapes=[pltpu.VMEM((n_ctx, groups, col), F32)],
        compiler_params=params(24),
        name="project",
    )(index, *received, *blocks, own_patches, gain_merge)

    gathered = []
    for rows_out in done:
        crossed = gather_cross(rows_out, n_ctx)
        if gathered:
            for k in cross:
                crossed[k], gathered[0][k ^ 1] = together(crossed[k], gathered[0][k ^ 1])
        for k in list(crossed):
            crossed[k ^ 1] = over_core(crossed[k])
        gathered.append(crossed)
    notes = [w_proj, blocks[4]]
    for k in cross:
        notes += [low[k], low_twin[k]]
    return pl.pallas_call(
        functools.partial(place_kernel, n_ctx),
        out_shape=shape(groups, feat),
        in_specs=[SMEM] + [VMEM] * (3 * n_ctx),
        out_specs=VMEM,
        compiler_params=params(28),
        name="placement",
    )(index, *notes, *[half[k] for k in range(n_ctx) for half in gathered])


def solution(mesh):
    in_specs = (
        P(("dp", "context"), None),
        P(("dp", "context")),
        P(("dp", "context")),
        P(),
        P("context", None, "tensor"),
        P("tensor", "context"),
        P(),
    )
    out_specs = P(("dp", "context"), "tensor")
    sizes = [mesh.shape[name] for name in ("dp", "context", "tensor")]
    body = functools.partial(local, *sizes)
    return jax.shard_map(body, mesh=mesh, in_specs=in_specs, out_specs=out_specs, check_vma=False)
```

```python
import functools
import math

import jax
import jax.numpy as jnp
from jax import lax
from jax.experimental import pallas as pl
from jax.experimental.pallas import tpu as pltpu
from jax.sharding import PartitionSpec as P

HD = 80
WIN = 64
PAIR = 2 * WIN
LANES = 128
F32 = jnp.float32
BF16 = jnp.bfloat16
VMEM = pl.BlockSpec(memory_space=pltpu.VMEM)
SMEM = pl.BlockSpec(memory_space=pltpu.SMEM)


def params(mib):
    return pltpu.CompilerParams(vmem_limit_bytes=mib * 1024 * 1024)


def swap(x, axis, size, bit):
    return lax.ppermute(x, axis, [(i, i ^ bit) for i in range(size)])


def cross_keys(size):
    return range(2, size, 2)


def gather_cross(x, size):
    blocks = {0: x}
    bit = size // 2
    while bit > 1:
        for key in list(blocks):
            blocks[key ^ bit] = swap(blocks[key], "context", size, bit)
        bit //= 2
    return blocks


def gather_xor(x, size):
    blocks = gather_cross(x, size)
    for key in list(blocks):
        blocks[key ^ 1] = swap(blocks[key], "context", size, 1)
    return blocks


def together(*values):
    return lax.optimization_barrier(values)


def one_hot(mask):
    return mask.astype(F32).astype(BF16)


def shape(*dims):
    return jax.ShapeDtypeStruct(dims, BF16)


def packs(rows, cols):
    return rows % 32 == 0 and cols == 2 * LANES + LANES // 2


def packed_shape(rows, cols):
    return (rows * 5 // 2, LANES) if packs(rows, cols) else (rows, cols)


def pack(x):
    rows, cols = x.shape
    if not packs(rows, cols):
        return x
    rest = x[:, 2 * LANES :]
    tail = jnp.concatenate([rest[: rows // 2], rest[rows // 2 :]], axis=1)
    return jnp.concatenate([x[:, :LANES], x[:, LANES : 2 * LANES], tail], axis=0)


def unpack(p, rows, cols):
    if not packs(rows, cols):
        return p[:rows, : 2 * LANES], p[:rows, 2 * LANES :]
    tail = p[2 * rows : 5 * rows // 2]
    rest = jnp.concatenate([tail[:, : LANES // 2], tail[:, LANES // 2 :]], axis=0)
    return jnp.concatenate([p[:rows], p[rows : 2 * rows]], axis=1), rest


NOTE = 16
SPARE = 32


def write_note(place, lanes):
    count = place.shape[1]
    filled = []
    for digit in (place >> 6, place & 63):
        for at in range(0, count, lanes):
            part = digit[:, at : at + lanes].astype(F32)
            spare = lanes - part.shape[1]
            filled.append(jnp.concatenate([part, jnp.zeros((1, spare), F32)], axis=1) if spare else part)
    filled.append(jnp.zeros((NOTE - len(filled), lanes), F32))
    return jnp.concatenate(filled, axis=0).astype(BF16)


def read_note(ref, count):
    note = ref[ref.shape[0] - NOTE :, :].astype(F32)
    lanes = note.shape[1]
    lines = -(-count // lanes)
    digits = []
    for d in range(2):
        parts = [
            note[d * lines + i : d * lines + i + 1, : min(lanes, count - i * lanes)]
            for i in range(lines)
        ]
        digits.append(parts[0] if lines == 1 else jnp.concatenate(parts, axis=1))
    return digits[0] * 64 + digits[1]


def pack_kernel(index_ref, qkv_ref, first_ref, value_ref, all_ref):
    count = all_ref.shape[1] - SPARE
    for j in range(3):
        all_ref[j, :count, :] = pack(qkv_ref[j])
        all_ref[j, count:, :] = jnp.zeros((SPARE, all_ref.shape[2]), BF16)
    first_ref[...] = all_ref[index_ref[2]]
    value_ref[...] = all_ref[2]


def pack_proj_kernel(proj_ref, place_ref, out_ref):
    count = out_ref.shape[0] - NOTE
    out_ref[:count, :] = pack(proj_ref[...])
    out_ref[count:, :] = write_note(place_ref[...], out_ref.shape[1])


def norm_kernel(index_ref, patches_ref, gain_ref, hidden_ref, own_ref):
    rows = patches_ref.shape[0]
    x = patches_ref[...]
    xf = x.astype(F32)
    mean_sq = jnp.mean(xf * xf, axis=-1, keepdims=True)
    gain = gain_ref[...].reshape(1, -1)
    hidden_ref[...] = (xf * lax.rsqrt(mean_sq + 1e-06) * gain).astype(BF16)
    step = 256
    pick = step // 4
    row = lax.broadcasted_iota(jnp.int32, (pick, step), 0)
    col = lax.broadcasted_iota(jnp.int32, (pick, step), 1)
    chosen = one_hot(col == 4 * row + index_ref[1])
    for i in range(rows // step):
        own_ref[i * pick : (i + 1) * pick, :] = jnp.dot(
            chosen, x[i * step : (i + 1) * step], preferred_element_type=F32
        ).astype(BF16)


def attend(index_ref, hidden_ref, valid_ref, w_ref, out_refs, q_ref, k_ref, v_ref, mix_ref):
    rows, width = q_ref.shape
    heads = width // HD
    main = 2 * LANES
    rest = width - main
    qkv = jnp.dot(hidden_ref[...], w_ref[...], preferred_element_type=F32)
    for j, ref in enumerate((q_ref, k_ref, v_ref)):
        ref[:, :main] = qkv[:, j * main : (j + 1) * main].astype(BF16)
        at = 3 * main + j * rest
        ref[:, main:] = qkv[:, at : at + rest].astype(BF16)
    q_win = lax.broadcasted_iota(jnp.int32, (PAIR, PAIR), 1) // WIN
    k_win = lax.broadcasted_iota(jnp.int32, (PAIR, PAIR), 0) // WIN
    same = q_win == k_win
    floor = jnp.where(same, F32(-1e30), F32(-3e38))
    pick = PAIR // 4
    src = lax.broadcasted_iota(jnp.int32, (PAIR, PAIR), 1)
    dst = lax.broadcasted_iota(jnp.int32, (PAIR, PAIR), 0)
    order = one_hot(src == 4 * (dst % pick) + dst // pick)
    zero = jnp.zeros((HD, PAIR), BF16)
    factor = F32(HD ** (-0.5) * math.log2(math.e))
    for p in range(rows // PAIR):
        at = p * PAIR
        q_turned = q_ref[at : at + PAIR, :].T
        v_turned = v_ref[at : at + PAIR, :].T
        q_all = jnp.concatenate(
            [
                jnp.concatenate(
                    [q_turned[h * HD : (h + 1) * HD] if i == h else zero for i in range(heads)], axis=1
                )
                for h in range(heads)
            ],
            axis=0,
        )
        scores = jnp.dot(k_ref[at : at + PAIR, :], q_all, preferred_element_type=F32)
        live = jnp.broadcast_to(valid_ref[p : p + 1, :].astype(F32), (PAIR, PAIR)).T > 0
        bias = jnp.where(same & live, F32(0), floor)
        mixed = []
        for h in range(heads):
            s = scores[:, h * PAIR : (h + 1) * PAIR] + bias
            e = jnp.exp2((s - jnp.max(s, axis=0, keepdims=True)) * factor)
            weights = (e * (1.0 / jnp.sum(e, axis=0, keepdims=True))).astype(BF16)
            mixed.append(
                jnp.dot(v_turned[h * HD : (h + 1) * HD], weights, preferred_element_type=F32)
            )
        mixed = jnp.concatenate(mixed, axis=0).astype(BF16)
        mixed = lax.dot_general(
            order, mixed, (((1,), (1,)), ((), ())), preferred_element_type=F32
        ).astype(BF16)
        for t in range(4):
            mix_ref[t, p * pick : (p + 1) * pick, :] = mixed[t * pick : (t + 1) * pick]
    for s, out_ref in enumerate(out_refs):
        out_ref[...] = pack(mix_ref[index_ref[1] ^ s])


def attention_kernel(n_ctx, width, index_ref, hidden_ref, valid_ref, *refs):
    shards = list(refs[: 2 + 3 * (n_ctx - 2)])
    *out_refs, w_ref, q_ref, k_ref, v_ref, mix_ref = refs[len(shards) :]
    depth = w_ref.shape[0] // n_ctx
    me = index_ref[0]
    flip = index_ref[2] > 0
    main = 2 * LANES
    for key in range(n_ctx):
        rows = pl.ds(pl.multiple_of((me ^ key) * depth, depth), depth)
        if key < 2:
            block = shards.pop(0)
            thirds = [block[j] for j in range(3)]
        else:
            first, second, value = [shards.pop(0)[...] for _ in range(3)]
            thirds = [jnp.where(flip, second, first), jnp.where(flip, first, second), value]
        tails = []
        for j, third in enumerate(thirds):
            w_ref[rows, j * main : (j + 1) * main], tail = unpack(third, depth, width)
            tails.append(tail)
        w_ref[rows, 3 * main :] = jnp.concatenate(tails, axis=1)
    attend(index_ref, hidden_ref, valid_ref, w_ref, out_refs, q_ref, k_ref, v_ref, mix_ref)


def project_kernel(n_ctx, width, col, index_ref, *refs):
    *blocks, own_ref, gain_ref, low_ref, high_ref, part_ref = refs[4:]
    rows = own_ref.shape[0]
    mixes = [unpack(m[...], rows, width) for m in refs[:4]]
    flip = index_ref[2] > 0
    mixes[2:] = [
        [jnp.where(flip, b, a) for a, b in zip(mixes[2], mixes[3])],
        [jnp.where(flip, a, b) for a, b in zip(mixes[2], mixes[3])],
    ]
    me = index_ref[0]
    main = 2 * LANES
    mixed = jnp.concatenate([m for m, _ in mixes] + [r for _, r in mixes], axis=1)
    mains = []
    rests = []
    for key in range(n_ctx):
        pieces = []
        for ref in [blocks.pop(0) for _ in range((4, 1)[key] if key < 2 else 2)]:
            pieces += [ref[...]] if len(ref.shape) == 2 else [ref[i] for i in range(ref.shape[0])]
        halves = [unpack(p, width, col) for p in pieces]
        both = []
        for half in ([h[0] for h in halves], [h[1] for h in halves]):
            both.append(jnp.concatenate([h[:main] for h in half] + [h[main:] for h in half], axis=0))
        mains.append(jnp.dot(mixed, both[0], preferred_element_type=F32))
        rests.append(both[1])
    if rests[0].shape[1]:
        rest = jnp.dot(mixed, jnp.concatenate(rests, axis=1), preferred_element_type=F32)
        count = rests[0].shape[1]
        mains = [
            jnp.concatenate([m, rest[:, key * count : (key + 1) * count]], axis=1)
            for key, m in enumerate(mains)
        ]
    for key in range(n_ctx):
        part_ref[me ^ key] = mains[key]
    total = jnp.concatenate([part_ref[i] for i in range(n_ctx)], axis=1)
    total = total + own_ref[...].astype(F32)
    mean_sq = jnp.mean(total * total, axis=-1, keepdims=True)
    gain = gain_ref[...].reshape(1, -1)
    normed = (total * lax.rsqrt(mean_sq + 1e-06) * gain).astype(BF16)
    half = low_ref.shape[0]
    low_ref[...] = normed[:half]
    high_ref[...] = normed[half:]


def place_kernel(count, index_ref, *refs):
    place_refs = refs[:count]
    *row_refs, out_ref, stage_ref, sem = refs[count:]
    spots = out_ref.shape[0]
    chosen = []
    base = (index_ref[0] * spots).astype(F32)
    for place_ref in place_refs:
        note_ref = place_ref.at[0] if len(place_ref.shape) == 3 else place_ref
        target = read_note(note_ref, spots) - base
        grid = lax.broadcasted_iota(jnp.int32, (spots, spots), 0).astype(F32)
        chosen.append(one_hot(grid == target))
    chosen = jnp.concatenate(chosen, axis=1)
    step = stage_ref.shape[2]
    copies = []
    for i in range(out_ref.shape[1] // step):
        cols = slice(i * step, (i + 1) * step)
        slot = stage_ref.at[i]
        slot[...] = jnp.dot(
            chosen,
            jnp.concatenate([ref[:, cols] for ref in row_refs], axis=0),
            preferred_element_type=F32,
        ).astype(BF16)
        copies.append(pltpu.make_async_copy(slot, out_ref.at[:, cols], sem.at[i]))
        copies[i].start()
    for copy in copies:
        copy.wait()


def local(n_dp, n_ctx, n_ten, patches, valid, place, gain_attn, w_qkv, w_proj, gain_merge):
    rows, feat = patches.shape
    depth, _, width = w_qkv.shape
    col = w_proj.shape[1]
    groups = rows // 4
    ten = lax.axis_index("tensor")
    half = lax.axis_index("dp") % 2
    index = jnp.stack([lax.axis_index("context"), ten, half]).astype(jnp.int32)
    cross = list(cross_keys(n_ctx))

    def over_dp(x):
        return swap(x, "dp", n_dp, 1)

    def over_core(x):
        return swap(x, "context", n_ctx, 1)

    third = packed_shape(depth, width)
    third = (third[0] + SPARE, third[1])
    piece = packed_shape(width, col)
    first, value, own = pl.pallas_call(
        pack_kernel,
        out_shape=(shape(*third), shape(*third), shape(3, *third)),
        in_specs=[SMEM, VMEM],
        out_specs=(VMEM,) * 3,
        compiler_params=params(8),
        name="pack",
    )(index, jnp.transpose(w_qkv, (1, 0, 2)))
    w_proj = pl.pallas_call(
        pack_proj_kernel,
        out_shape=shape(piece[0] + NOTE, piece[1]),
        in_specs=[VMEM, VMEM],
        out_specs=VMEM,
        compiler_params=params(8),
        name="pack_proj",
    )(w_proj, place.reshape(1, groups))
    first = gather_cross(first, n_ctx)
    value = gather_cross(value, n_ctx)
    twin = over_core(own)
    far = lax.ppermute(
        w_proj,
        ("dp", "tensor"),
        [
            (d * n_ten + t, d * n_ten + (t ^ (2 + d % 2)))
            for d in range(n_dp)
            for t in range(n_ten)
        ],
    )
    by_one = swap(w_proj, "tensor", n_ten, 1)
    first, twin, patches = together(first, twin, patches)

    second = {k: over_dp(first[k]) for k in cross}
    first_twin = {k: over_core(first[k]) for k in cross}
    hidden, own_patches = pl.pallas_call(
        norm_kernel,
        out_shape=(shape(rows, feat), shape(groups, feat)),
        in_specs=[SMEM, VMEM, VMEM],
        out_specs=(VMEM, VMEM),
        compiler_params=params(16),
        name="norm",
    )(index, patches, gain_attn)
    by_one, hidden = together(by_one, hidden)
    low = gather_cross(jnp.stack([w_proj, by_one]), n_ctx)
    second, value, first_twin, hidden = together(second, value, first_twin, hidden)

    second_twin = {k: over_core(second[k]) for k in cross}
    value_twin = {k: over_core(value[k]) for k in cross}
    far, *_ = together(far, *second.values())
    far2 = over_dp(far)

    shard_list = [own, twin]
    for k in cross:
        shard_list += [first[k], second[k], value[k], first_twin[k], second_twin[k], value_twin[k]]

    mix_shapes = (shape(*packed_shape(groups, width)),) * n_ten
    mixed = pl.pallas_call(
        functools.partial(attention_kernel, n_ctx, width),
        out_shape=mix_shapes,
        in_specs=[SMEM] + [VMEM] * (2 + len(shard_list)),
        out_specs=(VMEM,) * n_ten,
        scratch_shapes=[pltpu.VMEM((feat, 3 * width), BF16)]
        + [pltpu.VMEM((rows, width), BF16)] * 3
        + [pltpu.VMEM((4, groups, width), BF16)],
        compiler_params=params(20),
        name="attention",
    )(index, hidden, valid.reshape(rows // PAIR, PAIR), *shard_list)

    mixed, far, far2, low = together(list(mixed), far, far2, low)
    received = [mixed[0]] + [swap(mixed[s], "tensor", n_ten, s) for s in range(1, n_ten)]
    high = gather_cross(jnp.stack([far, far2]), n_ctx)
    blocks = [w_proj, by_one, far, far2, over_core(jnp.stack([w_proj, by_one, far, far2]))]
    low_twin = {k: over_core(low[k]) for k in cross}
    received, high = together(received, high)
    for k in cross:
        blocks += [low[k], high[k], low_twin[k], over_core(high[k])]
    done = pl.pallas_call(
        functools.partial(project_kernel, n_ctx, width, col),
        out_shape=(shape(groups // 2, feat),) * 2,
        in_specs=[SMEM] + [VMEM] * (n_ten + len(blocks) + 2),
        out_specs=(VMEM,) * 2,
        scratch_shapes=[pltpu.VMEM((n_ctx, groups, col), F32)],
        compiler_params=params(24),
        name="project",
    )(index, *received, *blocks, own_patches, gain_merge)

    gathered = []
    for rows_out in done:
        crossed = gather_cross(rows_out, n_ctx)
        if gathered:
            for k in cross:
                crossed[k], gathered[0][k ^ 1] = together(crossed[k], gathered[0][k ^ 1])
        for k in list(crossed):
            crossed[k ^ 1] = over_core(crossed[k])
        gathered.append(crossed)
    notes = [w_proj, blocks[4]]
    for k in cross:
        notes += [low[k], low_twin[k]]
    return pl.pallas_call(
        functools.partial(place_kernel, n_ctx),
        out_shape=shape(groups, feat),
        in_specs=[SMEM] + [VMEM] * (3 * n_ctx),
        out_specs=pl.BlockSpec(memory_space=pl.ANY),
        scratch_shapes=[
            pltpu.VMEM((feat // 256, groups, 256), BF16),
            pltpu.SemaphoreType.DMA((feat // 256,)),
        ],
        compiler_params=params(28),
        name="placement",
    )(index, *notes, *[half[k] for k in range(n_ctx) for half in gathered])


def solution(mesh):
    in_specs = (
        P(("dp", "context"), None),
        P(("dp", "context")),
        P(("dp", "context")),
        P(),
        P("context", None, "tensor"),
        P("tensor", "context"),
        P(),
    )
    out_specs = P(("dp", "context"), "tensor")
    sizes = [mesh.shape[name] for name in ("dp", "context", "tensor")]
    body = functools.partial(local, *sizes)
    return jax.shard_map(body, mesh=mesh, in_specs=in_specs, out_specs=out_specs, check_vma=False)
```

```python
import functools
import math

import jax
import jax.numpy as jnp
from jax import lax
from jax.experimental import pallas as pl
from jax.experimental.pallas import tpu as pltpu
from jax.sharding import PartitionSpec as P

HD = 80
WIN = 64
PAIR = 2 * WIN
LANES = 128
F32 = jnp.float32
BF16 = jnp.bfloat16
VMEM = pl.BlockSpec(memory_space=pltpu.VMEM)
SMEM = pl.BlockSpec(memory_space=pltpu.SMEM)


def params(mib):
    return pltpu.CompilerParams(vmem_limit_bytes=mib * 1024 * 1024)


def swap(x, axis, size, bit):
    return lax.ppermute(x, axis, [(i, i ^ bit) for i in range(size)])


def cross_keys(size):
    return range(2, size, 2)


def gather_cross(x, size):
    blocks = {0: x}
    bit = size // 2
    while bit > 1:
        for key in list(blocks):
            blocks[key ^ bit] = swap(blocks[key], "context", size, bit)
        bit //= 2
    return blocks


def gather_xor(x, size):
    blocks = gather_cross(x, size)
    for key in list(blocks):
        blocks[key ^ 1] = swap(blocks[key], "context", size, 1)
    return blocks


def together(*values):
    return lax.optimization_barrier(values)


def one_hot(mask):
    return mask.astype(F32).astype(BF16)


def shape(*dims):
    return jax.ShapeDtypeStruct(dims, BF16)


def packs(rows, cols):
    return rows % 32 == 0 and cols == 2 * LANES + LANES // 2


def packed_shape(rows, cols):
    return (rows * 5 // 2, LANES) if packs(rows, cols) else (rows, cols)


def pack(x):
    rows, cols = x.shape
    if not packs(rows, cols):
        return x
    rest = x[:, 2 * LANES :]
    tail = jnp.concatenate([rest[: rows // 2], rest[rows // 2 :]], axis=1)
    return jnp.concatenate([x[:, :LANES], x[:, LANES : 2 * LANES], tail], axis=0)


def unpack(p, rows, cols):
    if not packs(rows, cols):
        return p[:rows, : 2 * LANES], p[:rows, 2 * LANES :]
    tail = p[2 * rows : 5 * rows // 2]
    rest = jnp.concatenate([tail[:, : LANES // 2], tail[:, LANES // 2 :]], axis=0)
    return jnp.concatenate([p[:rows], p[rows : 2 * rows]], axis=1), rest


NOTE = 16
SPARE = 16
FAR_SPARE = 48


def write_note(place, lanes):
    count = place.shape[1]
    filled = []
    for digit in (place >> 6, place & 63):
        for at in range(0, count, lanes):
            part = digit[:, at : at + lanes].astype(F32)
            spare = lanes - part.shape[1]
            filled.append(jnp.concatenate([part, jnp.zeros((1, spare), F32)], axis=1) if spare else part)
    filled.append(jnp.zeros((NOTE - len(filled), lanes), F32))
    return jnp.concatenate(filled, axis=0).astype(BF16)


def read_note(ref, count):
    note = ref[ref.shape[0] - NOTE :, :].astype(F32)
    lanes = note.shape[1]
    lines = -(-count // lanes)
    digits = []
    for d in range(2):
        parts = [
            note[d * lines + i : d * lines + i + 1, : min(lanes, count - i * lanes)]
            for i in range(lines)
        ]
        digits.append(parts[0] if lines == 1 else jnp.concatenate(parts, axis=1))
    return digits[0] * 64 + digits[1]


def pack_kernel(index_ref, qkv_ref, first_ref, value_ref, all_ref):
    count = all_ref.shape[1] - SPARE
    for j in range(3):
        all_ref[j, :count, :] = pack(qkv_ref[j])
        all_ref[j, count:, :] = jnp.zeros((SPARE, all_ref.shape[2]), BF16)
    first_ref[...] = all_ref[index_ref[2]]
    value_ref[...] = all_ref[2]


def pack_proj_kernel(proj_ref, out_ref, far_ref):
    count = out_ref.shape[0]
    out_ref[...] = pack(proj_ref[...])
    far_ref[:count, :] = out_ref[...]
    far_ref[count:, :] = jnp.zeros((far_ref.shape[0] - count, far_ref.shape[1]), BF16)


def near_kernel(own_ref, next_ref, place_ref, out_ref):
    count = own_ref.shape[0]
    for i, ref in enumerate((own_ref, next_ref)):
        out_ref[i, :count, :] = ref[...]
        out_ref[i, count:, :] = write_note(place_ref[...], out_ref.shape[2])


def norm_kernel(index_ref, patches_ref, gain_ref, hidden_ref, own_ref):
    rows = patches_ref.shape[0]
    x = patches_ref[...]
    xf = x.astype(F32)
    mean_sq = jnp.mean(xf * xf, axis=-1, keepdims=True)
    gain = gain_ref[...].reshape(1, -1)
    hidden_ref[...] = (xf * lax.rsqrt(mean_sq + 1e-06) * gain).astype(BF16)
    step = 256
    pick = step // 4
    row = lax.broadcasted_iota(jnp.int32, (pick, step), 0)
    col = lax.broadcasted_iota(jnp.int32, (pick, step), 1)
    chosen = one_hot(col == 4 * row + index_ref[1])
    for i in range(rows // step):
        own_ref[i * pick : (i + 1) * pick, :] = jnp.dot(
            chosen, x[i * step : (i + 1) * step], preferred_element_type=F32
        ).astype(BF16)


def attend(index_ref, hidden_ref, valid_ref, w_ref, out_refs, q_ref, k_ref, v_ref, mix_ref):
    rows, width = q_ref.shape
    heads = width // HD
    main = 2 * LANES
    rest = width - main
    qkv = jnp.dot(hidden_ref[...], w_ref[...], preferred_element_type=F32)
    for j, ref in enumerate((q_ref, k_ref, v_ref)):
        ref[:, :main] = qkv[:, j * main : (j + 1) * main].astype(BF16)
        at = 3 * main + j * rest
        ref[:, main:] = qkv[:, at : at + rest].astype(BF16)
    q_win = lax.broadcasted_iota(jnp.int32, (PAIR, PAIR), 1) // WIN
    k_win = lax.broadcasted_iota(jnp.int32, (PAIR, PAIR), 0) // WIN
    same = q_win == k_win
    floor = jnp.where(same, F32(-1e30), F32(-3e38))
    pick = PAIR // 4
    src = lax.broadcasted_iota(jnp.int32, (PAIR, PAIR), 1)
    dst = lax.broadcasted_iota(jnp.int32, (PAIR, PAIR), 0)
    order = one_hot(src == 4 * (dst % pick) + dst // pick)
    zero = jnp.zeros((HD, PAIR), BF16)
    factor = F32(HD ** (-0.5) * math.log2(math.e))
    for p in range(rows // PAIR):
        at = p * PAIR
        q_turned = q_ref[at : at + PAIR, :].T
        v_turned = v_ref[at : at + PAIR, :].T
        q_all = jnp.concatenate(
            [
                jnp.concatenate(
                    [q_turned[h * HD : (h + 1) * HD] if i == h else zero for i in range(heads)], axis=1
                )
                for h in range(heads)
            ],
            axis=0,
        )
        scores = jnp.dot(k_ref[at : at + PAIR, :], q_all, preferred_element_type=F32)
        live = jnp.broadcast_to(valid_ref[p : p + 1, :].astype(F32), (PAIR, PAIR)).T > 0
        bias = jnp.where(same & live, F32(0), floor)
        mixed = []
        for h in range(heads):
            s = scores[:, h * PAIR : (h + 1) * PAIR] + bias
            e = jnp.exp2((s - jnp.max(s, axis=0, keepdims=True)) * factor)
            weights = (e * (1.0 / jnp.sum(e, axis=0, keepdims=True))).astype(BF16)
            mixed.append(
                jnp.dot(v_turned[h * HD : (h + 1) * HD], weights, preferred_element_type=F32)
            )
        mixed = jnp.concatenate(mixed, axis=0).astype(BF16)
        mixed = lax.dot_general(
            order, mixed, (((1,), (1,)), ((), ())), preferred_element_type=F32
        ).astype(BF16)
        for t in range(4):
            mix_ref[t, p * pick : (p + 1) * pick, :] = mixed[t * pick : (t + 1) * pick]
    for s, out_ref in enumerate(out_refs):
        out_ref[...] = pack(mix_ref[index_ref[1] ^ s])


def attention_kernel(n_ctx, width, index_ref, hidden_ref, valid_ref, *refs):
    shards = list(refs[: 2 + 3 * (n_ctx - 2)])
    *out_refs, w_ref, q_ref, k_ref, v_ref, mix_ref = refs[len(shards) :]
    depth = w_ref.shape[0] // n_ctx
    me = index_ref[0]
    flip = index_ref[2] > 0
    main = 2 * LANES
    for key in range(n_ctx):
        rows = pl.ds(pl.multiple_of((me ^ key) * depth, depth), depth)
        if key < 2:
            block = shards.pop(0)
            thirds = [block[j] for j in range(3)]
        else:
            first, second, value = [shards.pop(0)[...] for _ in range(3)]
            thirds = [jnp.where(flip, second, first), jnp.where(flip, first, second), value]
        tails = []
        for j, third in enumerate(thirds):
            w_ref[rows, j * main : (j + 1) * main], tail = unpack(third, depth, width)
            tails.append(tail)
        w_ref[rows, 3 * main :] = jnp.concatenate(tails, axis=1)
    attend(index_ref, hidden_ref, valid_ref, w_ref, out_refs, q_ref, k_ref, v_ref, mix_ref)


def project_kernel(n_ctx, width, col, index_ref, *refs):
    *blocks, own_ref, gain_ref, low_ref, high_ref, part_ref = refs[4:]
    rows = own_ref.shape[0]
    mixes = [unpack(m[...], rows, width) for m in refs[:4]]
    flip = index_ref[2] > 0
    mixes[2:] = [
        [jnp.where(flip, b, a) for a, b in zip(mixes[2], mixes[3])],
        [jnp.where(flip, a, b) for a, b in zip(mixes[2], mixes[3])],
    ]
    me = index_ref[0]
    main = 2 * LANES
    mixed = jnp.concatenate([m for m, _ in mixes] + [r for _, r in mixes], axis=1)
    mains = []
    rests = []
    for key in range(n_ctx):
        pieces = [ref[i] for ref in (blocks.pop(0), blocks.pop(0)) for i in range(2)]
        halves = [unpack(p, width, col) for p in pieces]
        both = []
        for half in ([h[0] for h in halves], [h[1] for h in halves]):
            both.append(jnp.concatenate([h[:main] for h in half] + [h[main:] for h in half], axis=0))
        mains.append(jnp.dot(mixed, both[0], preferred_element_type=F32))
        rests.append(both[1])
    if rests[0].shape[1]:
        rest = jnp.dot(mixed, jnp.concatenate(rests, axis=1), preferred_element_type=F32)
        count = rests[0].shape[1]
        mains = [
            jnp.concatenate([m, rest[:, key * count : (key + 1) * count]], axis=1)
            for key, m in enumerate(mains)
        ]
    for key in range(n_ctx):
        part_ref[me ^ key] = mains[key]
    total = jnp.concatenate([part_ref[i] for i in range(n_ctx)], axis=1)
    total = total + own_ref[...].astype(F32)
    mean_sq = jnp.mean(total * total, axis=-1, keepdims=True)
    gain = gain_ref[...].reshape(1, -1)
    normed = (total * lax.rsqrt(mean_sq + 1e-06) * gain).astype(BF16)
    half = low_ref.shape[0]
    low_ref[...] = normed[:half]
    high_ref[...] = normed[half:]


def place_kernel(count, index_ref, *refs):
    place_refs = refs[:count]
    *row_refs, out_ref, stage_ref, sem = refs[count:]
    spots = out_ref.shape[0]
    chosen = []
    base = (index_ref[0] * spots).astype(F32)
    for place_ref in place_refs:
        note_ref = place_ref.at[0] if len(place_ref.shape) == 3 else place_ref
        target = read_note(note_ref, spots) - base
        grid = lax.broadcasted_iota(jnp.int32, (spots, spots), 0).astype(F32)
        chosen.append(one_hot(grid == target))
    chosen = jnp.concatenate(chosen, axis=1)
    step = stage_ref.shape[2]
    copies = []
    for i in range(out_ref.shape[1] // step):
        cols = slice(i * step, (i + 1) * step)
        slot = stage_ref.at[i]
        slot[...] = jnp.dot(
            chosen,
            jnp.concatenate([ref[:, cols] for ref in row_refs], axis=0),
            preferred_element_type=F32,
        ).astype(BF16)
        copies.append(pltpu.make_async_copy(slot, out_ref.at[:, cols], sem.at[i]))
        copies[i].start()
    for copy in copies:
        copy.wait()


def local(n_dp, n_ctx, n_ten, patches, valid, place, gain_attn, w_qkv, w_proj, gain_merge):
    rows, feat = patches.shape
    depth, _, width = w_qkv.shape
    col = w_proj.shape[1]
    groups = rows // 4
    ten = lax.axis_index("tensor")
    half = lax.axis_index("dp") % 2
    index = jnp.stack([lax.axis_index("context"), ten, half]).astype(jnp.int32)
    cross = list(cross_keys(n_ctx))

    def over_dp(x):
        return swap(x, "dp", n_dp, 1)

    def over_core(x):
        return swap(x, "context", n_ctx, 1)

    third = packed_shape(depth, width)
    third = (third[0] + SPARE, third[1])
    piece = packed_shape(width, col)
    first, value, own = pl.pallas_call(
        pack_kernel,
        out_shape=(shape(*third), shape(*third), shape(3, *third)),
        in_specs=[SMEM, VMEM],
        out_specs=(VMEM,) * 3,
        compiler_params=params(8),
        name="pack",
    )(index, jnp.transpose(w_qkv, (1, 0, 2)))
    w_proj, far = pl.pallas_call(
        pack_proj_kernel,
        out_shape=(shape(*piece), shape(piece[0] + FAR_SPARE, piece[1])),
        in_specs=[VMEM],
        out_specs=(VMEM, VMEM),
        compiler_params=params(8),
        name="pack_proj",
    )(w_proj)
    first = gather_cross(first, n_ctx)
    value = gather_cross(value, n_ctx)
    twin = over_core(own)
    far = lax.ppermute(
        far,
        ("dp", "tensor"),
        [
            (d * n_ten + t, d * n_ten + (t ^ (2 + d % 2)))
            for d in range(n_dp)
            for t in range(n_ten)
        ],
    )
    by_one = swap(w_proj, "tensor", n_ten, 1)
    first, twin, patches = together(first, twin, patches)

    second = {k: over_dp(first[k]) for k in cross}
    first_twin = {k: over_core(first[k]) for k in cross}
    hidden, own_patches = pl.pallas_call(
        norm_kernel,
        out_shape=(shape(rows, feat), shape(groups, feat)),
        in_specs=[SMEM, VMEM, VMEM],
        out_specs=(VMEM, VMEM),
        compiler_params=params(16),
        name="norm",
    )(index, patches, gain_attn)
    by_one, hidden = together(by_one, hidden)
    near = pl.pallas_call(
        near_kernel,
        out_shape=shape(2, piece[0] + NOTE, piece[1]),
        in_specs=[VMEM] * 3,
        out_specs=VMEM,
        compiler_params=params(8),
        name="near",
    )(w_proj, by_one, place.reshape(1, groups))
    low = gather_cross(near, n_ctx)
    second, value, first_twin, hidden = together(second, value, first_twin, hidden)

    second_twin = {k: over_core(second[k]) for k in cross}
    value_twin = {k: over_core(value[k]) for k in cross}
    far, *_ = together(far, *second.values())
    far = far[: piece[0]]
    far2 = over_dp(far)

    shard_list = [own, twin]
    for k in cross:
        shard_list += [first[k], second[k], value[k], first_twin[k], second_twin[k], value_twin[k]]

    mix_shapes = (shape(*packed_shape(groups, width)),) * n_ten
    mixed = pl.pallas_call(
        functools.partial(attention_kernel, n_ctx, width),
        out_shape=mix_shapes,
        in_specs=[SMEM] + [VMEM] * (2 + len(shard_list)),
        out_specs=(VMEM,) * n_ten,
        scratch_shapes=[pltpu.VMEM((feat, 3 * width), BF16)]
        + [pltpu.VMEM((rows, width), BF16)] * 3
        + [pltpu.VMEM((4, groups, width), BF16)],
        compiler_params=params(20),
        name="attention",
    )(index, hidden, valid.reshape(rows // PAIR, PAIR), *shard_list)

    mixed, far, far2, low = together(list(mixed), far, far2, low)
    received = [mixed[0]] + [swap(mixed[s], "tensor", n_ten, s) for s in range(1, n_ten)]
    high = gather_cross(jnp.stack([far, far2]), n_ctx)
    far_pair = jnp.stack([far, far2])
    blocks = [near, far_pair, over_core(near), over_core(far_pair)]
    low_twin = {k: over_core(low[k]) for k in cross}
    received, high = together(received, high)
    for k in cross:
        blocks += [low[k], high[k], low_twin[k], over_core(high[k])]
    done = pl.pallas_call(
        functools.partial(project_kernel, n_ctx, width, col),
        out_shape=(shape(groups // 2, feat),) * 2,
        in_specs=[SMEM] + [VMEM] * (n_ten + len(blocks) + 2),
        out_specs=(VMEM,) * 2,
        scratch_shapes=[pltpu.VMEM((n_ctx, groups, col), F32)],
        compiler_params=params(24),
        name="project",
    )(index, *received, *blocks, own_patches, gain_merge)

    gathered = []
    for rows_out in done:
        crossed = gather_cross(rows_out, n_ctx)
        if gathered:
            for k in cross:
                crossed[k], gathered[0][k ^ 1] = together(crossed[k], gathered[0][k ^ 1])
        for k in list(crossed):
            crossed[k ^ 1] = over_core(crossed[k])
        gathered.append(crossed)
    notes = [near, blocks[2]]
    for k in cross:
        notes += [low[k], low_twin[k]]
    return pl.pallas_call(
        functools.partial(place_kernel, n_ctx),
        out_shape=shape(groups, feat),
        in_specs=[SMEM] + [VMEM] * (3 * n_ctx),
        out_specs=pl.BlockSpec(memory_space=pl.ANY),
        scratch_shapes=[
            pltpu.VMEM((feat // 256, groups, 256), BF16),
            pltpu.SemaphoreType.DMA((feat // 256,)),
        ],
        compiler_params=params(28),
        name="placement",
    )(index, *notes, *[half[k] for k in range(n_ctx) for half in gathered])


def solution(mesh):
    in_specs = (
        P(("dp", "context"), None),
        P(("dp", "context")),
        P(("dp", "context")),
        P(),
        P("context", None, "tensor"),
        P("tensor", "context"),
        P(),
    )
    out_specs = P(("dp", "context"), "tensor")
    sizes = [mesh.shape[name] for name in ("dp", "context", "tensor")]
    body = functools.partial(local, *sizes)
    return jax.shard_map(body, mesh=mesh, in_specs=in_specs, out_specs=out_specs, check_vma=False)
```

```python
import functools
import math

import jax
import jax.numpy as jnp
from jax import lax
from jax.experimental import pallas as pl
from jax.experimental.pallas import tpu as pltpu
from jax.sharding import PartitionSpec as P

HD = 80
WIN = 64
PAIR = 2 * WIN
LANES = 128
F32 = jnp.float32
BF16 = jnp.bfloat16
VMEM = pl.BlockSpec(memory_space=pltpu.VMEM)
SMEM = pl.BlockSpec(memory_space=pltpu.SMEM)


def params(mib):
    return pltpu.CompilerParams(vmem_limit_bytes=mib * 1024 * 1024)


def swap(x, axis, size, bit):
    return lax.ppermute(x, axis, [(i, i ^ bit) for i in range(size)])


def cross_keys(size):
    return range(2, size, 2)


def gather_cross(x, size):
    blocks = {0: x}
    bit = size // 2
    while bit > 1:
        for key in list(blocks):
            blocks[key ^ bit] = swap(blocks[key], "context", size, bit)
        bit //= 2
    return blocks


def gather_xor(x, size):
    blocks = gather_cross(x, size)
    for key in list(blocks):
        blocks[key ^ 1] = swap(blocks[key], "context", size, 1)
    return blocks


def together(*values):
    return lax.optimization_barrier(values)


def one_hot(mask):
    return mask.astype(F32).astype(BF16)


def shape(*dims):
    return jax.ShapeDtypeStruct(dims, BF16)


def packs(rows, cols):
    return rows % 32 == 0 and cols == 2 * LANES + LANES // 2


def packed_shape(rows, cols):
    return (rows * 5 // 2, LANES) if packs(rows, cols) else (rows, cols)


def pack(x):
    rows, cols = x.shape
    if not packs(rows, cols):
        return x
    rest = x[:, 2 * LANES :]
    tail = jnp.concatenate([rest[: rows // 2], rest[rows // 2 :]], axis=1)
    return jnp.concatenate([x[:, :LANES], x[:, LANES : 2 * LANES], tail], axis=0)


def unpack(p, rows, cols):
    if not packs(rows, cols):
        return p[:rows, : 2 * LANES], p[:rows, 2 * LANES :]
    tail = p[2 * rows : 5 * rows // 2]
    rest = jnp.concatenate([tail[:, : LANES // 2], tail[:, LANES // 2 :]], axis=0)
    return jnp.concatenate([p[:rows], p[rows : 2 * rows]], axis=1), rest


NOTE = 16
SPARE = 16
FAR_SPARE = 48


def write_note(place, lanes):
    count = place.shape[1]
    filled = []
    for digit in (place >> 6, place & 63):
        for at in range(0, count, lanes):
            part = digit[:, at : at + lanes].astype(F32)
            spare = lanes - part.shape[1]
            filled.append(jnp.concatenate([part, jnp.zeros((1, spare), F32)], axis=1) if spare else part)
    filled.append(jnp.zeros((NOTE - len(filled), lanes), F32))
    return jnp.concatenate(filled, axis=0).astype(BF16)


def read_note(ref, count):
    note = ref[ref.shape[0] - NOTE :, :].astype(F32)
    lanes = note.shape[1]
    lines = -(-count // lanes)
    digits = []
    for d in range(2):
        parts = [
            note[d * lines + i : d * lines + i + 1, : min(lanes, count - i * lanes)]
            for i in range(lines)
        ]
        digits.append(parts[0] if lines == 1 else jnp.concatenate(parts, axis=1))
    return digits[0] * 64 + digits[1]


def pack_kernel(index_ref, qkv_ref, first_ref, value_ref, all_ref):
    count = all_ref.shape[1] - SPARE
    for j in range(3):
        all_ref[j, :count, :] = pack(qkv_ref[j])
        all_ref[j, count:, :] = jnp.zeros((SPARE, all_ref.shape[2]), BF16)
    first_ref[...] = all_ref[index_ref[2]]
    value_ref[...] = all_ref[2]


def pack_proj_kernel(proj_ref, out_ref, far_ref):
    count = out_ref.shape[0]
    out_ref[...] = pack(proj_ref[...])
    far_ref[:count, :] = out_ref[...]
    far_ref[count:, :] = jnp.zeros((far_ref.shape[0] - count, far_ref.shape[1]), BF16)


def near_kernel(own_ref, next_ref, place_ref, out_ref):
    count = own_ref.shape[0]
    for i, ref in enumerate((own_ref, next_ref)):
        out_ref[i, :count, :] = ref[...]
        out_ref[i, count:, :] = write_note(place_ref[...], out_ref.shape[2])


def norm_kernel(index_ref, patches_ref, gain_ref, hidden_ref, own_ref):
    rows = patches_ref.shape[0]
    x = patches_ref[...]
    xf = x.astype(F32)
    mean_sq = jnp.mean(xf * xf, axis=-1, keepdims=True)
    gain = gain_ref[...].reshape(1, -1)
    hidden_ref[...] = (xf * lax.rsqrt(mean_sq + 1e-06) * gain).astype(BF16)
    step = 256
    pick = step // 4
    row = lax.broadcasted_iota(jnp.int32, (pick, step), 0)
    col = lax.broadcasted_iota(jnp.int32, (pick, step), 1)
    chosen = one_hot(col == 4 * row + index_ref[1])
    for i in range(rows // step):
        own_ref[i * pick : (i + 1) * pick, :] = jnp.dot(
            chosen, x[i * step : (i + 1) * step], preferred_element_type=F32
        ).astype(BF16)


def attend(index_ref, hidden_ref, valid_ref, w_ref, out_refs, q_ref, k_ref, v_ref, mix_ref):
    rows, width = q_ref.shape
    heads = width // HD
    main = 2 * LANES
    rest = width - main
    qkv = jnp.dot(hidden_ref[...], w_ref[...], preferred_element_type=F32)
    for j, ref in enumerate((q_ref, k_ref, v_ref)):
        ref[:, :main] = qkv[:, j * main : (j + 1) * main].astype(BF16)
        at = 3 * main + j * rest
        ref[:, main:] = qkv[:, at : at + rest].astype(BF16)
    q_win = lax.broadcasted_iota(jnp.int32, (PAIR, PAIR), 1) // WIN
    k_win = lax.broadcasted_iota(jnp.int32, (PAIR, PAIR), 0) // WIN
    same = q_win == k_win
    floor = jnp.where(same, F32(-1e30), F32(-3e38))
    pick = PAIR // 4
    src = lax.broadcasted_iota(jnp.int32, (PAIR, PAIR), 1)
    dst = lax.broadcasted_iota(jnp.int32, (PAIR, PAIR), 0)
    order = one_hot(src == 4 * (dst % pick) + dst // pick)
    zero = jnp.zeros((HD, PAIR), BF16)
    factor = F32(HD ** (-0.5) * math.log2(math.e))
    for p in range(rows // PAIR):
        at = p * PAIR
        q_turned = q_ref[at : at + PAIR, :].T
        v_turned = v_ref[at : at + PAIR, :].T
        q_all = jnp.concatenate(
            [
                jnp.concatenate(
                    [q_turned[h * HD : (h + 1) * HD] if i == h else zero for i in range(heads)], axis=1
                )
                for h in range(heads)
            ],
            axis=0,
        )
        scores = jnp.dot(k_ref[at : at + PAIR, :], q_all, preferred_element_type=F32)
        live = jnp.broadcast_to(valid_ref[p : p + 1, :].astype(F32), (PAIR, PAIR)).T > 0
        bias = jnp.where(same & live, F32(0), floor)
        mixed = []
        for h in range(heads):
            s = scores[:, h * PAIR : (h + 1) * PAIR] + bias
            e = jnp.exp2((s - jnp.max(s, axis=0, keepdims=True)) * factor)
            weights = (e * (1.0 / jnp.sum(e, axis=0, keepdims=True))).astype(BF16)
            mixed.append(
                jnp.dot(v_turned[h * HD : (h + 1) * HD], weights, preferred_element_type=F32)
            )
        mixed = jnp.concatenate(mixed, axis=0).astype(BF16)
        mixed = lax.dot_general(
            order, mixed, (((1,), (1,)), ((), ())), preferred_element_type=F32
        ).astype(BF16)
        for t in range(4):
            mix_ref[t, p * pick : (p + 1) * pick, :] = mixed[t * pick : (t + 1) * pick]
    for s, out_ref in enumerate(out_refs):
        out_ref[...] = pack(mix_ref[index_ref[1] ^ s])


def attention_kernel(n_ctx, width, index_ref, hidden_ref, valid_ref, *refs):
    shards = list(refs[: 2 + 3 * (n_ctx - 2)])
    *out_refs, w_ref, q_ref, k_ref, v_ref, mix_ref = refs[len(shards) :]
    depth = w_ref.shape[0] // n_ctx
    me = index_ref[0]
    flip = index_ref[2] > 0
    main = 2 * LANES
    for key in range(n_ctx):
        rows = pl.ds(pl.multiple_of((me ^ key) * depth, depth), depth)
        if key < 2:
            block = shards.pop(0)
            thirds = [block[j] for j in range(3)]
        else:
            first, second, value = [shards.pop(0)[...] for _ in range(3)]
            thirds = [jnp.where(flip, second, first), jnp.where(flip, first, second), value]
        tails = []
        for j, third in enumerate(thirds):
            w_ref[rows, j * main : (j + 1) * main], tail = unpack(third, depth, width)
            tails.append(tail)
        w_ref[rows, 3 * main :] = jnp.concatenate(tails, axis=1)
    attend(index_ref, hidden_ref, valid_ref, w_ref, out_refs, q_ref, k_ref, v_ref, mix_ref)


def project_kernel(n_ctx, width, col, index_ref, *refs):
    *blocks, own_ref, gain_ref, low_ref, high_ref, part_ref = refs[4:]
    rows = own_ref.shape[0]
    mixes = [unpack(m[...], rows, width) for m in refs[:4]]
    flip = index_ref[2] > 0
    mixes[2:] = [
        [jnp.where(flip, b, a) for a, b in zip(mixes[2], mixes[3])],
        [jnp.where(flip, a, b) for a, b in zip(mixes[2], mixes[3])],
    ]
    me = index_ref[0]
    main = 2 * LANES
    mixed = jnp.concatenate([m for m, _ in mixes] + [r for _, r in mixes], axis=1)
    mains = []
    rests = []
    for key in range(n_ctx):
        pieces = [ref[i] for ref in (blocks.pop(0), blocks.pop(0)) for i in range(2)]
        halves = [unpack(p, width, col) for p in pieces]
        both = []
        for half in ([h[0] for h in halves], [h[1] for h in halves]):
            both.append(jnp.concatenate([h[:main] for h in half] + [h[main:] for h in half], axis=0))
        mains.append(jnp.dot(mixed, both[0], preferred_element_type=F32))
        rests.append(both[1])
    if rests[0].shape[1]:
        rest = jnp.dot(mixed, jnp.concatenate(rests, axis=1), preferred_element_type=F32)
        count = rests[0].shape[1]
        mains = [
            jnp.concatenate([m, rest[:, key * count : (key + 1) * count]], axis=1)
            for key, m in enumerate(mains)
        ]
    for key in range(n_ctx):
        part_ref[me ^ key] = mains[key]
    total = jnp.concatenate([part_ref[i] for i in range(n_ctx)], axis=1)
    total = total + own_ref[...].astype(F32)
    mean_sq = jnp.mean(total * total, axis=-1, keepdims=True)
    gain = gain_ref[...].reshape(1, -1)
    normed = (total * lax.rsqrt(mean_sq + 1e-06) * gain).astype(BF16)
    half = low_ref.shape[0]
    low_ref[...] = normed[:half]
    high_ref[...] = normed[half:]


def place_kernel(count, index_ref, *refs):
    place_refs = refs[:count]
    *row_refs, out_ref, stage_ref, sem = refs[count:]
    spots = out_ref.shape[0]
    chosen = []
    base = (index_ref[0] * spots).astype(F32)
    for place_ref in place_refs:
        note_ref = place_ref.at[0] if len(place_ref.shape) == 3 else place_ref
        target = read_note(note_ref, spots) - base
        grid = lax.broadcasted_iota(jnp.int32, (spots, spots), 0).astype(F32)
        chosen.append(one_hot(grid == target))
    chosen = jnp.concatenate(chosen, axis=1)
    step = stage_ref.shape[2]
    copies = []
    for i in range(out_ref.shape[1] // step):
        cols = slice(i * step, (i + 1) * step)
        slot = stage_ref.at[i]
        slot[...] = jnp.dot(
            chosen,
            jnp.concatenate([ref[:, cols] for ref in row_refs], axis=0),
            preferred_element_type=F32,
        ).astype(BF16)
        copies.append(pltpu.make_async_copy(slot, out_ref.at[:, cols], sem.at[i]))
        copies[i].start()
    for copy in copies:
        copy.wait()


def local(n_dp, n_ctx, n_ten, patches, valid, place, gain_attn, w_qkv, w_proj, gain_merge):
    rows, feat = patches.shape
    depth, _, width = w_qkv.shape
    col = w_proj.shape[1]
    groups = rows // 4
    ten = lax.axis_index("tensor")
    half = lax.axis_index("dp") % 2
    index = jnp.stack([lax.axis_index("context"), ten, half]).astype(jnp.int32)
    cross = list(cross_keys(n_ctx))

    def over_dp(x):
        return swap(x, "dp", n_dp, 1)

    def over_core(x):
        return swap(x, "context", n_ctx, 1)

    third = packed_shape(depth, width)
    third = (third[0] + SPARE, third[1])
    piece = packed_shape(width, col)
    first, value, own = pl.pallas_call(
        pack_kernel,
        out_shape=(shape(*third), shape(*third), shape(3, *third)),
        in_specs=[SMEM, VMEM],
        out_specs=(VMEM,) * 3,
        compiler_params=params(8),
        name="pack",
    )(index, jnp.transpose(w_qkv, (1, 0, 2)))
    w_proj, far = pl.pallas_call(
        pack_proj_kernel,
        out_shape=(shape(*piece), shape(piece[0] + FAR_SPARE, piece[1])),
        in_specs=[VMEM],
        out_specs=(VMEM, VMEM),
        compiler_params=params(8),
        name="pack_proj",
    )(w_proj)
    first = gather_cross(first, n_ctx)
    value = gather_cross(value, n_ctx)
    twin = over_core(own)
    far = lax.ppermute(
        far,
        ("dp", "tensor"),
        [
            (d * n_ten + t, d * n_ten + (t ^ (2 + d % 2)))
            for d in range(n_dp)
            for t in range(n_ten)
        ],
    )
    by_one = swap(w_proj, "tensor", n_ten, 1)
    first, twin, patches = together(first, twin, patches)

    second = {k: over_dp(first[k]) for k in cross}
    first_twin = {k: over_core(first[k]) for k in cross}
    hidden, own_patches = pl.pallas_call(
        norm_kernel,
        out_shape=(shape(rows, feat), shape(groups, feat)),
        in_specs=[SMEM, VMEM, VMEM],
        out_specs=(VMEM, VMEM),
        compiler_params=params(16),
        name="norm",
    )(index, patches, gain_attn)
    by_one, hidden = together(by_one, hidden)
    near = pl.pallas_call(
        near_kernel,
        out_shape=shape(2, piece[0] + NOTE, piece[1]),
        in_specs=[VMEM] * 3,
        out_specs=VMEM,
        compiler_params=params(8),
        name="near",
    )(w_proj, by_one, place.reshape(1, groups))
    low = gather_cross(near, n_ctx)
    second, value, first_twin, hidden = together(second, value, first_twin, hidden)

    second_twin = {k: over_core(second[k]) for k in cross}
    value_twin = {k: over_core(value[k]) for k in cross}
    far, *_ = together(far, *second.values())
    far = far[: piece[0]]
    far2 = over_dp(far)

    shard_list = [own, twin]
    for k in cross:
        shard_list += [first[k], second[k], value[k], first_twin[k], second_twin[k], value_twin[k]]

    mix_shapes = (shape(*packed_shape(groups, width)),) * n_ten
    mixed = pl.pallas_call(
        functools.partial(attention_kernel, n_ctx, width),
        out_shape=mix_shapes,
        in_specs=[SMEM] + [VMEM] * (2 + len(shard_list)),
        out_specs=(VMEM,) * n_ten,
        scratch_shapes=[pltpu.VMEM((feat, 3 * width), BF16)]
        + [pltpu.VMEM((rows, width), BF16)] * 3
        + [pltpu.VMEM((4, groups, width), BF16)],
        compiler_params=params(20),
        name="attention",
    )(index, hidden, valid.reshape(rows // PAIR, PAIR), *shard_list)

    mixed, far, far2 = together(list(mixed), far, far2)
    for k in cross:
        low[k] = together(low[k], mixed[0])[0]
    received = [mixed[0]] + [swap(mixed[s], "tensor", n_ten, s) for s in range(1, n_ten)]
    high = gather_cross(jnp.stack([far, far2]), n_ctx)
    far_pair = jnp.stack([far, far2])
    blocks = [near, far_pair, over_core(near), over_core(far_pair)]
    low_twin = {k: over_core(low[k]) for k in cross}
    received, high = together(received, high)
    for k in cross:
        blocks += [low[k], high[k], low_twin[k], over_core(high[k])]
    done = pl.pallas_call(
        functools.partial(project_kernel, n_ctx, width, col),
        out_shape=(shape(groups // 2, feat),) * 2,
        in_specs=[SMEM] + [VMEM] * (n_ten + len(blocks) + 2),
        out_specs=(VMEM,) * 2,
        scratch_shapes=[pltpu.VMEM((n_ctx, groups, col), F32)],
        compiler_params=params(24),
        name="project",
    )(index, *received, *blocks, own_patches, gain_merge)

    gathered = []
    for rows_out in done:
        crossed = gather_cross(rows_out, n_ctx)
        if gathered:
            for k in cross:
                crossed[k], gathered[0][k ^ 1] = together(crossed[k], gathered[0][k ^ 1])
        for k in list(crossed):
            crossed[k ^ 1] = over_core(crossed[k])
        gathered.append(crossed)
    notes = [near, blocks[2]]
    for k in cross:
        notes += [low[k], low_twin[k]]
    return pl.pallas_call(
        functools.partial(place_kernel, n_ctx),
        out_shape=shape(groups, feat),
        in_specs=[SMEM] + [VMEM] * (3 * n_ctx),
        out_specs=pl.BlockSpec(memory_space=pl.ANY),
        scratch_shapes=[
            pltpu.VMEM((feat // 256, groups, 256), BF16),
            pltpu.SemaphoreType.DMA((feat // 256,)),
        ],
        compiler_params=params(28),
        name="placement",
    )(index, *notes, *[half[k] for k in range(n_ctx) for half in gathered])


def solution(mesh):
    in_specs = (
        P(("dp", "context"), None),
        P(("dp", "context")),
        P(("dp", "context")),
        P(),
        P("context", None, "tensor"),
        P("tensor", "context"),
        P(),
    )
    out_specs = P(("dp", "context"), "tensor")
    sizes = [mesh.shape[name] for name in ("dp", "context", "tensor")]
    body = functools.partial(local, *sizes)
    return jax.shard_map(body, mesh=mesh, in_specs=in_specs, out_specs=out_specs, check_vma=False)
```

```python
import functools
import math

import jax
import jax.numpy as jnp
from jax import lax
from jax.experimental import pallas as pl
from jax.experimental.pallas import tpu as pltpu
from jax.sharding import PartitionSpec as P

HD = 80
WIN = 64
PAIR = 2 * WIN
LANES = 128
F32 = jnp.float32
BF16 = jnp.bfloat16
VMEM = pl.BlockSpec(memory_space=pltpu.VMEM)
SMEM = pl.BlockSpec(memory_space=pltpu.SMEM)


def params(mib):
    return pltpu.CompilerParams(vmem_limit_bytes=mib * 1024 * 1024)


def swap(x, axis, size, bit):
    return lax.ppermute(x, axis, [(i, i ^ bit) for i in range(size)])


def cross_keys(size):
    return range(2, size, 2)


def gather_cross(x, size):
    blocks = {0: x}
    bit = size // 2
    while bit > 1:
        for key in list(blocks):
            blocks[key ^ bit] = swap(blocks[key], "context", size, bit)
        bit //= 2
    return blocks


def gather_xor(x, size):
    blocks = gather_cross(x, size)
    for key in list(blocks):
        blocks[key ^ 1] = swap(blocks[key], "context", size, 1)
    return blocks


def together(*values):
    return lax.optimization_barrier(values)


def one_hot(mask):
    return mask.astype(F32).astype(BF16)


def shape(*dims):
    return jax.ShapeDtypeStruct(dims, BF16)


def packs(rows, cols):
    return rows % 32 == 0 and cols == 2 * LANES + LANES // 2


def packed_shape(rows, cols):
    return (rows * 5 // 2, LANES) if packs(rows, cols) else (rows, cols)


def pack(x):
    rows, cols = x.shape
    if not packs(rows, cols):
        return x
    rest = x[:, 2 * LANES :]
    tail = jnp.concatenate([rest[: rows // 2], rest[rows // 2 :]], axis=1)
    return jnp.concatenate([x[:, :LANES], x[:, LANES : 2 * LANES], tail], axis=0)


def unpack(p, rows, cols):
    if not packs(rows, cols):
        return p[:rows, : 2 * LANES], p[:rows, 2 * LANES :]
    tail = p[2 * rows : 5 * rows // 2]
    rest = jnp.concatenate([tail[:, : LANES // 2], tail[:, LANES // 2 :]], axis=0)
    return jnp.concatenate([p[:rows], p[rows : 2 * rows]], axis=1), rest


NOTE = 16
SPARE = 16
FAR_SPARE = 48


def write_note(place, lanes):
    count = place.shape[1]
    filled = []
    for digit in (place >> 6, place & 63):
        for at in range(0, count, lanes):
            part = digit[:, at : at + lanes].astype(F32)
            spare = lanes - part.shape[1]
            filled.append(jnp.concatenate([part, jnp.zeros((1, spare), F32)], axis=1) if spare else part)
    filled.append(jnp.zeros((NOTE - len(filled), lanes), F32))
    return jnp.concatenate(filled, axis=0).astype(BF16)


def read_note(ref, count):
    note = ref[ref.shape[0] - NOTE :, :].astype(F32)
    lanes = note.shape[1]
    lines = -(-count // lanes)
    digits = []
    for d in range(2):
        parts = [
            note[d * lines + i : d * lines + i + 1, : min(lanes, count - i * lanes)]
            for i in range(lines)
        ]
        digits.append(parts[0] if lines == 1 else jnp.concatenate(parts, axis=1))
    return digits[0] * 64 + digits[1]


def pack_kernel(index_ref, qkv_ref, first_ref, value_ref, all_ref):
    count = all_ref.shape[1] - SPARE
    for j in range(3):
        all_ref[j, :count, :] = pack(qkv_ref[j])
        all_ref[j, count:, :] = jnp.zeros((SPARE, all_ref.shape[2]), BF16)
    first_ref[...] = all_ref[index_ref[2]]
    value_ref[...] = all_ref[2]


def pack_proj_kernel(proj_ref, out_ref, far_ref):
    count = out_ref.shape[0]
    out_ref[...] = pack(proj_ref[...])
    far_ref[:count, :] = out_ref[...]
    far_ref[count:, :] = jnp.zeros((far_ref.shape[0] - count, far_ref.shape[1]), BF16)


def near_kernel(own_ref, next_ref, place_ref, out_ref):
    count = own_ref.shape[0]
    for i, ref in enumerate((own_ref, next_ref)):
        out_ref[i, :count, :] = ref[...]
        out_ref[i, count:, :] = write_note(place_ref[...], out_ref.shape[2])


def norm_kernel(index_ref, patches_ref, gain_ref, hidden_ref, own_ref):
    rows = patches_ref.shape[0]
    x = patches_ref[...]
    xf = x.astype(F32)
    mean_sq = jnp.mean(xf * xf, axis=-1, keepdims=True)
    gain = gain_ref[...].reshape(1, -1)
    hidden_ref[...] = (xf * lax.rsqrt(mean_sq + 1e-06) * gain).astype(BF16)
    step = 256
    pick = step // 4
    row = lax.broadcasted_iota(jnp.int32, (pick, step), 0)
    col = lax.broadcasted_iota(jnp.int32, (pick, step), 1)
    chosen = one_hot(col == 4 * row + index_ref[1])
    for i in range(rows // step):
        own_ref[i * pick : (i + 1) * pick, :] = jnp.dot(
            chosen, x[i * step : (i + 1) * step], preferred_element_type=F32
        ).astype(BF16)


def attend(index_ref, hidden_ref, valid_ref, w_ref, out_refs, q_ref, k_ref, v_ref, mix_ref):
    rows, width = q_ref.shape
    heads = width // HD
    main = 2 * LANES
    rest = width - main
    qkv = jnp.dot(hidden_ref[...], w_ref[...], preferred_element_type=F32)
    for j, ref in enumerate((q_ref, k_ref, v_ref)):
        ref[:, :main] = qkv[:, j * main : (j + 1) * main].astype(BF16)
        at = 3 * main + j * rest
        ref[:, main:] = qkv[:, at : at + rest].astype(BF16)
    q_win = lax.broadcasted_iota(jnp.int32, (PAIR, PAIR), 1) // WIN
    k_win = lax.broadcasted_iota(jnp.int32, (PAIR, PAIR), 0) // WIN
    same = q_win == k_win
    floor = jnp.where(same, F32(-1e30), F32(-3e38))
    pick = PAIR // 4
    src = lax.broadcasted_iota(jnp.int32, (PAIR, PAIR), 1)
    dst = lax.broadcasted_iota(jnp.int32, (PAIR, PAIR), 0)
    order = one_hot(src == 4 * (dst % pick) + dst // pick)
    zero = jnp.zeros((HD, PAIR), BF16)
    factor = F32(HD ** (-0.5) * math.log2(math.e))
    for p in range(rows // PAIR):
        at = p * PAIR
        q_turned = q_ref[at : at + PAIR, :].T
        v_turned = v_ref[at : at + PAIR, :].T
        q_all = jnp.concatenate(
            [
                jnp.concatenate(
                    [q_turned[h * HD : (h + 1) * HD] if i == h else zero for i in range(heads)], axis=1
                )
                for h in range(heads)
            ],
            axis=0,
        )
        scores = jnp.dot(k_ref[at : at + PAIR, :], q_all, preferred_element_type=F32)
        live = jnp.broadcast_to(valid_ref[p : p + 1, :].astype(F32), (PAIR, PAIR)).T > 0
        bias = jnp.where(same & live, F32(0), floor)
        mixed = []
        for h in range(heads):
            s = scores[:, h * PAIR : (h + 1) * PAIR] + bias
            e = jnp.exp2((s - jnp.max(s, axis=0, keepdims=True)) * factor)
            part = jnp.dot(
                v_turned[h * HD : (h + 1) * HD], e.astype(BF16), preferred_element_type=F32
            )
            mixed.append(part * (1.0 / jnp.sum(e, axis=0, keepdims=True)))
        mixed = jnp.concatenate(mixed, axis=0).astype(BF16)
        mixed = lax.dot_general(
            order, mixed, (((1,), (1,)), ((), ())), preferred_element_type=F32
        ).astype(BF16)
        for t in range(4):
            mix_ref[t, p * pick : (p + 1) * pick, :] = mixed[t * pick : (t + 1) * pick]
    for s, out_ref in enumerate(out_refs):
        out_ref[...] = pack(mix_ref[index_ref[1] ^ s])


def attention_kernel(n_ctx, width, index_ref, hidden_ref, valid_ref, *refs):
    shards = list(refs[: 2 + 3 * (n_ctx - 2)])
    *out_refs, w_ref, q_ref, k_ref, v_ref, mix_ref = refs[len(shards) :]
    depth = w_ref.shape[0] // n_ctx
    me = index_ref[0]
    flip = index_ref[2] > 0
    main = 2 * LANES
    for key in range(n_ctx):
        rows = pl.ds(pl.multiple_of((me ^ key) * depth, depth), depth)
        if key < 2:
            block = shards.pop(0)
            thirds = [block[j] for j in range(3)]
        else:
            first, second, value = [shards.pop(0)[...] for _ in range(3)]
            thirds = [jnp.where(flip, second, first), jnp.where(flip, first, second), value]
        tails = []
        for j, third in enumerate(thirds):
            w_ref[rows, j * main : (j + 1) * main], tail = unpack(third, depth, width)
            tails.append(tail)
        w_ref[rows, 3 * main :] = jnp.concatenate(tails, axis=1)
    attend(index_ref, hidden_ref, valid_ref, w_ref, out_refs, q_ref, k_ref, v_ref, mix_ref)


def project_kernel(n_ctx, width, col, index_ref, *refs):
    *blocks, own_ref, gain_ref, low_ref, high_ref, part_ref = refs[4:]
    rows = own_ref.shape[0]
    mixes = [unpack(m[...], rows, width) for m in refs[:4]]
    flip = index_ref[2] > 0
    mixes[2:] = [
        [jnp.where(flip, b, a) for a, b in zip(mixes[2], mixes[3])],
        [jnp.where(flip, a, b) for a, b in zip(mixes[2], mixes[3])],
    ]
    me = index_ref[0]
    main = 2 * LANES
    mixed = jnp.concatenate([m for m, _ in mixes] + [r for _, r in mixes], axis=1)
    mains = []
    rests = []
    for key in range(n_ctx):
        pieces = [ref[i] for ref in (blocks.pop(0), blocks.pop(0)) for i in range(2)]
        halves = [unpack(p, width, col) for p in pieces]
        both = []
        for half in ([h[0] for h in halves], [h[1] for h in halves]):
            both.append(jnp.concatenate([h[:main] for h in half] + [h[main:] for h in half], axis=0))
        mains.append(jnp.dot(mixed, both[0], preferred_element_type=F32))
        rests.append(both[1])
    if rests[0].shape[1]:
        rest = jnp.dot(mixed, jnp.concatenate(rests, axis=1), preferred_element_type=F32)
        count = rests[0].shape[1]
        mains = [
            jnp.concatenate([m, rest[:, key * count : (key + 1) * count]], axis=1)
            for key, m in enumerate(mains)
        ]
    for key in range(n_ctx):
        part_ref[me ^ key] = mains[key]
    total = jnp.concatenate([part_ref[i] for i in range(n_ctx)], axis=1)
    total = total + own_ref[...].astype(F32)
    mean_sq = jnp.mean(total * total, axis=-1, keepdims=True)
    gain = gain_ref[...].reshape(1, -1)
    normed = (total * lax.rsqrt(mean_sq + 1e-06) * gain).astype(BF16)
    half = low_ref.shape[0]
    low_ref[...] = normed[:half]
    high_ref[...] = normed[half:]


def place_kernel(count, index_ref, *refs):
    place_refs = refs[:count]
    *row_refs, out_ref, stage_ref, sem = refs[count:]
    spots = out_ref.shape[0]
    chosen = []
    base = (index_ref[0] * spots).astype(F32)
    for place_ref in place_refs:
        note_ref = place_ref.at[0] if len(place_ref.shape) == 3 else place_ref
        target = read_note(note_ref, spots) - base
        grid = lax.broadcasted_iota(jnp.int32, (spots, spots), 0).astype(F32)
        chosen.append(one_hot(grid == target))
    chosen = jnp.concatenate(chosen, axis=1)
    step = stage_ref.shape[2]
    copies = []
    for i in range(out_ref.shape[1] // step):
        cols = slice(i * step, (i + 1) * step)
        slot = stage_ref.at[i]
        slot[...] = jnp.dot(
            chosen,
            jnp.concatenate([ref[:, cols] for ref in row_refs], axis=0),
            preferred_element_type=F32,
        ).astype(BF16)
        copies.append(pltpu.make_async_copy(slot, out_ref.at[:, cols], sem.at[i]))
        copies[i].start()
    for copy in copies:
        copy.wait()


def local(n_dp, n_ctx, n_ten, patches, valid, place, gain_attn, w_qkv, w_proj, gain_merge):
    rows, feat = patches.shape
    depth, _, width = w_qkv.shape
    col = w_proj.shape[1]
    groups = rows // 4
    ten = lax.axis_index("tensor")
    half = lax.axis_index("dp") % 2
    index = jnp.stack([lax.axis_index("context"), ten, half]).astype(jnp.int32)
    cross = list(cross_keys(n_ctx))

    def over_dp(x):
        return swap(x, "dp", n_dp, 1)

    def over_core(x):
        return swap(x, "context", n_ctx, 1)

    third = packed_shape(depth, width)
    third = (third[0] + SPARE, third[1])
    piece = packed_shape(width, col)
    first, value, own = pl.pallas_call(
        pack_kernel,
        out_shape=(shape(*third), shape(*third), shape(3, *third)),
        in_specs=[SMEM, VMEM],
        out_specs=(VMEM,) * 3,
        compiler_params=params(8),
        name="pack",
    )(index, jnp.transpose(w_qkv, (1, 0, 2)))
    w_proj, far = pl.pallas_call(
        pack_proj_kernel,
        out_shape=(shape(*piece), shape(piece[0] + FAR_SPARE, piece[1])),
        in_specs=[VMEM],
        out_specs=(VMEM, VMEM),
        compiler_params=params(8),
        name="pack_proj",
    )(w_proj)
    first = gather_cross(first, n_ctx)
    value = gather_cross(value, n_ctx)
    twin = over_core(own)
    far = lax.ppermute(
        far,
        ("dp", "tensor"),
        [
            (d * n_ten + t, d * n_ten + (t ^ (2 + d % 2)))
            for d in range(n_dp)
            for t in range(n_ten)
        ],
    )
    by_one = swap(w_proj, "tensor", n_ten, 1)
    first, twin, patches = together(first, twin, patches)

    second = {k: over_dp(first[k]) for k in cross}
    first_twin = {k: over_core(first[k]) for k in cross}
    hidden, own_patches = pl.pallas_call(
        norm_kernel,
        out_shape=(shape(rows, feat), shape(groups, feat)),
        in_specs=[SMEM, VMEM, VMEM],
        out_specs=(VMEM, VMEM),
        compiler_params=params(16),
        name="norm",
    )(index, patches, gain_attn)
    by_one, hidden = together(by_one, hidden)
    near = pl.pallas_call(
        near_kernel,
        out_shape=shape(2, piece[0] + NOTE, piece[1]),
        in_specs=[VMEM] * 3,
        out_specs=VMEM,
        compiler_params=params(8),
        name="near",
    )(w_proj, by_one, place.reshape(1, groups))
    low = gather_cross(near, n_ctx)
    second, value, first_twin, hidden = together(second, value, first_twin, hidden)

    second_twin = {k: over_core(second[k]) for k in cross}
    value_twin = {k: over_core(value[k]) for k in cross}
    far, *_ = together(far, *second.values())
    far = far[: piece[0]]
    far2 = over_dp(far)

    shard_list = [own, twin]
    for k in cross:
        shard_list += [first[k], second[k], value[k], first_twin[k], second_twin[k], value_twin[k]]

    mix_shapes = (shape(*packed_shape(groups, width)),) * n_ten
    mixed = pl.pallas_call(
        functools.partial(attention_kernel, n_ctx, width),
        out_shape=mix_shapes,
        in_specs=[SMEM] + [VMEM] * (2 + len(shard_list)),
        out_specs=(VMEM,) * n_ten,
        scratch_shapes=[pltpu.VMEM((feat, 3 * width), BF16)]
        + [pltpu.VMEM((rows, width), BF16)] * 3
        + [pltpu.VMEM((4, groups, width), BF16)],
        compiler_params=params(20),
        name="attention",
    )(index, hidden, valid.reshape(rows // PAIR, PAIR), *shard_list)

    mixed, far, far2, low = together(list(mixed), far, far2, low)
    received = [mixed[0]] + [swap(mixed[s], "tensor", n_ten, s) for s in range(1, n_ten)]
    high = gather_cross(jnp.stack([far, far2]), n_ctx)
    far_pair = jnp.stack([far, far2])
    blocks = [near, far_pair, over_core(near), over_core(far_pair)]
    low_twin = {k: over_core(low[k]) for k in cross}
    received, high = together(received, high)
    for k in cross:
        blocks += [low[k], high[k], low_twin[k], over_core(high[k])]
    done = pl.pallas_call(
        functools.partial(project_kernel, n_ctx, width, col),
        out_shape=(shape(groups // 2, feat),) * 2,
        in_specs=[SMEM] + [VMEM] * (n_ten + len(blocks) + 2),
        out_specs=(VMEM,) * 2,
        scratch_shapes=[pltpu.VMEM((n_ctx, groups, col), F32)],
        compiler_params=params(24),
        name="project",
    )(index, *received, *blocks, own_patches, gain_merge)

    gathered = []
    for rows_out in done:
        crossed = gather_cross(rows_out, n_ctx)
        if gathered:
            for k in cross:
                crossed[k], gathered[0][k ^ 1] = together(crossed[k], gathered[0][k ^ 1])
        for k in list(crossed):
            crossed[k ^ 1] = over_core(crossed[k])
        gathered.append(crossed)
    notes = [near, blocks[2]]
    for k in cross:
        notes += [low[k], low_twin[k]]
    return pl.pallas_call(
        functools.partial(place_kernel, n_ctx),
        out_shape=shape(groups, feat),
        in_specs=[SMEM] + [VMEM] * (3 * n_ctx),
        out_specs=pl.BlockSpec(memory_space=pl.ANY),
        scratch_shapes=[
            pltpu.VMEM((feat // 256, groups, 256), BF16),
            pltpu.SemaphoreType.DMA((feat // 256,)),
        ],
        compiler_params=params(28),
        name="placement",
    )(index, *notes, *[half[k] for k in range(n_ctx) for half in gathered])


def solution(mesh):
    in_specs = (
        P(("dp", "context"), None),
        P(("dp", "context")),
        P(("dp", "context")),
        P(),
        P("context", None, "tensor"),
        P("tensor", "context"),
        P(),
    )
    out_specs = P(("dp", "context"), "tensor")
    sizes = [mesh.shape[name] for name in ("dp", "context", "tensor")]
    body = functools.partial(local, *sizes)
    return jax.shard_map(body, mesh=mesh, in_specs=in_specs, out_specs=out_specs, check_vma=False)
```
